32 devices in a mesh: dp: 8 (over y, x, core), section: 4 (over z).
Axes of the slice: x: 2, y: 2, z: 4, core: 2. Of those that a mesh axis runs over, the one named last changes fastest.
Arguments:
- inputs: bfloat16 [16, 128, 768], P('dp', 'section'), may hold values from -6 to 6
- other_view: bfloat16 [16, 256, 768], P('dp', 'section'), may hold values from -6 to 6
- mats: bfloat16 [4, 2, 768, 3072], P('section'), may hold values from -24 to 24
- vectors: float32 [4, 7, 768], P('section'), may hold values from -2 to 2
- mixing: float32 [16], P('dp'), may hold values from 0.2 to 0.8
- partner: int32 [16], P('dp'), may hold values from 0 to 1
- segments: int32 [16, 128], P('dp'), may hold values from 0 to 2, never falling along the last dimension, each value on 1 to 64 neighbouring positions
- cotangent: bfloat16 [16, 128, 768], P('dp'), may hold values from -6 to 6
Outputs:
- activations: bfloat16 [4, 16, 128, 768], P('section', 'dp')
- input_grad: bfloat16 [16, 128, 768], P('dp', 'section')
- view_grad: bfloat16 [16, 256, 768], P('dp', 'section')
- mats_grad: float32 [4, 2, 768, 3072], P('section')
- vectors_grad: float32 [4, 7, 768], P('section')
The draws below stay inside these ranges and needn't reach their ends.
Inputs may be any that keep to these rules, and one draw needn't show every extreme that they name: `segments`: clip numbers never fall along a row; each clip has 1 to 64 tokens and one has exactly that many.
All inputs are finite; a program needn't handle non-finite values.
Results may differ from the reference program's by a relative error of at most 0.018.
Values may be sent and summed in bfloat16 or wider, within the bound.
A program may use at most 192 MiB of HBM per device.

```python
import math
import jax
import jax.numpy as jnp
import numpy as np
from jax import lax

D = 768
HEADS = 12
HEAD = 64
FF = 3072
TOK_ROW = 128
MB = 2
VIEW_ROW = 256
ROWS = 16
N_DP = 8
N_SECTION = 4


def draw_mats(key, part):
    key = jax.random.fold_in(key, 11)
    section_index = jnp.arange(N_SECTION)[:, None, None, None]
    matrix_slot = jnp.arange(2)[None, :, None, None]
    column = jnp.arange(FF)[None, None, None, :]
    attention = section_index % 2 == 0
    out_block = column >= 3 * D
    scaling_attention = jnp.where(out_block, 6.0, 1.0) * D ** (-0.5)
    scaling_forward = jnp.where(matrix_slot == 0, D ** (-0.5), 1.5 * FF ** (-0.5))
    scaling = jnp.where(attention, scaling_attention, scaling_forward)
    entries = jax.random.truncated_normal(key, -4.0, 4.0, (N_SECTION, 2, D, FF), jnp.float32)
    return (entries * scaling).astype(jnp.bfloat16)


def draw_vectors(key, part):
    key = jax.random.fold_in(key, 23)
    section_index = jnp.arange(N_SECTION)[:, None, None]
    row_index = jnp.arange(7)[None, :, None]
    merging_section = section_index % 2 == 0
    gain_rows = (row_index == 0) | merging_section & (row_index == 2)
    gain_key, bias_key = jax.random.split(key)
    gains = 1.0 + 0.25 * jax.random.truncated_normal(gain_key, -2.0, 2.0, (N_SECTION, 7, D), jnp.float32)
    biases = 0.4 * jax.random.truncated_normal(bias_key, -4.0, 4.0, (N_SECTION, 7, D), jnp.float32)
    return jnp.where(gain_rows, gains, biases)


def place_ends(values, rng, least, largest):
    spot = [jax.random.randint(jax.random.fold_in(rng, axis), (), 0, length) for axis, length in enumerate(values.shape)]
    longest = values.shape.index(max(values.shape))
    neighbour = spot[:longest] + [(spot[longest] + 1) % values.shape[longest]] + spot[longest + 1:]
    return values.at[tuple(spot)].set(least).at[tuple(neighbour)].set(largest)


def level_of(rng, dims, pieces, low, high):
    def one(position, parts):
        steps = jax.random.uniform(jax.random.fold_in(jax.random.fold_in(rng, 6), position), (parts,), jnp.float32, low / len(pieces), high / len(pieces))
        return jnp.repeat(jnp.exp(steps), dims[position] // parts).reshape((-1,) + (1,) * (len(dims) - position - 1))

    loudness = one(*pieces[0])
    for cut in pieces[1:]:
        loudness = loudness * one(*cut)
    return loudness


def length_profile(number_of, total, bound, lean):
    weights = [(1 << 20) // math.isqrt(standing ** lean) + 1 for standing in range(2, number_of + 1)]
    rest, counts = total - bound - (number_of - 1), [1] * (number_of - 1)
    while rest > 0:
        free = [i for i in range(number_of - 1) if counts[i] < bound]
        pool, budget = sum([weights[i] for i in free]), rest
        for i in free:
            more = min(bound - counts[i], max(1, budget * weights[i] // pool), rest)
            counts[i] = counts[i] + more
            rest = rest - more
    return np.array([bound] + counts)


def uneven_parts(stream_key, count, total, reach, slope):
    if count == 2:
        one = jax.random.randint(stream_key, (), max(1, total - reach), min(reach, total - 1) + 1)
        return jnp.stack([one, total - one])
    lengths = jnp.asarray(length_profile(count, total, reach, slope), jnp.int32)
    twos = (count - 1) // 2
    source_of, receiver = lengths[1:1 + 2 * twos:2], lengths[2:2 + 2 * twos:2]
    room = jnp.minimum(source_of - 1, reach - receiver)
    moved = jax.random.randint(jax.random.fold_in(stream_key, 1), (twos,), 0, 1 << 20) % (room + 1)
    lengths = lengths.at[1:1 + 2 * twos:2].set(source_of - moved).at[2:2 + 2 * twos:2].set(receiver + moved)
    return lengths[jax.random.permutation(jax.random.fold_in(stream_key, 2), count)]


def centred(own_key, dims, deviation, most, cuts=(), held_as=jnp.bfloat16):
    gain = level_of(own_key, dims, cuts, -0.22, 0.18) if cuts else 1.0
    values = jax.random.normal(own_key, dims, jnp.float32) * deviation * gain
    return jnp.minimum(jnp.maximum(values, -most), most).astype(held_as)


def setup_inputs(seed: int = 0) -> dict:
    keys = jax.random.split(jax.random.key(seed), 9)
    return {
        "inputs": centred(keys[0], (ROWS, TOK_ROW, D), 1.0, 6.0, ((0, 8), (1, 4))),
        "other_view": centred(keys[1], (ROWS, VIEW_ROW, D), 1.0, 6.0, ((0, 8), (1, 4))),
        "mats": draw_mats(jax.random.fold_in(keys[8], 71), 0),
        "vectors": draw_vectors(jax.random.fold_in(keys[8], 71), 0),
        "mixing": jnp.clip(0.2 + 0.6 * jax.random.uniform(keys[4], (ROWS,), jnp.float32) ** level_of(keys[4], (ROWS,), ((0, 8),), -0.2, 0.2), 0.2, 0.8),
        "partner": place_ends(jax.random.randint(keys[5], (ROWS,), 0, MB), jax.random.fold_in(keys[5], 1), 0, MB - 1).astype(jnp.int32),
        "segments": jax.vmap(lambda own: jnp.searchsorted(jnp.cumsum(uneven_parts(own, 3, TOK_ROW, TOK_ROW // 2, 1)), jnp.arange(TOK_ROW), side="right"))(jax.random.split(keys[6], ROWS)).reshape((ROWS, TOK_ROW)).astype(jnp.int32),
        "cotangent": centred(keys[7], (ROWS, TOK_ROW, D), 1.0, 6.0, ((0, 8),)),
    }


@jax.custom_vjp
def low(v):
    return lax.optimization_barrier(v.astype(jnp.bfloat16)).astype(jnp.float32)

@jax.custom_vjp
def low_back(v):
    return v

def low_keep(v):
    return (low(v), None)

def low_pass(kept, grad):
    return (grad,)

def back_keep(v):
    return (v, None)

def back_low(kept, grad):
    return (low(grad),)
low.defvjp(low_keep, low_pass)
low_back.defvjp(back_keep, back_low)

def rounded_both(value):
    return low(low_back(value))

def product(multiplier, multiplicand):
    return jnp.dot(multiplier, multiplicand, precision=lax.Precision.HIGHEST, preferred_element_type=jnp.float32)

def normalize(stream, norm_gain, norm_shift):
    center = stream - lax.optimization_barrier(jnp.mean(stream, axis=-1, keepdims=True))
    spread = lax.optimization_barrier(jnp.mean(center * center, axis=-1, keepdims=True))
    return center * lax.rsqrt(spread + 1e-06) * norm_gain + norm_shift

def attend(queries, key_states, value_states, query_ids, key_ids):
    query_count = queries.shape[0]
    split_q = queries.reshape(query_count, HEADS, HEAD)
    split_k = key_states.reshape(key_states.shape[0], HEADS, HEAD)
    split_v = value_states.reshape(value_states.shape[0], HEADS, HEAD)
    scores = low_back(jnp.einsum('qhd,khd->hqk', split_q, split_k, precision=lax.Precision.HIGHEST) * HEAD ** (-0.5))
    allowed = (query_ids[:, None] == key_ids[None, :])[None]
    scores = jnp.where(allowed, scores, -1000000000.0)
    row_max = lax.optimization_barrier(jnp.max(scores, axis=-1, keepdims=True))
    weights = jnp.exp(scores - row_max)
    weights = weights / lax.optimization_barrier(jnp.sum(weights, axis=-1, keepdims=True))
    attended = jnp.einsum('hqk,khd->qhd', low(weights), split_v, precision=lax.Precision.HIGHEST)
    return rounded_both(attended.reshape(query_count, HEADS * HEAD))

def self_layer(stream, query_ids, first, vector):
    normed = low(normalize(stream, vector[0], vector[1]))
    queries = rounded_both(product(normed, first[:, :D]) + vector[5])
    key_states = rounded_both(product(normed, first[:, D:2 * D]))
    value_states = rounded_both(product(normed, first[:, 2 * D:3 * D]) + vector[2])
    attended = attend(queries, key_states, value_states, query_ids, query_ids)
    return stream + low_back(product(attended, first[:, 3 * D:])) + vector[4]

def merging_layer(stream, source, query_ids, first, second, vector):
    source_ids = jnp.repeat(query_ids, 2)
    normed = low(normalize(stream, vector[0], vector[1]))
    queries = rounded_both(product(normed, first[:, :D]))
    key_states = rounded_both(product(source, first[:, D:2 * D]))
    value_states = rounded_both(product(source, first[:, 2 * D:3 * D]))
    attended = attend(queries, key_states, value_states, query_ids, source_ids)
    stream = stream + low_back(product(attended, first[:, 3 * D:])) + vector[4]
    normed = low(normalize(stream, vector[2], vector[3]))
    queries = rounded_both(product(normed, second[:, :D]) + vector[5])
    key_states = rounded_both(product(normed, second[:, D:2 * D]))
    value_states = rounded_both(product(normed, second[:, 2 * D:3 * D]))
    attended = attend(queries, key_states, value_states, query_ids, query_ids)
    return stream + low_back(product(attended, second[:, 3 * D:])) + vector[6]

def feed_forward(stream, first, second, vector):
    normed = low(normalize(stream, vector[0], vector[1]))
    hidden = low_back(product(normed, first) + vector[2:6].reshape(FF))
    active = low(jax.nn.gelu(hidden, approximate=False))
    return stream + low_back(product(active, second.T)) + vector[6]

def forward(inputs, other_view, mats, vectors, mixing, partner, segments):
    device_of = jnp.arange(inputs.shape[0], dtype=jnp.int32) // MB
    source_row = (device_of + N_DP // 2) % N_DP * MB + partner
    share = mixing[:, None, None]
    blended = share * inputs + (1.0 - share) * low_back(inputs)[source_row]
    blended_view = low(share * other_view + (1.0 - share) * low_back(other_view)[source_row])

    def run_row(scan_carry, row_items):
        stream, source, query_ids = row_items
        outputs = []
        for section_index in range(N_SECTION):
            if section_index == 0:
                stream = self_layer(stream, query_ids, mats[0, 0], vectors[0])
            elif section_index % 2 == 0:
                stream = merging_layer(stream, source, query_ids, mats[section_index, 0], mats[section_index, 1], vectors[section_index])
            else:
                stream = feed_forward(stream, mats[section_index, 0], mats[section_index, 1], vectors[section_index])
            stream = rounded_both(stream)
            outputs.append(stream)
        return (scan_carry, jnp.stack(outputs))
    final_carry, stacked = lax.scan(jax.checkpoint(run_row), jnp.zeros((), jnp.float32), (blended, blended_view, segments))
    return jnp.transpose(stacked, (1, 0, 2, 3))

def reference(inputs, other_view, mats, vectors, mixing, partner, segments, cotangent):

    def wrapped(inputs_wide, view_wide, mats_wide, vectors_wide):
        return forward(inputs_wide, view_wide, mats_wide, vectors_wide, mixing, partner, segments)
    activations, pullback = jax.vjp(wrapped, inputs.astype(jnp.float32), other_view.astype(jnp.float32), mats.astype(jnp.float32), vectors)
    cotangent_full = jnp.zeros_like(activations).at[N_SECTION - 1].set(cotangent.astype(jnp.float32))
    grad_inputs, grad_view, grad_mats, grad_vectors = pullback(cotangent_full)
    return (activations.astype(jnp.bfloat16), grad_inputs.astype(jnp.bfloat16), grad_view.astype(jnp.bfloat16), grad_mats, grad_vectors)
```

```python
from functools import partial

import jax
import jax.numpy as jnp
from jax import lax
from jax.experimental import pallas as pl
from jax.experimental.pallas import tpu as pltpu
from jax.sharding import PartitionSpec as P

HEAD = 64
PAIR = 2 * HEAD
MESH = pl.DeviceIdType.MESH
bf16 = jnp.bfloat16
f32 = jnp.float32


def dot(a, b):
    return lax.dot_general(a, b, (((1,), (0,)), ((), ())), preferred_element_type=f32)


def dot_t(a, b):
    return lax.dot_general(a, b, (((1,), (1,)), ((), ())), preferred_element_type=f32)


def t_dot(a, b):
    return lax.dot_general(a, b, (((0,), (0,)), ((), ())), preferred_element_type=f32)


def row_mean(x):
    return jnp.sum(x, axis=-1, keepdims=True) * (1.0 / x.shape[-1])


def normalize(h):
    center = h - row_mean(h)
    scale = lax.rsqrt(row_mean(center * center) + 1e-06)
    return center * scale, scale


def normalize_back(grad, unit, scale, gain):
    inner = grad * gain
    return scale * (inner - row_mean(inner) - unit * row_mean(inner * unit))


def gelu_parts(a):
    cdf = 0.5 * (1.0 + lax.erf(a * (0.5**0.5)))
    pdf = jnp.exp(a * a * (-0.5)) * 0.3989422804014327
    return a * cdf, cdf + a * pdf


def halves(x):
    low = lax.broadcasted_iota(jnp.int32, x.shape, 1) < HEAD
    zero = jnp.zeros_like(x)
    return jnp.concatenate([jnp.where(low, x, zero), jnp.where(low, zero, x)], axis=0)


def softmax(scores, allowed):
    scores = jnp.where(allowed, scores, -1000000000.0)
    weights = jnp.exp(scores - jnp.max(scores, axis=-1, keepdims=True))
    return weights * (1.0 / jnp.sum(weights, axis=-1, keepdims=True))


def attend_pair(q, k, v, allowed):
    n = k.shape[0]
    scores = dot_t(q, halves(k))
    weights = jnp.concatenate(
        [softmax(scores[:, :n], allowed), softmax(scores[:, n:], allowed)], axis=1
    )
    return dot(weights.astype(bf16), halves(v)), weights


def attend_pair_back(q, k, v, weights, grad):
    n = k.shape[0]
    grad_weights = dot_t(grad, halves(v))
    product = weights * grad_weights
    parts = []
    for part in (slice(0, n), slice(n, 2 * n)):
        total = jnp.sum(product[:, part], axis=-1, keepdims=True)
        parts.append((product[:, part] - weights[:, part] * total).astype(bf16))
    grad_q = dot(jnp.concatenate(parts, axis=1), halves(k)) * (HEAD**-0.5)
    grad_k = t_dot(jnp.concatenate(parts, axis=0), halves(q))
    rounded = weights.astype(bf16)
    grad_v = t_dot(jnp.concatenate([rounded[:, :n], rounded[:, n:]], axis=0), halves(grad))
    return grad_q, grad_k, grad_v


def column_sum(x):
    return jnp.sum(x.astype(f32), axis=0, keepdims=True)


def kernel(names, *refs):
    R = dict(zip(names, refs))
    inputs, other_view, mats, vec = (R[k] for k in ("inputs", "other_view", "mats", "vec"))
    mixing, partner, cot = R["mixing"], R["partner"], R["cot"]
    seg_q, seg_k, seg_v = R["seg_q"], R["seg_k"], R["seg_v"]
    records, in_grad, view_grad = R["records"], R["in_grad"], R["view_grad"]
    G, gv = R["G"], R["gv"]
    w, hin, gin, gout = R["w"], R["hin"], R["gin"], R["gout"]
    B, TS, D = inputs.shape
    VS = other_view.shape[1]
    T = records.shape[1]
    S = lax.axis_size("section")
    n_dp = lax.axis_size("dp")
    z = lax.axis_index("section")
    d = lax.axis_index("dp")
    far = {"dp": lax.rem(d + n_dp // 2, n_dp)}
    pairs = D // PAIR

    def remote(src, dst, send, recv, device):
        return pltpu.make_async_remote_copy(
            src_ref=src,
            dst_ref=dst,
            send_sem=send,
            recv_sem=recv,
            device_id=device,
            device_id_type=MESH,
        )

    def table(t):
        return pltpu.make_async_copy(mats.at[0, t], w.at[t], R["w_sem"].at[t])

    table(0).start()
    table(1).start()

    barrier = pltpu.get_barrier_semaphore()
    pl.semaphore_signal(barrier, inc=1, device_id=far, device_id_type=MESH)
    for o in range(1, S):
        pl.semaphore_signal(
            barrier, inc=1, device_id={"section": lax.rem(z + o, S)}, device_id_type=MESH
        )
    pl.semaphore_wait(barrier, S)

    ex = R["ex_sem"]
    far_i = remote(inputs, R["far_i"], ex.at[0], ex.at[1], far)
    far_v = remote(other_view, R["far_v"], ex.at[2], ex.at[3], far)
    far_i.start()
    far_v.start()
    gv[...] = jnp.zeros_like(gv)
    pick = [[(partner[r] == j).astype(f32) for j in range(B)] for r in range(B)]
    mix = [mixing[r] for r in range(B)]

    def blend(own, other, r):
        chosen = sum(pick[r][j] * other[j].astype(f32) for j in range(B))
        return (mix[r] * own[r].astype(f32) + (1.0 - mix[r]) * chosen).astype(bf16)

    def gather_i(r, source):
        return remote(
            R["stage_i"].at[r],
            hin.at[r, pl.ds(source * TS, TS)],
            R["gi_send"].at[r],
            R["gi_recv"].at[r, source],
            {"section": 0},
        )

    def gather_v(r, source):
        return remote(
            R["stage_v"].at[r],
            R["view"].at[r, pl.ds(source * VS, VS)],
            R["gv_send"].at[r],
            R["gv_recv"].at[r, source],
            {"section": 2},
        )

    far_i.wait_recv()
    for r in range(B):
        mixed = blend(inputs, R["far_i"], r)

        @pl.when(z == 0)
        def _():
            hin[r, :TS] = mixed

        @pl.when(z != 0)
        def _():
            R["stage_i"][r] = mixed
            gather_i(r, z).start()

    far_v.wait_recv()
    for r in range(B):
        mixed_view = blend(other_view, R["far_v"], r)

        @pl.when(z == 2)
        def _():
            R["view"][r, 2 * VS : 3 * VS] = mixed_view

        @pl.when(z != 2)
        def _():
            R["stage_v"][r] = mixed_view
            gather_v(r, z).start()

    far_i.wait_send()
    far_v.wait_send()

    def forward_hop(r):
        return remote(
            records.at[r], hin.at[r], R["f_send"].at[r], R["f_recv"].at[r], {"section": z + 1}
        )

    def backward_hop(r):
        return remote(
            gout.at[r], gin.at[r], R["b_send"].at[r], R["b_recv"].at[r], {"section": z - 1}
        )

    def entered(r):
        remote(
            hin.at[r], hin.at[r], R["f_send"].at[r], R["f_recv"].at[r], {"section": z - 1}
        ).wait_recv()

    def returned(r):
        remote(
            gin.at[r], gin.at[r], R["b_send"].at[r], R["b_recv"].at[r], {"section": z + 1}
        ).wait_recv()

    def each_row(step):
        lax.fori_loop(0, B, lambda r, c: (step(r), c)[1], 0)

    def cols(b, width=D):
        return slice(b * width, (b + 1) * width)

    def flat(x):
        return x[...].reshape(B * T, x.shape[2])

    def norm_in(h, r, unit, scale, normed, gain, shift):
        unit_value, scale_value = normalize(h)
        unit[r] = unit_value
        scale[r] = scale_value
        value = (unit_value * vec[gain : gain + 1] + vec[shift : shift + 1]).astype(bf16)
        normed[r] = value
        return value

    def norm_out(grad, r, unit, scale, gain):
        return normalize_back(grad, unit[r], scale[r], vec[gain : gain + 1])

    def norm_sums(grad, r, unit, gain, shift):
        gv[gain : gain + 1] += column_sum(grad * unit[r])
        gv[shift : shift + 1] += column_sum(grad)

    def self_attend(r, qkv, weights, attended):
        allowed = seg_q[r] == seg_k[r]
        for p in range(pairs):
            c = cols(p, PAIR)
            k = slice(D + c.start, D + c.stop)
            v = slice(2 * D + c.start, 2 * D + c.stop)
            out, kept = attend_pair(qkv[r, :, c], qkv[r, :, k], qkv[r, :, v], allowed)
            attended[r, :, c] = out.astype(bf16)
            weights[r, p] = kept

    def self_attend_back(r, qkv, weights, grad, dqkv):
        for p in range(pairs):
            c = cols(p, PAIR)
            k = slice(D + c.start, D + c.stop)
            v = slice(2 * D + c.start, 2 * D + c.stop)
            dq, dk, dv = attend_pair_back(
                qkv[r, :, c], qkv[r, :, k], qkv[r, :, v], weights[r, p], grad[r, :, c]
            )
            dqkv[r, :, c] = dq.astype(bf16)
            dqkv[r, :, k] = dk.astype(bf16)
            dqkv[r, :, v] = dv.astype(bf16)

    n1, u1, s1, p1, a1 = R["n1"], R["u1"], R["s1"], R["p1"], R["a1"]
    qkv1, dqkv1, do1 = R["qkv1"], R["dqkv1"], R["do1"]
    n2, u2, s2, p2, a2 = R["n2"], R["u2"], R["s2"], R["p2"], R["a2"]
    q2, dq2, kv2, dkv2, do2 = R["q2"], R["dq2"], R["kv2"], R["dkv2"], R["do2"]
    view, dm = R["view"], R["dm"]
    g, gp, da = R["g"], R["gp"], R["da"]
    SCALE = HEAD**-0.5

    @pl.when(z == 0)
    def _():
        table(0).wait()
        table(1).wait()

        def forward(r):
            for k in range(1, S):
                gather_i(r, k).wait_recv()
            h = hin[r].astype(f32)
            n = norm_in(h, r, u1, s1, n1, 0, 1)
            q = (dot(n, w[0, :, cols(0)]) + vec[5:6]).astype(bf16)
            qkv1[r, :, cols(0)] = q * SCALE
            qkv1[r, :, cols(1)] = dot(n, w[0, :, cols(1)]).astype(bf16)
            qkv1[r, :, cols(2)] = (dot(n, w[0, :, cols(2)]) + vec[2:3]).astype(bf16)
            self_attend(r, qkv1, p1, a1)
            out = h + dot(a1[r], w[0, :, cols(3)]) + vec[4:5]
            records[r] = out.astype(bf16)
            forward_hop(r).start()

        each_row(forward)

        def backward(r):
            returned(r)
            e = gin[r]
            do1[r] = dot_t(e, w[0, :, cols(3)]).astype(bf16)
            self_attend_back(r, qkv1, p1, do1, dqkv1)
            dn = dot_t(dqkv1[r], w[0, :, : 3 * D])
            gout[r] = (e.astype(f32) + norm_out(dn, r, u1, s1, 0)).astype(bf16)
            norm_sums(dn, r, u1, 0, 1)
            gv[2:3] += column_sum(dqkv1[r, :, cols(2)])
            gv[4:5] += column_sum(e)
            gv[5:6] += column_sum(dqkv1[r, :, cols(0)])

        each_row(backward)
        G[3] = t_dot(flat(a1), flat(gin)).astype(bf16)
        for b in range(3):
            G[b] = t_dot(flat(n1), dqkv1[:, :, cols(b)].reshape(B * T, D)).astype(bf16)
        for b in range(4, 8):
            G[b] = jnp.zeros_like(G[b])

    def feed_hidden(n, c):
        a = dot(n, w[0, :, cols(c)]) + vec[2 + c : 3 + c]
        return gelu_parts(a)

    def feed_grads(e_rows):
        def one(c, _):
            cc = pl.ds(pl.multiple_of(c * D, D), D)
            G[4 + c] = t_dot(flat(e_rows), g[:, :, cc].reshape(B * T, D)).astype(bf16)
            G[c] = t_dot(flat(n1), da[:, :, cc].reshape(B * T, D)).astype(bf16)
            return 0

        lax.fori_loop(0, 4, one, 0)

    def feed_sums(r, e):
        for c in range(4):
            gv[2 + c : 3 + c] += column_sum(da[r, :, cols(c)])
        gv[6:7] += column_sum(e)

    @pl.when(z == 1)
    def _():
        table(0).wait()
        table(1).wait()

        def forward(r):
            entered(r)
            h = hin[r].astype(f32)
            n = norm_in(h, r, u1, s1, n1, 0, 1)
            out = h + vec[6:7]
            for c in range(4):
                active, slope = feed_hidden(n, c)
                active = active.astype(bf16)
                g[r, :, cols(c)] = active
                gp[r, :, cols(c)] = slope
                out += dot_t(active, w[1, :, cols(c)])
            records[r] = out.astype(bf16)
            forward_hop(r).start()

        each_row(forward)

        def backward(r):
            returned(r)
            e = gin[r]
            dn = jnp.zeros((T, D), f32)
            for c in range(4):
                dg = dot(e, w[1, :, cols(c)])
                dc = (dg * gp[r, :, cols(c)]).astype(bf16)
                da[r, :, cols(c)] = dc
                dn += dot_t(dc, w[0, :, cols(c)])
            gout[r] = (e.astype(f32) + norm_out(dn, r, u1, s1, 0)).astype(bf16)
            backward_hop(r).start()
            norm_sums(dn, r, u1, 0, 1)
            feed_sums(r, e)

        each_row(backward)
        feed_grads(gin)

    @pl.when(z == 3)
    def _():
        table(0).wait()
        table(1).wait()

        def ahead(r):
            e = cot[r]
            for c in range(4):
                gp[r, :, cols(c)] = dot(e, w[1, :, cols(c)])

        each_row(ahead)

        def turn(r):
            entered(r)
            e = cot[r]
            n = norm_in(hin[r].astype(f32), r, u1, s1, n1, 0, 1)
            dn = jnp.zeros((T, D), f32)
            for c in range(4):
                active, slope = feed_hidden(n, c)
                g[r, :, cols(c)] = active.astype(bf16)
                dc = (gp[r, :, cols(c)] * slope).astype(bf16)
                da[r, :, cols(c)] = dc
                dn += dot_t(dc, w[0, :, cols(c)])
            gout[r] = (e.astype(f32) + norm_out(dn, r, u1, s1, 0)).astype(bf16)
            backward_hop(r).start()
            norm_sums(dn, r, u1, 0, 1)
            feed_sums(r, e)

        each_row(turn)

        def output(r):
            records[r] = (hin[r].astype(f32) + dot_t(g[r], w[1]) + vec[6:7]).astype(bf16)

        each_row(output)
        feed_grads(cot)

    @pl.when(z == 2)
    def _():
        table(0).wait()
        table(1).wait()

        def ahead(r):
            for k in (0, 1, 3):
                gather_v(r, k).wait_recv()
            for b in range(2):
                kv2[r, :, cols(b)] = dot(view[r], w[0, :, cols(1 + b)]).astype(bf16)

        each_row(ahead)

        def forward(r):
            entered(r)
            h = hin[r].astype(f32)
            n = norm_in(h, r, u2, s2, n2, 0, 1)
            q2[r] = dot(n, w[0, :, cols(0)]).astype(bf16) * SCALE
            allowed = seg_q[r] == seg_v[r]
            for p in range(pairs):
                c = cols(p, PAIR)
                v = slice(D + c.start, D + c.stop)
                out, kept = attend_pair(q2[r, :, c], kv2[r, :, c], kv2[r, :, v], allowed)
                a2[r, :, c] = out.astype(bf16)
                p2[r, p] = kept
            m = h + dot(a2[r], w[0, :, cols(3)]) + vec[4:5]
            n = norm_in(m, r, u1, s1, n1, 2, 3)
            q = (dot(n, w[1, :, cols(0)]) + vec[5:6]).astype(bf16)
            qkv1[r, :, cols(0)] = q * SCALE
            qkv1[r, :, cols(1)] = dot(n, w[1, :, cols(1)]).astype(bf16)
            qkv1[r, :, cols(2)] = dot(n, w[1, :, cols(2)]).astype(bf16)
            self_attend(r, qkv1, p1, a1)
            out = m + dot(a1[r], w[1, :, cols(3)]) + vec[6:7]
            records[r] = out.astype(bf16)
            forward_hop(r).start()

        each_row(forward)

        def backward(r):
            returned(r)
            e = gin[r]
            do1[r] = dot_t(e, w[1, :, cols(3)]).astype(bf16)
            self_attend_back(r, qkv1, p1, do1, dqkv1)
            dn = dot_t(dqkv1[r], w[1, :, : 3 * D])
            dmid = e.astype(f32) + norm_out(dn, r, u1, s1, 2)
            dm[r] = dmid.astype(bf16)
            norm_sums(dn, r, u1, 2, 3)
            gv[4:5] += column_sum(dmid)
            gv[5:6] += column_sum(dqkv1[r, :, cols(0)])
            gv[6:7] += column_sum(e)
            do2[r] = dot_t(dm[r], w[0, :, cols(3)]).astype(bf16)
            for p in range(pairs):
                c = cols(p, PAIR)
                v = slice(D + c.start, D + c.stop)
                dq, dk, dv = attend_pair_back(
                    q2[r, :, c], kv2[r, :, c], kv2[r, :, v], p2[r, p], do2[r, :, c]
                )
                dq2[r, :, c] = dq.astype(bf16)
                dkv2[r, :, c] = dk.astype(bf16)
                dkv2[r, :, v] = dv.astype(bf16)
            dn = dot_t(dq2[r], w[0, :, cols(0)])
            gout[r] = (dmid + norm_out(dn, r, u2, s2, 0)).astype(bf16)
            backward_hop(r).start()
            norm_sums(dn, r, u2, 0, 1)

        each_row(backward)

        def source_grad(r):
            R["dw"][r] = dot_t(dkv2[r], w[0, :, D : 3 * D]).astype(bf16)

        each_row(source_grad)
        G[7] = t_dot(flat(a1), flat(gin)).astype(bf16)
        for b in range(3):
            G[4 + b] = t_dot(flat(n1), dqkv1[:, :, cols(b)].reshape(B * T, D)).astype(bf16)
        G[3] = t_dot(flat(a2), flat(dm)).astype(bf16)
        G[0] = t_dot(flat(n2), flat(dq2)).astype(bf16)
        for b in range(2):
            wide = view.shape[1]
            G[1 + b] = t_dot(
                view[...].reshape(B * wide, D), dkv2[:, :, cols(b)].reshape(B * wide, D)
            ).astype(bf16)

    part_i, part_v = R["part_i"], R["part_v"]

    def scatter_i(k):
        return remote(
            gout.at[:, pl.ds(k * TS, TS)],
            part_i,
            R["si_send"].at[k],
            R["s_recv"].at[0],
            {"section": k},
        )

    def scatter_v(k):
        return remote(
            R["dw"].at[:, pl.ds(k * VS, VS)],
            part_v,
            R["sv_send"].at[k],
            R["s_recv"].at[1],
            {"section": k},
        )

    @pl.when(z == 0)
    def _():
        for k in range(1, S):
            scatter_i(k).start()
        part_i[...] = gout[:, :TS]

    @pl.when(z == 2)
    def _():
        for k in (0, 1, 3):
            scatter_v(k).start()
        part_v[...] = R["dw"][:, 2 * VS : 3 * VS]

    @pl.when(z != 0)
    def _():
        scatter_i(0).wait_recv()

    @pl.when(z != 2)
    def _():
        scatter_v(0).wait_recv()

    owed_i, owed_v = R["owed_i"], R["owed_v"]
    back = []
    for part, owed, arrive, s in (
        (part_i, owed_i, R["arr_i"], 4),
        (part_v, owed_v, R["arr_v"], 6),
    ):
        for t in range(B):
            owed[t] = sum(
                pick[r][t] * (1.0 - mix[r]) * part[r].astype(f32) for r in range(B)
            ).astype(bf16)
        copy = remote(owed, arrive, ex.at[s], ex.at[s + 1], far)
        copy.start()
        back.append(copy)
    for copy, part, arrive, out in (
        (back[0], part_i, R["arr_i"], in_grad),
        (back[1], part_v, R["arr_v"], view_grad),
    ):
        copy.wait_recv()
        for r in range(B):
            out[r] = (mix[r] * part[r].astype(f32) + arrive[r].astype(f32)).astype(bf16)
        copy.wait_send()

    @pl.when(z == 0)
    def _():
        for k in range(1, S):
            scatter_i(k).wait_send()

    @pl.when(z == 2)
    def _():
        for k in (0, 1, 3):
            scatter_v(k).wait_send()

    for r in range(B):

        @pl.when(z != 0)
        def _():
            gather_i(r, z).wait_send()
            backward_hop(r).wait_send()

        @pl.when(z != 2)
        def _():
            gather_v(r, z).wait_send()

        @pl.when(z != S - 1)
        def _():
            forward_hop(r).wait_send()


def on_device(inputs, other_view, mats, vectors, mixing, partner, segments, cotangent):
    B, TS, D = inputs.shape
    VS = other_view.shape[1]
    T = segments.shape[1]
    S = lax.axis_size("section")
    V = VS * S
    H = mats.shape[3]
    pairs = D // PAIR
    vmem = pl.BlockSpec(memory_space=pltpu.VMEM)
    smem = pl.BlockSpec(memory_space=pltpu.SMEM)
    hbm = pl.BlockSpec(memory_space=pl.ANY)
    args = {
        "inputs": (inputs, vmem),
        "other_view": (other_view, vmem),
        "mats": (mats, hbm),
        "vec": (vectors[0], vmem),
        "mixing": (mixing, smem),
        "partner": (partner, smem),
        "seg_q": (segments[:, :, None], vmem),
        "seg_k": (segments[:, None, :], vmem),
        "seg_v": (jnp.repeat(segments, V // T, axis=1)[:, None, :], vmem),
        "cot": (cotangent, vmem),
    }
    outs = {
        "records": (B, T, D, bf16),
        "in_grad": (B, TS, D, bf16),
        "view_grad": (B, VS, D, bf16),
        "G": (8, D, D, bf16),
        "gv": (8, D, f32),
    }
    dma = pltpu.SemaphoreType.DMA

    def buf(*shape, dtype=bf16):
        return pltpu.VMEM(shape, dtype)

    scratch = {
        "w": buf(2, D, H),
        "hin": buf(B, T, D),
        "gin": buf(B, T, D),
        "gout": buf(B, T, D),
        "far_i": buf(B, TS, D),
        "far_v": buf(B, VS, D),
        "stage_i": buf(B, TS, D),
        "stage_v": buf(B, VS, D),
        "part_i": buf(B, TS, D),
        "part_v": buf(B, VS, D),
        "owed_i": buf(B, TS, D),
        "owed_v": buf(B, VS, D),
        "arr_i": buf(B, TS, D),
        "arr_v": buf(B, VS, D),
        "view": buf(B, V, D),
        "dw": buf(B, V, D),
        "n1": buf(B, T, D),
        "u1": buf(B, T, D, dtype=f32),
        "s1": buf(B, T, 1, dtype=f32),
        "p1": buf(B, pairs, T, 2 * T, dtype=f32),
        "a1": buf(B, T, D),
        "qkv1": buf(B, T, 3 * D),
        "dqkv1": buf(B, T, 3 * D),
        "do1": buf(B, T, D),
        "n2": buf(B, T, D),
        "u2": buf(B, T, D, dtype=f32),
        "s2": buf(B, T, 1, dtype=f32),
        "p2": buf(B, pairs, T, 2 * V, dtype=f32),
        "a2": buf(B, T, D),
        "q2": buf(B, T, D),
        "dq2": buf(B, T, D),
        "kv2": buf(B, V, 2 * D),
        "dkv2": buf(B, V, 2 * D),
        "do2": buf(B, T, D),
        "dm": buf(B, T, D),
        "g": buf(B, T, H),
        "gp": buf(B, T, H, dtype=f32),
        "da": buf(B, T, H),
        "w_sem": dma((2,)),
        "ex_sem": dma((8,)),
        "gi_send": dma((B,)),
        "gi_recv": dma((B, S)),
        "gv_send": dma((B,)),
        "gv_recv": dma((B, S)),
        "f_send": dma((B,)),
        "f_recv": dma((B,)),
        "b_send": dma((B,)),
        "b_recv": dma((B,)),
        "si_send": dma((S,)),
        "sv_send": dma((S,)),
        "s_recv": dma((2,)),
    }
    names = list(args) + list(outs) + list(scratch)
    records, in_grad, view_grad, G, gv = pl.pallas_call(
        partial(kernel, names),
        out_shape=[jax.ShapeDtypeStruct(s[:-1], s[-1]) for s in outs.values()],
        in_specs=[spec for _, spec in args.values()],
        out_specs=[vmem] * len(outs),
        scratch_shapes=list(scratch.values()),
        compiler_params=pltpu.CompilerParams(
            collective_id=0, has_side_effects=True, vmem_limit_bytes=60 << 20
        ),
        name="relay",
    )(*[value for value, _ in args.values()])
    total = lax.psum(G, "dp").astype(f32)
    total = total.reshape(2, 4, D, D).transpose(0, 2, 1, 3).reshape(mats.shape)
    summed = lax.psum(gv[: vectors.shape[1]], "dp")
    return records[None], in_grad, view_grad, total, summed[None]


def solution(mesh):
    in_specs = (
        P("dp", "section", None),
        P("dp", "section", None),
        P("section", None, None, None),
        P("section", None, None),
        P("dp"),
        P("dp"),
        P("dp", None),
        P("dp", None, None),
    )
    out_specs = (
        P("section", "dp", None, None),
        P("dp", "section", None),
        P("dp", "section", None),
        P("section", None, None, None),
        P("section", None, None),
    )
    return jax.shard_map(
        on_device, mesh=mesh, in_specs=in_specs, out_specs=out_specs, check_vma=False
    )
```

```python
from functools import partial

import jax
import jax.numpy as jnp
from jax import lax
from jax.experimental import pallas as pl
from jax.experimental.pallas import tpu as pltpu
from jax.sharding import PartitionSpec as P

HEAD = 64
PAIR = 2 * HEAD
MESH = pl.DeviceIdType.MESH
bf16 = jnp.bfloat16
f32 = jnp.float32


def dot(a, b):
    return lax.dot_general(a, b, (((1,), (0,)), ((), ())), preferred_element_type=f32)


def dot_t(a, b):
    return lax.dot_general(a, b, (((1,), (1,)), ((), ())), preferred_element_type=f32)


def t_dot(a, b):
    return lax.dot_general(a, b, (((0,), (0,)), ((), ())), preferred_element_type=f32)


def row_mean(x):
    return jnp.sum(x, axis=-1, keepdims=True) * (1.0 / x.shape[-1])


def normalize(h):
    center = h - row_mean(h)
    scale = lax.rsqrt(row_mean(center * center) + 1e-06)
    return center * scale, scale


def normalize_back(grad, unit, scale, gain):
    inner = grad * gain
    return scale * (inner - row_mean(inner) - unit * row_mean(inner * unit))


def gelu_parts(a):
    cdf = 0.5 * (1.0 + lax.erf(a * (0.5**0.5)))
    pdf = jnp.exp(a * a * (-0.5)) * 0.3989422804014327
    return a * cdf, cdf + a * pdf


def halves(x):
    low = lax.broadcasted_iota(jnp.int32, x.shape, 1) < HEAD
    zero = jnp.zeros_like(x)
    return jnp.concatenate([jnp.where(low, x, zero), jnp.where(low, zero, x)], axis=0)


def softmax(scores, allowed):
    scores = jnp.where(allowed, scores, -1000000000.0)
    weights = jnp.exp(scores - jnp.max(scores, axis=-1, keepdims=True))
    return weights * (1.0 / jnp.sum(weights, axis=-1, keepdims=True))


def attend_pair(q, k, v, allowed):
    n = k.shape[0]
    scores = dot_t(q, halves(k))
    weights = jnp.concatenate(
        [softmax(scores[:, :n], allowed), softmax(scores[:, n:], allowed)], axis=1
    )
    return dot(weights.astype(bf16), halves(v)), weights


def attend_pair_back(q, k, v, weights, grad):
    n = k.shape[0]
    grad_weights = dot_t(grad, halves(v))
    product = weights * grad_weights
    parts = []
    for part in (slice(0, n), slice(n, 2 * n)):
        total = jnp.sum(product[:, part], axis=-1, keepdims=True)
        parts.append((product[:, part] - weights[:, part] * total).astype(bf16))
    grad_q = dot(jnp.concatenate(parts, axis=1), halves(k)) * (HEAD**-0.5)
    grad_k = t_dot(jnp.concatenate(parts, axis=0), halves(q))
    rounded = weights.astype(bf16)
    grad_v = t_dot(jnp.concatenate([rounded[:, :n], rounded[:, n:]], axis=0), halves(grad))
    return grad_q, grad_k, grad_v


def column_sum(x):
    return jnp.sum(x.astype(f32), axis=0, keepdims=True)


def kernel(names, fused, *refs):
    R = dict(zip(names, refs))
    inputs, other_view, mats, vec = (R[k] for k in ("inputs", "other_view", "mats", "vec"))
    mixing, partner, cot = R["mixing"], R["partner"], R["cot"]
    segments, seg_q, seg_v = R["segments"], R["seg_q"], R["seg_v"]
    records, in_grad, view_grad = R["records"], R["in_grad"], R["view_grad"]
    G, gv, w = R["G"], R["gv"], R["w"]
    hin, gin, gout = R["hin"], R["gin"], R["gout"]
    B, TS, D = inputs.shape
    VS = other_view.shape[1]
    T = records.shape[1]
    S = lax.axis_size("section")
    n_dp = lax.axis_size("dp")
    z = lax.axis_index("section")
    d = lax.axis_index("dp")
    far = {"dp": lax.rem(d + n_dp // 2, n_dp)}
    pairs = D // PAIR
    core, x_bit, y_bit = lax.rem(d, 2), lax.rem(d // 2, 2), d // 4
    beside = {"dp": d + 1 - 2 * core}
    x_next = {"dp": d + 2 - 4 * x_bit}

    def remote(src, dst, send, recv, device):
        return pltpu.make_async_remote_copy(
            src_ref=src,
            dst_ref=dst,
            send_sem=send,
            recv_sem=recv,
            device_id=device,
            device_id_type=MESH,
        )

    def table(t):
        return pltpu.make_async_copy(mats.at[0, t], w.at[t], R["w_sem"].at[t])

    table(0).start()
    table(1).start()

    barrier = pltpu.get_barrier_semaphore()
    others = [far] + [{"section": lax.rem(z + o, S)} for o in range(1, S)]
    if fused:
        others += [beside, x_next]
    for other in others:
        pl.semaphore_signal(barrier, inc=1, device_id=other, device_id_type=MESH)
    pl.semaphore_wait(barrier, len(others))

    ex = R["ex_sem"]
    far_i = remote(inputs, R["far_i"], ex.at[0], ex.at[1], far)
    far_v = remote(other_view, R["far_v"], ex.at[2], ex.at[3], far)
    far_i.start()
    far_v.start()
    gv[...] = jnp.zeros_like(gv)
    V = seg_v.shape[2]
    across = lax.broadcasted_iota(jnp.int32, (T, T), 1)
    down = lax.broadcasted_iota(jnp.int32, (T, T), 0)
    wide_across = lax.broadcasted_iota(jnp.int32, (T, V), 1)
    wide_down = lax.broadcasted_iota(jnp.int32, (T, V), 0)
    spread = (wide_across // (V // T) == wide_down).astype(f32)
    for r in range(B):
        ids = segments[r : r + 1].astype(f32)
        column = jnp.sum(jnp.where(across == down, ids, 0.0), axis=1, keepdims=True)
        seg_q[r] = column
        seg_v[r] = jnp.sum(spread * column, axis=0, keepdims=True)
    pick = [[(partner[r] == j).astype(f32) for j in range(B)] for r in range(B)]
    mix = [mixing[r] for r in range(B)]

    def blend(own, other, r):
        chosen = sum(pick[r][j] * other[j].astype(f32) for j in range(B))
        return (mix[r] * own[r].astype(f32) + (1.0 - mix[r]) * chosen).astype(bf16)

    def gather_i(r, source):
        return remote(
            R["stage_i"].at[r],
            hin.at[r, pl.ds(source * TS, TS)],
            R["gi_send"].at[r],
            R["gi_recv"].at[r, source],
            {"section": 0},
        )

    def gather_v(r, source):
        return remote(
            R["stage_v"].at[r],
            R["view"].at[r, pl.ds(source * VS, VS)],
            R["gv_send"].at[r],
            R["gv_recv"].at[r, source],
            {"section": 2},
        )

    far_i.wait_recv()
    for r in range(B):
        mixed = blend(inputs, R["far_i"], r)

        @pl.when(z == 0)
        def _():
            hin[r, :TS] = mixed

        @pl.when(z != 0)
        def _():
            R["stage_i"][r] = mixed
            gather_i(r, z).start()

    far_v.wait_recv()
    for r in range(B):
        mixed_view = blend(other_view, R["far_v"], r)

        @pl.when(z == 2)
        def _():
            R["view"][r, 2 * VS : 3 * VS] = mixed_view

        @pl.when(z != 2)
        def _():
            R["stage_v"][r] = mixed_view
            gather_v(r, z).start()

    far_i.wait_send()
    far_v.wait_send()

    def forward_hop(r):
        return remote(
            records.at[r], hin.at[r], R["f_send"].at[r], R["f_recv"].at[r], {"section": z + 1}
        )

    def backward_hop(r):
        return remote(
            gout.at[r], gin.at[r], R["b_send"].at[r], R["b_recv"].at[r], {"section": z - 1}
        )

    def entered(r):
        remote(
            hin.at[r], hin.at[r], R["f_send"].at[r], R["f_recv"].at[r], {"section": z - 1}
        ).wait_recv()

    def returned(r):
        remote(
            gin.at[r], gin.at[r], R["b_send"].at[r], R["b_recv"].at[r], {"section": z + 1}
        ).wait_recv()

    def each_row(step):
        lax.fori_loop(0, B, lambda r, c: (step(r), c)[1], 0)

    def cols(b, width=D):
        return slice(b * width, (b + 1) * width)

    def flat(x):
        return x[...].reshape(B * T, x.shape[2])

    def norm_in(h, r, unit, scale, normed, gain, shift):
        unit_value, scale_value = normalize(h)
        unit[r] = unit_value
        scale[r] = scale_value
        value = (unit_value * vec[gain : gain + 1] + vec[shift : shift + 1]).astype(bf16)
        normed[r] = value
        return value

    def norm_out(grad, r, unit, scale, gain):
        return normalize_back(grad, unit[r], scale[r], vec[gain : gain + 1])

    def norm_sums(grad, r, unit, gain, shift):
        gv[gain : gain + 1] += column_sum(grad * unit[r])
        gv[shift : shift + 1] += column_sum(grad)

    def self_attend(r, qkv, weights, attended):
        allowed = seg_q[r] == segments[pl.ds(r, 1)].astype(f32)
        for p in range(pairs):
            c = cols(p, PAIR)
            k = slice(D + c.start, D + c.stop)
            v = slice(2 * D + c.start, 2 * D + c.stop)
            out, kept = attend_pair(qkv[r, :, c], qkv[r, :, k], qkv[r, :, v], allowed)
            attended[r, :, c] = out.astype(bf16)
            weights[r, p] = kept

    def self_attend_back(r, qkv, weights, grad, dqkv):
        for p in range(pairs):
            c = cols(p, PAIR)
            k = slice(D + c.start, D + c.stop)
            v = slice(2 * D + c.start, 2 * D + c.stop)
            dq, dk, dv = attend_pair_back(
                qkv[r, :, c], qkv[r, :, k], qkv[r, :, v], weights[r, p], grad[r, :, c]
            )
            dqkv[r, :, c] = dq.astype(bf16)
            dqkv[r, :, k] = dk.astype(bf16)
            dqkv[r, :, v] = dv.astype(bf16)

    def core_send(b):
        rows = pl.ds(pl.multiple_of((1 - core) * half, half), half)
        return remote(G.at[b, rows], R["core_in"].at[b], *sems(0, b), beside)

    def sems(kind, b):
        return R["r_send"].at[kind, b], R["r_recv"].at[kind, b]

    half = D // 2

    def produce(b, value):
        G[b] = value.astype(bf16)
        if fused:
            core_send(b).start()

    n1, u1, s1, p1, a1 = R["n1"], R["u1"], R["s1"], R["p1"], R["a1"]
    qkv1, dqkv1, do1 = R["qkv1"], R["dqkv1"], R["do1"]
    n2, u2, s2, p2, a2 = R["n2"], R["u2"], R["s2"], R["p2"], R["a2"]
    q2, dq2, kv2, dkv2, do2 = R["q2"], R["dq2"], R["kv2"], R["dkv2"], R["do2"]
    view, dm = R["view"], R["dm"]
    g, gp, da = R["g"], R["gp"], R["da"]
    SCALE = HEAD**-0.5

    @pl.when(z == 0)
    def _():
        table(0).wait()
        table(1).wait()

        def forward(r):
            for k in range(1, S):
                gather_i(r, k).wait_recv()
            h = hin[r].astype(f32)
            n = norm_in(h, r, u1, s1, n1, 0, 1)
            q = (dot(n, w[0, :, cols(0)]) + vec[5:6]).astype(bf16)
            qkv1[r, :, cols(0)] = q * SCALE
            qkv1[r, :, cols(1)] = dot(n, w[0, :, cols(1)]).astype(bf16)
            qkv1[r, :, cols(2)] = (dot(n, w[0, :, cols(2)]) + vec[2:3]).astype(bf16)
            self_attend(r, qkv1, p1, a1)
            out = h + dot(a1[r], w[0, :, cols(3)]) + vec[4:5]
            records[r] = out.astype(bf16)
            forward_hop(r).start()

        each_row(forward)

        def backward(r):
            returned(r)
            e = gin[r]
            do1[r] = dot_t(e, w[0, :, cols(3)]).astype(bf16)
            self_attend_back(r, qkv1, p1, do1, dqkv1)
            dn = dot_t(dqkv1[r], w[0, :, : 3 * D])
            gout[r] = (e.astype(f32) + norm_out(dn, r, u1, s1, 0)).astype(bf16)
            norm_sums(dn, r, u1, 0, 1)
            gv[2:3] += column_sum(dqkv1[r, :, cols(2)])
            gv[4:5] += column_sum(e)
            gv[5:6] += column_sum(dqkv1[r, :, cols(0)])

        each_row(backward)
        for b in range(3):
            produce(b, t_dot(flat(n1), dqkv1[:, :, cols(b)].reshape(B * T, D)))
        produce(3, t_dot(flat(a1), flat(gin)))
        if fused:
            w[1] = jnp.zeros(w.shape[1:], bf16)
        else:
            for b in range(4, 8):
                G[b] = jnp.zeros((D, D), bf16)

    def feed_hidden(n, c):
        a = dot(n, w[0, :, cols(c)]) + vec[2 + c : 3 + c]
        return gelu_parts(a)

    def feed_grads(e_rows):
        def one(c, _):
            cc = pl.ds(pl.multiple_of(c * D, D), D)
            produce(4 + c, t_dot(flat(e_rows), g[:, :, cc].reshape(B * T, D)))
            produce(c, t_dot(flat(n1), da[:, :, cc].reshape(B * T, D)))
            return 0

        lax.fori_loop(0, 4, one, 0)

    def feed_sums(r, e):
        for c in range(4):
            gv[2 + c : 3 + c] += column_sum(da[r, :, cols(c)])
        gv[6:7] += column_sum(e)

    @pl.when(z == 1)
    def _():
        table(0).wait()
        table(1).wait()

        def forward(r):
            entered(r)
            h = hin[r].astype(f32)
            n = norm_in(h, r, u1, s1, n1, 0, 1)
            out = h + vec[6:7]
            for c in range(4):
                active, slope = feed_hidden(n, c)
                active = active.astype(bf16)
                g[r, :, cols(c)] = active
                gp[r, :, cols(c)] = slope
                out += dot_t(active, w[1, :, cols(c)])
            records[r] = out.astype(bf16)
            forward_hop(r).start()

        each_row(forward)

        def backward(r):
            returned(r)
            e = gin[r]
            dn = jnp.zeros((T, D), f32)
            for c in range(4):
                dg = dot(e, w[1, :, cols(c)])
                dc = (dg * gp[r, :, cols(c)]).astype(bf16)
                da[r, :, cols(c)] = dc
                dn += dot_t(dc, w[0, :, cols(c)])
            gout[r] = (e.astype(f32) + norm_out(dn, r, u1, s1, 0)).astype(bf16)
            backward_hop(r).start()
            norm_sums(dn, r, u1, 0, 1)
            feed_sums(r, e)

        each_row(backward)
        feed_grads(gin)

    @pl.when(z == 3)
    def _():
        table(0).wait()
        table(1).wait()

        def ahead(r):
            e = cot[r]
            for c in range(4):
                gp[r, :, cols(c)] = dot(e, w[1, :, cols(c)])

        each_row(ahead)

        def turn(r):
            entered(r)
            e = cot[r]
            n = norm_in(hin[r].astype(f32), r, u1, s1, n1, 0, 1)
            dn = jnp.zeros((T, D), f32)
            for c in range(4):
                active, slope = feed_hidden(n, c)
                g[r, :, cols(c)] = active.astype(bf16)
                dc = (gp[r, :, cols(c)] * slope).astype(bf16)
                da[r, :, cols(c)] = dc
                dn += dot_t(dc, w[0, :, cols(c)])
            gout[r] = (e.astype(f32) + norm_out(dn, r, u1, s1, 0)).astype(bf16)
            backward_hop(r).start()
            norm_sums(dn, r, u1, 0, 1)
            feed_sums(r, e)

        each_row(turn)

        def output(r):
            records[r] = (hin[r].astype(f32) + dot_t(g[r], w[1]) + vec[6:7]).astype(bf16)

        each_row(output)
        feed_grads(cot)

    @pl.when(z == 2)
    def _():
        table(0).wait()
        table(1).wait()

        def ahead(r):
            for k in (0, 1, 3):
                gather_v(r, k).wait_recv()
            for b in range(2):
                kv2[r, :, cols(b)] = dot(view[r], w[0, :, cols(1 + b)]).astype(bf16)

        each_row(ahead)

        def forward(r):
            entered(r)
            h = hin[r].astype(f32)
            n = norm_in(h, r, u2, s2, n2, 0, 1)
            q2[r] = dot(n, w[0, :, cols(0)]).astype(bf16) * SCALE
            allowed = seg_q[r] == seg_v[r]
            for p in range(pairs):
                c = cols(p, PAIR)
                v = slice(D + c.start, D + c.stop)
                out, kept = attend_pair(q2[r, :, c], kv2[r, :, c], kv2[r, :, v], allowed)
                a2[r, :, c] = out.astype(bf16)
                p2[r, p] = kept
            m = h + dot(a2[r], w[0, :, cols(3)]) + vec[4:5]
            n = norm_in(m, r, u1, s1, n1, 2, 3)
            q = (dot(n, w[1, :, cols(0)]) + vec[5:6]).astype(bf16)
            qkv1[r, :, cols(0)] = q * SCALE
            qkv1[r, :, cols(1)] = dot(n, w[1, :, cols(1)]).astype(bf16)
            qkv1[r, :, cols(2)] = dot(n, w[1, :, cols(2)]).astype(bf16)
            self_attend(r, qkv1, p1, a1)
            out = m + dot(a1[r], w[1, :, cols(3)]) + vec[6:7]
            records[r] = out.astype(bf16)
            forward_hop(r).start()

        each_row(forward)

        def backward(r):
            returned(r)
            e = gin[r]
            do1[r] = dot_t(e, w[1, :, cols(3)]).astype(bf16)
            self_attend_back(r, qkv1, p1, do1, dqkv1)
            dn = dot_t(dqkv1[r], w[1, :, : 3 * D])
            dmid = e.astype(f32) + norm_out(dn, r, u1, s1, 2)
            dm[r] = dmid.astype(bf16)
            norm_sums(dn, r, u1, 2, 3)
            gv[4:5] += column_sum(dmid)
            gv[5:6] += column_sum(dqkv1[r, :, cols(0)])
            gv[6:7] += column_sum(e)
            do2[r] = dot_t(dm[r], w[0, :, cols(3)]).astype(bf16)
            for p in range(pairs):
                c = cols(p, PAIR)
                v = slice(D + c.start, D + c.stop)
                dq, dk, dv = attend_pair_back(
                    q2[r, :, c], kv2[r, :, c], kv2[r, :, v], p2[r, p], do2[r, :, c]
                )
                dq2[r, :, c] = dq.astype(bf16)
                dkv2[r, :, c] = dk.astype(bf16)
                dkv2[r, :, v] = dv.astype(bf16)
            dn = dot_t(dq2[r], w[0, :, cols(0)])
            gout[r] = (dmid + norm_out(dn, r, u2, s2, 0)).astype(bf16)
            backward_hop(r).start()
            norm_sums(dn, r, u2, 0, 1)

        each_row(backward)

        def source_grad(r):
            R["dw"][r] = dot_t(dkv2[r], w[0, :, D : 3 * D]).astype(bf16)

        each_row(source_grad)
        produce(0, t_dot(flat(n2), flat(dq2)))
        for b in range(2):
            wide = view.shape[1]
            grads = dkv2[:, :, cols(b)].reshape(B * wide, D)
            produce(1 + b, t_dot(view[...].reshape(B * wide, D), grads))
        produce(3, t_dot(flat(a2), flat(dm)))
        for b in range(3):
            produce(4 + b, t_dot(flat(n1), dqkv1[:, :, cols(b)].reshape(B * T, D)))
        produce(7, t_dot(flat(a1), flat(gin)))

    part_i, part_v = R["part_i"], R["part_v"]

    def scatter_i(k):
        return remote(
            gout.at[:, pl.ds(k * TS, TS)],
            part_i,
            R["si_send"].at[k],
            R["s_recv"].at[0],
            {"section": k},
        )

    def scatter_v(k):
        return remote(
            R["dw"].at[:, pl.ds(k * VS, VS)],
            part_v,
            R["sv_send"].at[k],
            R["s_recv"].at[1],
            {"section": k},
        )

    @pl.when(z == 0)
    def _():
        for k in range(1, S):
            scatter_i(k).start()
        part_i[...] = gout[:, :TS]

    @pl.when(z == 2)
    def _():
        for k in (0, 1, 3):
            scatter_v(k).start()
        part_v[...] = R["dw"][:, 2 * VS : 3 * VS]

    def mixup_back():
        @pl.when(z != 0)
        def _():
            scatter_i(0).wait_recv()

        @pl.when(z != 2)
        def _():
            scatter_v(0).wait_recv()

        owed_i, owed_v = R["owed_i"], R["owed_v"]
        back = []
        for part, owed, arrive, s in (
            (part_i, owed_i, R["arr_i"], 4),
            (part_v, owed_v, R["arr_v"], 6),
        ):
            for t in range(B):
                owed[t] = sum(
                    pick[r][t] * (1.0 - mix[r]) * part[r].astype(f32) for r in range(B)
                ).astype(bf16)
            copy = remote(owed, arrive, ex.at[s], ex.at[s + 1], far)
            copy.start()
            back.append(copy)
        for copy, part, arrive, out in (
            (back[0], part_i, R["arr_i"], in_grad),
            (back[1], part_v, R["arr_v"], view_grad),
        ):
            copy.wait_recv()
            for r in range(B):
                out[r] = (mix[r] * part[r].astype(f32) + arrive[r].astype(f32)).astype(bf16)
            copy.wait_send()

    rx, ry, rx2, ry2, core_in = (R[k] for k in ("rx", "ry", "rx2", "ry2", "core_in"))
    quarter, eighth = half // 4, half // 8
    own = core * half
    a0, b0 = own, own + half // 2
    a_own, a_far = a0 + x_bit * quarter, a0 + (1 - x_bit) * quarter
    b_own, b_far = b0 + y_bit * quarter, b0 + (1 - y_bit) * quarter
    a_end, a_out = a_own + y_bit * eighth, a_own + (1 - y_bit) * eighth
    b_end, b_out = b_own + x_bit * eighth, b_own + (1 - x_bit) * eighth
    blocks = jnp.where(z == 0, 4, 8)

    def part(start, length):
        return pl.ds(pl.multiple_of(start, eighth), length)

    def final(b, start, length):
        return w.at[b // 4, part(start, length), pl.ds(pl.multiple_of(lax.rem(b, 4) * D, D), D)]

    def scatter_x(b):
        return remote(G.at[b, part(a_far, quarter)], rx.at[b], *sems(1, b), x_next)

    def scatter_y(b):
        return remote(G.at[b, part(b_far, quarter)], ry.at[b], *sems(2, b), far)

    def scatter_xy(b):
        return remote(G.at[b, part(a_out, eighth)], ry2.at[b], *sems(3, b), far)

    def scatter_yx(b):
        return remote(G.at[b, part(b_out, eighth)], rx2.at[b], *sems(4, b), x_next)

    def spread_y(b):
        return remote(final(b, a_end, eighth), final(b, a_end, eighth), *sems(5, b), far)

    def spread_x(b):
        return remote(final(b, b_end, eighth), final(b, b_end, eighth), *sems(6, b), x_next)

    def spread_yx(b):
        return remote(final(b, a_own, quarter), final(b, a_own, quarter), *sems(7, b), x_next)

    def spread_xy(b):
        return remote(final(b, b_own, quarter), final(b, b_own, quarter), *sems(8, b), far)

    def spread_core(b):
        return remote(final(b, own, half), final(b, own, half), *sems(9, b), beside)

    def add(b, start, length, arrived):
        rows = part(start, length)
        G[b, rows] = (G[b, rows].astype(f32) + arrived[b].astype(f32)).astype(bf16)

    def finish(b, start, arrived):
        rows = part(start, eighth)
        total = (G[b, rows].astype(f32) + arrived[b].astype(f32)).astype(bf16)
        w[b // 4, rows, pl.ds(pl.multiple_of(lax.rem(b, 4) * D, D), D)] = total

    def sum_core(b):
        core_send(b).wait_recv()
        add(b, own, half, core_in)
        scatter_x(b).start()
        scatter_y(b).start()

    def sum_first(b):
        scatter_x(b).wait_recv()
        add(b, a_own, quarter, rx)
        scatter_xy(b).start()
        scatter_y(b).wait_recv()
        add(b, b_own, quarter, ry)
        scatter_yx(b).start()

    def sum_second(b):
        scatter_xy(b).wait_recv()
        finish(b, a_end, ry2)
        spread_y(b).start()
        scatter_yx(b).wait_recv()
        finish(b, b_end, rx2)
        spread_x(b).start()

    def pass_on(b):
        spread_y(b).wait_recv()
        spread_yx(b).start()
        spread_x(b).wait_recv()
        spread_xy(b).start()

    def pass_core(b):
        spread_yx(b).wait_recv()
        spread_xy(b).wait_recv()
        spread_core(b).start()

    def arrive(b):
        spread_core(b).wait_recv()

    def sent(b):
        for copy in (core_send, scatter_x, scatter_y, scatter_xy, scatter_yx, spread_y):
            copy(b).wait_send()
        for copy in (spread_x, spread_yx, spread_xy, spread_core):
            copy(b).wait_send()

    def vector_round(k, device):
        return remote(gv, R["gv_in"].at[k], R["v_send"].at[k], R["v_recv"].at[k], device)

    def vector_sum(k, device):
        copy = vector_round(k, device)
        copy.wait()
        gv[...] += R["gv_in"][k]

    def each_block(step):
        lax.fori_loop(0, blocks, lambda b, c: (step(b), c)[1], 0)

    if fused:
        vector_round(0, beside).start()
        each_block(sum_core)
        vector_sum(0, beside)
        vector_round(1, x_next).start()
        each_block(sum_first)
        vector_sum(1, x_next)
        vector_round(2, far).start()
        each_block(sum_second)
        vector_sum(2, far)
        each_block(pass_on)
        mixup_back()
        each_block(pass_core)
        each_block(arrive)
        each_block(sent)
    else:
        mixup_back()
        for b in range(8):
            w[b // 4, :, cols(b % 4)] = G[b]

    @pl.when(z == 0)
    def _():
        for k in range(1, S):
            scatter_i(k).wait_send()

    @pl.when(z == 2)
    def _():
        for k in (0, 1, 3):
            scatter_v(k).wait_send()

    for r in range(B):

        @pl.when(z != 0)
        def _():
            gather_i(r, z).wait_send()
            backward_hop(r).wait_send()

        @pl.when(z != 2)
        def _():
            gather_v(r, z).wait_send()

        @pl.when(z != S - 1)
        def _():
            forward_hop(r).wait_send()


def on_device(inputs, other_view, mats, vectors, mixing, partner, segments, cotangent):
    B, TS, D = inputs.shape
    VS = other_view.shape[1]
    T = segments.shape[1]
    S = lax.axis_size("section")
    V = VS * S
    H = mats.shape[3]
    pairs = D // PAIR
    vmem = pl.BlockSpec(memory_space=pltpu.VMEM)
    smem = pl.BlockSpec(memory_space=pltpu.SMEM)
    hbm = pl.BlockSpec(memory_space=pl.ANY)
    args = {
        "inputs": (inputs, vmem),
        "other_view": (other_view, vmem),
        "mats": (mats, hbm),
        "vec": (vectors[0], vmem),
        "mixing": (mixing, smem),
        "partner": (partner, smem),
        "segments": (segments, vmem),
        "cot": (cotangent, vmem),
    }
    outs = {
        "records": (B, T, D, bf16),
        "in_grad": (B, TS, D, bf16),
        "view_grad": (B, VS, D, bf16),
        "gv": (8, D, f32),
        "w": (2, D, H, bf16),
    }
    dma = pltpu.SemaphoreType.DMA

    def buf(*shape, dtype=bf16):
        return pltpu.VMEM(shape, dtype)

    scratch = {
        "G": buf(8, D, D),
        "core_in": buf(8, D // 2, D),
        "rx": buf(8, D // 8, D),
        "ry": buf(8, D // 8, D),
        "rx2": buf(8, D // 16, D),
        "ry2": buf(8, D // 16, D),
        "gv_in": buf(3, 8, D, dtype=f32),
        "seg_q": buf(B, T, 1, dtype=f32),
        "seg_v": buf(B, 1, V, dtype=f32),
        "hin": buf(B, T, D),
        "gin": buf(B, T, D),
        "gout": buf(B, T, D),
        "far_i": buf(B, TS, D),
        "far_v": buf(B, VS, D),
        "stage_i": buf(B, TS, D),
        "stage_v": buf(B, VS, D),
        "part_i": buf(B, TS, D),
        "part_v": buf(B, VS, D),
        "owed_i": buf(B, TS, D),
        "owed_v": buf(B, VS, D),
        "arr_i": buf(B, TS, D),
        "arr_v": buf(B, VS, D),
        "view": buf(B, V, D),
        "dw": buf(B, V, D),
        "n1": buf(B, T, D),
        "u1": buf(B, T, D, dtype=f32),
        "s1": buf(B, T, 1, dtype=f32),
        "p1": buf(B, pairs, T, 2 * T, dtype=f32),
        "a1": buf(B, T, D),
        "qkv1": buf(B, T, 3 * D),
        "dqkv1": buf(B, T, 3 * D),
        "do1": buf(B, T, D),
        "n2": buf(B, T, D),
        "u2": buf(B, T, D, dtype=f32),
        "s2": buf(B, T, 1, dtype=f32),
        "p2": buf(B, pairs, T, 2 * V, dtype=f32),
        "a2": buf(B, T, D),
        "q2": buf(B, T, D),
        "dq2": buf(B, T, D),
        "kv2": buf(B, V, 2 * D),
        "dkv2": buf(B, V, 2 * D),
        "do2": buf(B, T, D),
        "dm": buf(B, T, D),
        "g": buf(B, T, H),
        "gp": buf(B, T, H, dtype=f32),
        "da": buf(B, T, H),
        "w_sem": dma((2,)),
        "ex_sem": dma((8,)),
        "gi_send": dma((B,)),
        "gi_recv": dma((B, S)),
        "gv_send": dma((B,)),
        "gv_recv": dma((B, S)),
        "f_send": dma((B,)),
        "f_recv": dma((B,)),
        "b_send": dma((B,)),
        "b_recv": dma((B,)),
        "si_send": dma((S,)),
        "sv_send": dma((S,)),
        "s_recv": dma((2,)),
        "r_send": dma((10, 8)),
        "r_recv": dma((10, 8)),
        "v_send": dma((3,)),
        "v_recv": dma((3,)),
    }
    names = list(args) + list(outs) + list(scratch)
    fused = lax.axis_size("dp") == 8
    records, in_grad, view_grad, gv, total = pl.pallas_call(
        partial(kernel, names, fused),
        out_shape=[
            pltpu.VMEM(s[:-1], s[-1]) if k == "w" else jax.ShapeDtypeStruct(s[:-1], s[-1])
            for k, s in outs.items()
        ],
        in_specs=[spec for _, spec in args.values()],
        out_specs=[vmem] * len(outs),
        scratch_shapes=list(scratch.values()),
        compiler_params=pltpu.CompilerParams(
            collective_id=0, has_side_effects=True, vmem_limit_bytes=50 << 20
        ),
        name="relay",
    )(*[value for value, _ in args.values()])
    gv = gv[: vectors.shape[1]]
    if not fused:
        total, gv = lax.psum((total, gv), "dp")
    wide = pl.pallas_call(
        widen,
        grid=(2, H // D),
        out_shape=jax.ShapeDtypeStruct(mats.shape, f32),
        in_specs=[vmem],
        out_specs=pl.BlockSpec((1, 1, D, D), lambda t, c: (0, t, 0, c)),
        compiler_params=pltpu.CompilerParams(vmem_limit_bytes=24 << 20),
        name="widen",
    )(total)
    return records[None], in_grad, view_grad, wide, gv[None]


def widen(total, wide):
    t, c, D = pl.program_id(0), pl.program_id(1), wide.shape[2]
    wide[0, 0] = total[t, :, pl.ds(pl.multiple_of(c * D, D), D)].astype(f32)


def solution(mesh):
    in_specs = (
        P("dp", "section", None),
        P("dp", "section", None),
        P("section", None, None, None),
        P("section", None, None),
        P("dp"),
        P("dp"),
        P("dp", None),
        P("dp", None, None),
    )
    out_specs = (
        P("section", "dp", None, None),
        P("dp", "section", None),
        P("dp", "section", None),
        P("section", None, None, None),
        P("section", None, None),
    )
    return jax.shard_map(
        on_device, mesh=mesh, in_specs=in_specs, out_specs=out_specs, check_vma=False
    )
```

```python
from functools import partial

import jax
import jax.numpy as jnp
from jax import lax
from jax.experimental import pallas as pl
from jax.experimental.pallas import tpu as pltpu
from jax.sharding import PartitionSpec as P

HEAD = 64
PAIR = 2 * HEAD
MESH = pl.DeviceIdType.MESH
bf16 = jnp.bfloat16
f32 = jnp.float32


def dot(a, b):
    return lax.dot_general(a, b, (((1,), (0,)), ((), ())), preferred_element_type=f32)


def dot_t(a, b):
    return lax.dot_general(a, b, (((1,), (1,)), ((), ())), preferred_element_type=f32)


def t_dot(a, b):
    return lax.dot_general(a, b, (((0,), (0,)), ((), ())), preferred_element_type=f32)


def row_mean(x):
    return jnp.sum(x, axis=-1, keepdims=True) * (1.0 / x.shape[-1])


def normalize(h):
    center = h - row_mean(h)
    scale = lax.rsqrt(row_mean(center * center) + 1e-06)
    return center * scale, scale


def normalize_back(grad, unit, scale, gain):
    inner = grad * gain
    return scale * (inner - row_mean(inner) - unit * row_mean(inner * unit))


def gelu_parts(a):
    cdf = 0.5 * (1.0 + lax.erf(a * (0.5**0.5)))
    pdf = jnp.exp(a * a * (-0.5)) * 0.3989422804014327
    return a * cdf, cdf + a * pdf


def halves(x):
    low = lax.broadcasted_iota(jnp.int32, x.shape, 1) < HEAD
    zero = jnp.zeros_like(x)
    return jnp.concatenate([jnp.where(low, x, zero), jnp.where(low, zero, x)], axis=0)


def softmax(scores, allowed):
    scores = jnp.where(allowed, scores, -1000000000.0)
    weights = jnp.exp(scores - jnp.max(scores, axis=-1, keepdims=True))
    return weights * (1.0 / jnp.sum(weights, axis=-1, keepdims=True))


def attend_pair(q, k, v, allowed):
    n = k.shape[0]
    scores = dot_t(q, halves(k))
    weights = jnp.concatenate(
        [softmax(scores[:, :n], allowed), softmax(scores[:, n:], allowed)], axis=1
    )
    return dot(weights.astype(bf16), halves(v)), weights


def score_grads(v, weights, grad):
    n = v.shape[0]
    grad_weights = dot_t(grad, halves(v))
    product = weights * grad_weights
    parts = []
    for part in (slice(0, n), slice(n, 2 * n)):
        total = jnp.sum(product[:, part], axis=-1, keepdims=True)
        parts.append((product[:, part] - weights[:, part] * total).astype(bf16))
    return jnp.concatenate(parts, axis=1)


def query_grads(k, grad_scores):
    return dot(grad_scores, halves(k)) * (HEAD**-0.5)


def stacked(x):
    n = x.shape[1] // 2
    return jnp.concatenate([x[:, :n], x[:, n:]], axis=0)


def key_grads(q, weights, grad, grad_scores):
    grad_k = t_dot(stacked(grad_scores), halves(q))
    grad_v = t_dot(stacked(weights.astype(bf16)), halves(grad))
    return grad_k, grad_v


def column_sum(x):
    return jnp.sum(x.astype(f32), axis=0, keepdims=True)


def kernel(names, fused, *refs):
    R = dict(zip(names, refs))
    inputs, other_view, mats, vec = (R[k] for k in ("inputs", "other_view", "mats", "vec"))
    mixing, partner, cot = R["mixing"], R["partner"], R["gin"]
    segments, seg_q, seg_v = R["segments"], R["seg_q"], R["seg_v"]
    records, in_grad, view_grad = R["records"], R["in_grad"], R["view_grad"]
    G, gv, w = R["G"], R["gv"], R["w"]
    wt = G
    hin, gin, gout = R["hin"], R["gin"], R["gout"]
    B, TS, D = inputs.shape
    VS = other_view.shape[1]
    T = segments.shape[1]
    V = seg_v.shape[2]
    S = lax.axis_size("section")
    n_dp = lax.axis_size("dp")
    z = lax.axis_index("section")
    d = lax.axis_index("dp")
    far = {"dp": lax.rem(d + n_dp // 2, n_dp)}
    pairs = D // PAIR
    CH = T // 2
    chunks = B * 2
    core, x_bit, y_bit = lax.rem(d, 2), lax.rem(d // 2, 2), d // 4
    beside = {"dp": d + 1 - 2 * core}
    x_next = {"dp": d + 2 - 4 * x_bit}

    def remote(src, dst, send, recv, device):
        return pltpu.make_async_remote_copy(
            src_ref=src,
            dst_ref=dst,
            send_sem=send,
            recv_sem=recv,
            device_id=device,
            device_id_type=MESH,
        )

    def block_columns(b):
        return pl.ds(b * D, D)

    def table(b):
        return pltpu.make_async_copy(
            mats.at[0, b // 4, :, block_columns(b % 4)], w.at[b], R["w_sem"].at[b]
        )

    def local(src, dst, k):
        return pltpu.make_async_copy(src, dst, R["l_sem"].at[k])

    def at(i, length):
        return pl.ds(pl.multiple_of(i * length, length), length)

    own_i = local(inputs, R["own_i"], 0)
    own_v = local(other_view, R["own_v"], 1)
    own_cot = local(R["cot"], gin, 2)
    barrier = pltpu.get_barrier_semaphore()
    others = [far] + [{"section": lax.rem(z + o, S)} for o in range(1, S)]
    if fused:
        others += [beside, x_next]
    for other in others:
        pl.semaphore_signal(barrier, inc=1, device_id=other, device_id_type=MESH)
    own_i.start()
    own_v.start()
    for b in range(8):
        table(b).start()

    @pl.when(z == S - 1)
    def _():
        own_cot.start()

    gv[...] = jnp.zeros_like(gv)
    pick = [[(partner[r] == j).astype(f32) for j in range(B)] for r in range(B)]
    mix = [mixing[r] for r in range(B)]
    pl.semaphore_wait(barrier, len(others))

    ex = R["ex_sem"]
    far_i = remote(inputs, R["far_i"], ex.at[0], ex.at[1], far)
    far_v = remote(other_view, R["far_v"], ex.at[2], ex.at[3], far)
    far_i.start()

    @pl.when(z == 0)
    def _():
        far_v.start()

    across = lax.broadcasted_iota(jnp.int32, (T, T), 1)
    down = lax.broadcasted_iota(jnp.int32, (T, T), 0)
    wide_across = lax.broadcasted_iota(jnp.int32, (T, V), 1)
    wide_down = lax.broadcasted_iota(jnp.int32, (T, V), 0)
    spread = (wide_across // (V // T) == wide_down).astype(f32)
    for r in range(B):
        ids = segments[r : r + 1].astype(f32)
        column = jnp.sum(jnp.where(across == down, ids, 0.0), axis=1, keepdims=True)
        seg_q[r] = column
        seg_v[r] = jnp.sum(spread * column, axis=0, keepdims=True)

    def blend(own, other, r):
        chosen = sum(pick[r][j] * other[j].astype(f32) for j in range(B))
        return (mix[r] * own[r].astype(f32) + (1.0 - mix[r]) * chosen).astype(bf16)

    def gather_i(r, source):
        return remote(
            R["stage_i"].at[r],
            hin.at[pl.ds(pl.multiple_of(r * T + source * TS, TS), TS)],
            R["gi_send"].at[r],
            R["gi_recv"].at[r, source],
            {"section": 0},
        )

    def gather_v(r, source):
        return remote(
            R["stage_v"].at[r],
            R["view"].at[pl.ds(pl.multiple_of(r * V + source * VS, VS), VS)],
            R["gv_send"].at[r],
            R["gv_recv"].at[r, source],
            {"section": 2},
        )

    own_i.wait()
    far_i.wait_recv()
    for r in range(B):
        mixed = blend(R["own_i"], R["far_i"], r)

        @pl.when(z == 0)
        def _():
            hin[r * T : r * T + TS] = mixed

        @pl.when(z != 0)
        def _():
            R["stage_i"][r] = mixed
            gather_i(r, z).start()

    @pl.when(z != 0)
    def _():
        far_v.start()

    own_v.wait()
    far_v.wait_recv()
    for r in range(B):
        mixed_view = blend(R["own_v"], R["far_v"], r)

        @pl.when(z == 2)
        def _():
            R["view"][r * V + 2 * VS : r * V + 3 * VS] = mixed_view

        @pl.when(z != 2)
        def _():
            R["stage_v"][r] = mixed_view
            gather_v(r, z).start()

    far_i.wait_send()
    far_v.wait_send()

    def forward_hop(i):
        part = at(i, CH)
        return remote(
            records.at[part],
            hin.at[part],
            R["f_send"].at[i],
            R["f_recv"].at[i],
            {"section": z + 1},
        )

    def backward_hop(i):
        part = at(i, CH)
        return remote(
            gout.at[part], gin.at[part], R["b_send"].at[i], R["b_recv"].at[i], {"section": z - 1}
        )

    def entered(i):
        part = hin.at[at(i, CH)]
        remote(
            part, part, R["f_send"].at[i], R["f_recv"].at[i], {"section": z - 1}
        ).wait_recv()

    def returned(i):
        part = gin.at[at(i, CH)]
        remote(
            part, part, R["b_send"].at[i], R["b_recv"].at[i], {"section": z + 1}
        ).wait_recv()

    def both(step, r):
        step(2 * r)
        step(2 * r + 1)

    def forward_hops(r):
        forward_hop(2 * r).start()
        forward_hop(2 * r + 1).start()

    def backward_hops(r):
        backward_hop(2 * r).start()
        backward_hop(2 * r + 1).start()

    def each_row(step):
        lax.fori_loop(0, B, lambda r, c: (step(r), c)[1], 0)

    def each_chunk(step):
        lax.fori_loop(0, chunks, lambda i, c: (step(i), c)[1], 0)

    def cols(b, width=D):
        return slice(b * width, (b + 1) * width)

    def tables_ready():
        for b in range(8):
            table(b).wait()

    def turned(first, last):
        def one(b, c):
            wt[b] = jnp.transpose(w[b])
            return c

        lax.fori_loop(first, last, one, 0)

    def norm_in(h, rows, unit, scale, normed, gain, shift):
        unit_value, scale_value = normalize(h)
        unit[rows] = unit_value
        scale[rows] = scale_value
        value = (unit_value * vec[gain] + vec[shift]).astype(bf16)
        normed[rows] = value
        return value

    def norm_out(grad, rows, unit, scale, gain):
        return normalize_back(grad, unit[rows], scale[rows], vec[gain])

    def norm_sums(grad, unit, gain, shift):
        gv[gain : gain + 1] = column_sum(grad[...] * unit[...])
        gv[shift : shift + 1] = column_sum(grad[...])

    def key_columns(p, start):
        return slice(start + p * PAIR, start + (p + 1) * PAIR)

    def self_attend(r, rows, qkv, weights, attended):
        allowed = seg_q[r] == segments[pl.ds(r, 1)].astype(f32)
        for p in range(pairs):
            c, k, v = (key_columns(p, start) for start in (0, D, 2 * D))
            out, kept = attend_pair(qkv[rows, c], qkv[rows, k], qkv[rows, v], allowed)
            attended[rows, c] = out.astype(bf16)
            weights[r, p] = kept

    def self_attend_back(r, rows, qkv, weights, grad, dqkv):
        for p in range(pairs):
            c, k, v = (key_columns(p, start) for start in (0, D, 2 * D))
            kept, do = weights[r, p], grad[rows, c]
            ds = score_grads(qkv[rows, v], kept, do)
            dqkv[rows, c] = query_grads(qkv[rows, k], ds).astype(bf16)
            dk, dv = key_grads(qkv[rows, c], kept, do, ds)
            dqkv[rows, k] = dk.astype(bf16)
            dqkv[rows, v] = dv.astype(bf16)

    half = D // 2

    def sems(kind, b):
        return R["r_send"].at[kind, b], R["r_recv"].at[kind, b]

    def core_send(b):
        rows = pl.ds(pl.multiple_of((1 - core) * half, half), half)
        return remote(G.at[b, rows], R["core_in"].at[b], *sems(0, b), beside)

    def produce(b, value):
        G[b] = value.astype(bf16)
        if fused:
            core_send(b).start()

    def follow(b):
        if fused:
            sum_core(b)

    part_i, part_v = R["part_i"], R["part_v"]

    def part_copy_i(r, k):
        return remote(
            gout.at[pl.ds(pl.multiple_of(r * T + k * TS, TS), TS)],
            part_i.at[r],
            R["si_send"].at[r, k],
            R["si_recv"].at[r],
            {"section": k},
        )

    def part_copy_v(r, k):
        return remote(
            R["dw"].at[pl.ds(pl.multiple_of(r * V + k * VS, VS), VS)],
            part_v.at[r],
            R["sv_send"].at[r, k],
            R["sv_recv"].at[r],
            {"section": k},
        )

    def scatter_i(r):
        for k in range(1, S):
            part_copy_i(r, k).start()

    def scatter_v(r):
        for k in (0, 1, 3):
            part_copy_v(r, k).start()

    rx, ry, rx2, ry2, core_in = (R[k] for k in ("rx", "ry", "rx2", "ry2", "core_in"))
    quarter, eighth = half // 4, half // 8
    own = core * half
    a0, b0 = own, own + half // 2
    a_own, a_far = a0 + x_bit * quarter, a0 + (1 - x_bit) * quarter
    b_own, b_far = b0 + y_bit * quarter, b0 + (1 - y_bit) * quarter
    a_end, a_out = a_own + y_bit * eighth, a_own + (1 - y_bit) * eighth
    b_end, b_out = b_own + x_bit * eighth, b_own + (1 - x_bit) * eighth
    blocks = jnp.where(z == 0, 4, 8)
    shift = jnp.where(z == 2, 4, 0)

    def part(start, length):
        return pl.ds(pl.multiple_of(start, eighth), length)

    def final(b, start, length):
        return w.at[b, part(start, length)]

    def scatter_x(b):
        return remote(G.at[b, part(a_far, quarter)], rx.at[b], *sems(1, b), x_next)

    def scatter_y(b):
        return remote(G.at[b, part(b_far, quarter)], ry.at[b], *sems(2, b), far)

    def scatter_xy(b):
        return remote(G.at[b, part(a_out, eighth)], ry2.at[b], *sems(3, b), far)

    def scatter_yx(b):
        return remote(G.at[b, part(b_out, eighth)], rx2.at[b], *sems(4, b), x_next)

    def spread_y(b):
        return remote(final(b, a_end, eighth), final(b, a_end, eighth), *sems(5, b), far)

    def spread_x(b):
        return remote(final(b, b_end, eighth), final(b, b_end, eighth), *sems(6, b), x_next)

    def spread_yx(b):
        return remote(final(b, a_own, quarter), final(b, a_own, quarter), *sems(7, b), x_next)

    def spread_xy(b):
        return remote(final(b, b_own, quarter), final(b, b_own, quarter), *sems(8, b), far)

    def spread_core(b):
        return remote(final(b, own, half), final(b, own, half), *sems(9, b), beside)

    def add(b, start, length, arrived):
        rows = part(start, length)
        G[b, rows] = (G[b, rows].astype(f32) + arrived[b].astype(f32)).astype(bf16)

    def finish(b, start, arrived):
        rows = part(start, eighth)
        total = (G[b, rows].astype(f32) + arrived[b].astype(f32)).astype(bf16)
        w[b, rows] = total

    def sum_core(b):
        core_send(b).wait_recv()
        add(b, own, half, core_in)
        scatter_x(b).start()
        scatter_y(b).start()

    n1, u1, s1, p1, a1 = R["n1"], R["u1"], R["s1"], R["p1"], R["a1"]
    qkv1, dqkv1, do1, dn1 = R["qkv1"], R["dqkv1"], R["do1"], R["dn1"]
    n2, u2, s2, a2 = R["n2"], R["u2"], R["s2"], R["a2"]
    q2, dq2, kv2, dkv2, do2, dn2 = (R[k] for k in ("q2", "dq2", "kv2", "dkv2", "do2", "dn2"))
    view, dm = R["view"], R["dm"]
    g, gp, da = R["g"], R["gp"], R["da"]
    p2, ds2 = gp, da
    wide_pair = 2 * V
    SCALE = HEAD**-0.5

    def wide_t(first, count):
        return wt[first : first + count].reshape(count * D, D)

    @pl.when(z == 0)
    def _():
        tables_ready()

        def forward(r):
            rows = at(r, T)
            for k in range(1, S):
                gather_i(r, k).wait_recv()
            h = hin[rows].astype(f32)
            n = norm_in(h, rows, u1, s1, n1, 0, 1)
            q = (dot(n, w[0]) + vec[5]).astype(bf16)
            qkv1[rows, cols(0)] = q * SCALE
            qkv1[rows, cols(1)] = dot(n, w[1]).astype(bf16)
            qkv1[rows, cols(2)] = (dot(n, w[2]) + vec[2]).astype(bf16)
            self_attend(r, rows, qkv1, p1, a1)
            out = h + dot(a1[rows], w[3]) + vec[4]
            records[rows] = out.astype(bf16)
            forward_hops(r)

        each_row(forward)
        turned(0, 4)

        def backward(r):
            rows = at(r, T)
            both(returned, r)
            e = gin[rows]
            do1[rows] = dot(e, wt[3]).astype(bf16)
            self_attend_back(r, rows, qkv1, p1, do1, dqkv1)
            dn = dot(dqkv1[rows], wide_t(0, 3))
            dn1[rows] = dn
            gout[rows] = (e.astype(f32) + norm_out(dn, rows, u1, s1, 0)).astype(bf16)
            scatter_i(r)

        each_row(backward)
        for b in range(3):
            produce(b, t_dot(n1[...], dqkv1[:, cols(b)]))
        follow(0)
        produce(3, t_dot(a1[...], gin[...]))
        for b in range(1, 4):
            follow(b)
        norm_sums(dn1, u1, 0, 1)
        gv[2:3] = column_sum(dqkv1[:, cols(2)])
        gv[4:5] = column_sum(gin[...])
        gv[5:6] = column_sum(dqkv1[:, cols(0)])
        for r in range(B):
            part_i[r] = gout[r * T : r * T + TS]
        if fused:
            for b in range(4, 8):
                w[b] = jnp.zeros((D, D), bf16)
        else:
            for b in range(4, 8):
                G[b] = jnp.zeros((D, D), bf16)

    def feed_hidden(n, c):
        a = dot(n, w[c]) + vec[2 + c]
        return gelu_parts(a)

    def feed_grads(first, last, left, right, start):
        def one(c, _):
            produce(first + c, t_dot(left[...], right[:, at(c, D)]))
            pl.when(first + c >= 2)(lambda: follow(first + c - 2))
            return 0

        lax.fori_loop(0, last - first, one, 0)

    def feed_sums():
        norm_sums(dn1, u1, 0, 1)
        for c in range(4):
            gv[2 + c : 3 + c] = column_sum(da[:, cols(c)])
        gv[6:7] = column_sum(gin[...])

    @pl.when(z == 1)
    def _():
        tables_ready()
        turned(0, 8)

        def forward(i):
            rows = at(i, CH)
            entered(i)
            h = hin[rows].astype(f32)
            n = norm_in(h, rows, u1, s1, n1, 0, 1)
            out = h + vec[6]
            for c in range(4):
                active, slope = feed_hidden(n, c)
                active = active.astype(bf16)
                g[rows, cols(c)] = active
                gp[rows, cols(c)] = slope
                out += dot(active, wt[4 + c])
            records[rows] = out.astype(bf16)
            forward_hop(i).start()

        each_chunk(forward)

        def backward(i):
            rows = at(i, CH)
            returned(i)
            e = gin[rows]
            dn = jnp.zeros((CH, D), f32)
            for c in range(4):
                dg = dot(e, w[4 + c])
                dc = (dg * gp[rows, cols(c)]).astype(bf16)
                da[rows, cols(c)] = dc
                dn += dot(dc, wt[c])
            dn1[rows] = dn
            gout[rows] = (e.astype(f32) + norm_out(dn, rows, u1, s1, 0)).astype(bf16)
            backward_hop(i).start()

        each_chunk(backward)
        feed_grads(0, 4, n1, da, 0)
        feed_grads(4, 8, gin, g, 4)
        follow(6)
        follow(7)
        feed_sums()

    @pl.when(z == 3)
    def _():
        tables_ready()
        turned(0, 4)
        own_cot.wait()

        def ahead(r):
            rows = at(r, T)
            e = cot[rows]
            for c in range(4):
                gp[rows, cols(c)] = dot(e, w[4 + c])

        each_row(ahead)

        def turn(i):
            rows = at(i, CH)
            entered(i)
            e = cot[rows]
            n = norm_in(hin[rows].astype(f32), rows, u1, s1, n1, 0, 1)
            dn = jnp.zeros((CH, D), f32)
            for c in range(4):
                active, slope = feed_hidden(n, c)
                g[rows, cols(c)] = active.astype(bf16)
                dc = (gp[rows, cols(c)] * slope).astype(bf16)
                da[rows, cols(c)] = dc
                dn += dot(dc, wt[c])
            dn1[rows] = dn
            gout[rows] = (e.astype(f32) + norm_out(dn, rows, u1, s1, 0)).astype(bf16)
            backward_hop(i).start()

        each_chunk(turn)
        feed_grads(0, 4, n1, da, 0)

        def output(r):
            rows = at(r, T)
            out = hin[rows].astype(f32) + vec[6]
            for c in range(4):
                out += dot_t(g[rows, cols(c)], w[4 + c])
            records[rows] = out.astype(bf16)

        each_row(output)
        feed_grads(4, 8, cot, g, 4)
        follow(6)
        follow(7)
        feed_sums()

    @pl.when(z == 2)
    def _():
        tables_ready()

        def ahead(r):
            wide = at(r, V)
            for k in (0, 1, 3):
                gather_v(r, k).wait_recv()
            for b in range(2):
                kv2[wide, cols(b)] = dot(view[wide], w[1 + b]).astype(bf16)

        each_row(ahead)
        turned(3, 8)
        wt[0] = jnp.transpose(w[0])

        def forward(r):
            rows, wide = at(r, T), at(r, V)
            both(entered, r)
            h = hin[rows].astype(f32)
            n = norm_in(h, rows, u2, s2, n2, 0, 1)
            q2[rows] = dot(n, w[0]).astype(bf16) * SCALE
            allowed = seg_q[r] == seg_v[r]
            for p in range(pairs):
                c, v = (key_columns(p, start) for start in (0, D))
                out, kept = attend_pair(q2[rows, c], kv2[wide, c], kv2[wide, v], allowed)
                a2[rows, c] = out.astype(bf16)
                p2[rows, cols(p, wide_pair)] = kept
            m = h + dot(a2[rows], w[3]) + vec[4]
            n = norm_in(m, rows, u1, s1, n1, 2, 3)
            q = (dot(n, w[4]) + vec[5]).astype(bf16)
            qkv1[rows, cols(0)] = q * SCALE
            qkv1[rows, cols(1)] = dot(n, w[5]).astype(bf16)
            qkv1[rows, cols(2)] = dot(n, w[6]).astype(bf16)
            self_attend(r, rows, qkv1, p1, a1)
            out = m + dot(a1[rows], w[7]) + vec[6]
            records[rows] = out.astype(bf16)
            forward_hops(r)

        each_row(forward)

        def backward(r):
            rows, wide = at(r, T), at(r, V)
            both(returned, r)
            e = gin[rows]
            do1[rows] = dot(e, wt[7]).astype(bf16)
            self_attend_back(r, rows, qkv1, p1, do1, dqkv1)
            dn = dot(dqkv1[rows], wide_t(4, 3))
            dn1[rows] = dn
            dmid = e.astype(f32) + norm_out(dn, rows, u1, s1, 2)
            dm[rows] = dmid
            do2[rows] = dot(dmid.astype(bf16), wt[3]).astype(bf16)
            for p in range(pairs):
                c, v = (key_columns(p, start) for start in (0, D))
                ds = score_grads(kv2[wide, v], p2[rows, cols(p, wide_pair)], do2[rows, c])
                ds2[rows, cols(p, wide_pair)] = ds
                dq2[rows, c] = query_grads(kv2[wide, c], ds).astype(bf16)
            dn = dot(dq2[rows], wt[0])
            dn2[rows] = dn
            gout[rows] = (dmid + norm_out(dn, rows, u2, s2, 0)).astype(bf16)
            backward_hops(r)

        each_row(backward)
        for b in range(3):
            produce(4 + b, t_dot(n1[...], dqkv1[:, cols(b)]))
        follow(4)
        produce(7, t_dot(a1[...], gin[...]))
        follow(5)

        def source_grad(r):
            rows, wide = at(r, T), at(r, V)
            for p in range(pairs):
                c, v = (key_columns(p, start) for start in (0, D))
                x = cols(p, wide_pair)
                dk, dv = key_grads(q2[rows, c], p2[rows, x], do2[rows, c], ds2[rows, x])
                dkv2[wide, c] = dk.astype(bf16)
                dkv2[wide, v] = dv.astype(bf16)
            dw = dot_t(dkv2[wide, cols(0)], w[1]) + dot_t(dkv2[wide, cols(1)], w[2])
            R["dw"][wide] = dw.astype(bf16)
            scatter_v(r)

        each_row(source_grad)
        for b in range(2):
            produce(b, t_dot(n2[...], dq2[...]) if b == 0 else t_dot(view[...], dkv2[:, cols(0)]))
            follow(6 + b)
        produce(2, t_dot(view[...], dkv2[:, cols(1)]))
        follow(0)
        produce(3, t_dot(a2[...], dm[...].astype(bf16)))
        for b in range(1, 4):
            follow(b)
        norm_sums(dn1, u1, 2, 3)
        norm_sums(dn2, u2, 0, 1)
        gv[4:5] = column_sum(dm[...])
        gv[5:6] = column_sum(dqkv1[:, cols(0)])
        gv[6:7] = column_sum(gin[...])
        for r in range(B):
            part_v[r] = R["dw"][r * V + 2 * VS : r * V + 3 * VS]

    owed_i, owed_v = R["owed_i"], R["owed_v"]
    owed_to = [
        remote(owed_i, R["arr_i"], ex.at[4], ex.at[5], far),
        remote(owed_v, R["arr_v"], ex.at[6], ex.at[7], far),
    ]

    def mixup_back():
        @pl.when(z != 0)
        def _():
            for r in range(B):
                part_copy_i(r, 0).wait_recv()

        @pl.when(z != 2)
        def _():
            for r in range(B):
                part_copy_v(r, 0).wait_recv()

        for part, owed, copy in zip((part_i, part_v), (owed_i, owed_v), owed_to):
            for t in range(B):
                owed[t] = sum(
                    pick[r][t] * (1.0 - mix[r]) * part[r].astype(f32) for r in range(B)
                ).astype(bf16)
            copy.start()

    def mixup_end():
        for part, arrived, out, copy in zip(
            (part_i, part_v), (R["arr_i"], R["arr_v"]), (in_grad, view_grad), owed_to
        ):
            copy.wait_recv()
            for r in range(B):
                out[r] = (mix[r] * part[r].astype(f32) + arrived[r].astype(f32)).astype(bf16)
            copy.wait_send()

    def sum_first(b):
        scatter_x(b).wait_recv()
        add(b, a_own, quarter, rx)
        scatter_xy(b).start()
        scatter_y(b).wait_recv()
        add(b, b_own, quarter, ry)
        scatter_yx(b).start()

    def sum_second(b):
        scatter_xy(b).wait_recv()
        finish(b, a_end, ry2)
        spread_y(b).start()
        scatter_yx(b).wait_recv()
        finish(b, b_end, rx2)
        spread_x(b).start()

    def pass_on(b):
        spread_y(b).wait_recv()
        spread_yx(b).start()
        spread_x(b).wait_recv()
        spread_xy(b).start()

    def pass_core(b):
        spread_yx(b).wait_recv()
        spread_xy(b).wait_recv()
        spread_core(b).start()

    def arrive(b):
        spread_core(b).wait_recv()

    def sent(b):
        for copy in (core_send, scatter_x, scatter_y, scatter_xy, scatter_yx, spread_y):
            copy(b).wait_send()
        for copy in (spread_x, spread_yx, spread_xy, spread_core):
            copy(b).wait_send()

    def vector_round(k, device):
        return remote(gv, R["gv_in"].at[k], R["v_send"].at[k], R["v_recv"].at[k], device)

    def vector_sum(k, device):
        copy = vector_round(k, device)
        copy.wait()
        gv[...] += R["gv_in"][k]

    def each_block(step):
        lax.fori_loop(0, blocks, lambda i, c: (step(lax.rem(i + shift, 8)), c)[1], 0)

    if fused:
        vector_round(0, beside).start()
        vector_sum(0, beside)
        vector_round(1, x_next).start()
        each_block(sum_first)
        vector_sum(1, x_next)
        vector_round(2, far).start()
        each_block(sum_second)
        vector_sum(2, far)
        mixup_back()
        each_block(pass_on)
        each_block(pass_core)
        each_block(arrive)
        mixup_end()
        each_block(sent)
    else:
        mixup_back()
        mixup_end()
        for b in range(8):
            w[b] = G[b]

    for i in range(vec.shape[0]):
        R["gv_out"][i] = gv[i : i + 1]

    @pl.when(z == 0)
    def _():
        for r in range(B):
            for k in range(1, S):
                part_copy_i(r, k).wait_send()

    @pl.when(z == 2)
    def _():
        for r in range(B):
            for k in (0, 1, 3):
                part_copy_v(r, k).wait_send()

    for r in range(B):

        @pl.when(z != 0)
        def _():
            gather_i(r, z).wait_send()

        @pl.when(z != 2)
        def _():
            gather_v(r, z).wait_send()

    for i in range(chunks):

        @pl.when(z != 0)
        def _():
            backward_hop(i).wait_send()

        @pl.when(z != S - 1)
        def _():
            forward_hop(i).wait_send()


def on_device(inputs, other_view, mats, vectors, mixing, partner, segments, cotangent):
    B, TS, D = inputs.shape
    VS = other_view.shape[1]
    T = segments.shape[1]
    S = lax.axis_size("section")
    V = VS * S
    H = mats.shape[3]
    pairs = D // PAIR
    vmem = pl.BlockSpec(memory_space=pltpu.VMEM)
    smem = pl.BlockSpec(memory_space=pltpu.SMEM)
    hbm = pl.BlockSpec(memory_space=pl.ANY)
    args = {
        "inputs": (inputs, hbm),
        "other_view": (other_view, hbm),
        "mats": (mats, hbm),
        "vec": (jnp.swapaxes(vectors, 0, 1), vmem),
        "mixing": (mixing, smem),
        "partner": (partner, smem),
        "segments": (segments, vmem),
        "cot": (cotangent.reshape(B * T, D), hbm),
    }
    outs = {
        "records": (B * T, D, bf16),
        "in_grad": (B, TS, D, bf16),
        "view_grad": (B, VS, D, bf16),
        "gv_out": (vectors.shape[1], 1, D, f32),
        "w": (8, D, D, bf16),
    }
    dma = pltpu.SemaphoreType.DMA

    def buf(*shape, dtype=bf16):
        return pltpu.VMEM(shape, dtype)

    scratch = {"G": buf(8, D, D), "core_in": buf(8, D // 2, D)}
    scratch |= {k: buf(8, D // 8, D) for k in ("rx", "ry")}
    scratch |= {k: buf(8, D // 16, D) for k in ("rx2", "ry2")}
    scratch |= {"gv": buf(8, D, dtype=f32), "gv_in": buf(3, 8, D, dtype=f32)}
    scratch |= {"seg_q": buf(B, T, 1, dtype=f32), "seg_v": buf(B, 1, V, dtype=f32)}
    for k in ("own", "far", "stage", "part", "owed", "arr"):
        scratch |= {k + "_i": buf(B, TS, D), k + "_v": buf(B, VS, D)}
    scratch |= {k: buf(B * V, D) for k in ("view", "dw")}
    for k in ("hin", "gin", "gout", "n1", "a1", "do1", "n2", "a2", "q2", "dq2", "do2"):
        scratch[k] = buf(B * T, D)
    scratch |= {k: buf(B * T, D, dtype=f32) for k in ("u1", "u2", "dn1", "dn2", "dm")}
    scratch |= {k: buf(B * T, 1, dtype=f32) for k in ("s1", "s2")}
    scratch |= {k: buf(B * T, 3 * D) for k in ("qkv1", "dqkv1")}
    scratch |= {k: buf(B * V, 2 * D) for k in ("kv2", "dkv2")}
    scratch["p1"] = buf(B, pairs, T, 2 * T, dtype=f32)
    W = max(H, 2 * V * pairs)
    scratch |= {"g": buf(B * T, H), "da": buf(B * T, W), "gp": buf(B * T, W, dtype=f32)}
    scratch |= {
        "w_sem": dma((8,)),
        "ex_sem": dma((8,)),
        "l_sem": dma((3,)),
        "gi_send": dma((B,)),
        "gi_recv": dma((B, S)),
        "gv_send": dma((B,)),
        "gv_recv": dma((B, S)),
        "f_send": dma((2 * B,)),
        "f_recv": dma((2 * B,)),
        "b_send": dma((2 * B,)),
        "b_recv": dma((2 * B,)),
        "si_send": dma((B, S)),
        "sv_send": dma((B, S)),
        "si_recv": dma((B,)),
        "sv_recv": dma((B,)),
        "r_send": dma((10, 8)),
        "r_recv": dma((10, 8)),
        "v_send": dma((3,)),
        "v_recv": dma((3,)),
    }
    names = list(args) + list(outs) + list(scratch)
    fused = lax.axis_size("dp") == 8
    *small, total = pl.pallas_call(
        partial(kernel, names, fused),
        out_shape=[pltpu.VMEM(s[:-1], s[-1]) for s in outs.values()],
        in_specs=[spec for _, spec in args.values()],
        out_specs=[vmem] * len(outs),
        scratch_shapes=list(scratch.values()),
        compiler_params=pltpu.CompilerParams(
            collective_id=0, has_side_effects=True, vmem_limit_bytes=50 << 20
        ),
        name="relay",
    )(*[value for value, _ in args.values()])
    if not fused:
        total, small[-1] = lax.psum((total, small[-1]), "dp")
    piece = D // 4
    wide, records, in_grad, view_grad, vector_grad = pl.pallas_call(
        widen,
        out_shape=[jax.ShapeDtypeStruct(mats.shape, f32)]
        + [jax.ShapeDtypeStruct(x.shape, x.dtype) for x in small],
        in_specs=[vmem] * 5,
        out_specs=[hbm] * 5,
        scratch_shapes=[pltpu.VMEM((4, piece, H), f32), dma((4,)), dma((4,))],
        compiler_params=pltpu.CompilerParams(vmem_limit_bytes=16 << 20),
        name="widen",
    )(total, *small)
    records = records.reshape(1, B, T, D)
    return records, in_grad, view_grad, wide, jnp.swapaxes(vector_grad, 0, 1)


def widen(total, *refs):
    small, wide, outs, slots, sems, small_sems = refs[:4], refs[4], refs[5:9], *refs[9:]
    held, piece, H = slots.shape
    D = total.shape[1]
    copies = [
        pltpu.make_async_copy(a, b, small_sems.at[i]) for i, (a, b) in enumerate(zip(small, outs))
    ]
    for copy in copies:
        copy.start()

    def write(i):
        t, rows = i * piece // D, pl.ds(i * piece % D, piece)
        return pltpu.make_async_copy(slots.at[i % held], wide.at[0, t, rows], sems.at[i % held])

    steps = 2 * D // piece
    for i in range(steps):
        if i >= held:
            write(i - held).wait()
        t, start = i * piece // D, i * piece % D
        for c in range(H // D):
            values = total[t * (H // D) + c, start : start + piece].astype(f32)
            slots[i % held, :, c * D : (c + 1) * D] = values
        write(i).start()
    for i in range(steps - held, steps):
        write(i).wait()
    for copy in copies:
        copy.wait()


def solution(mesh):
    in_specs = (
        P("dp", "section", None),
        P("dp", "section", None),
        P("section", None, None, None),
        P("section", None, None),
        P("dp"),
        P("dp"),
        P("dp", None),
        P("dp", None, None),
    )
    out_specs = (
        P("section", "dp", None, None),
        P("dp", "section", None),
        P("dp", "section", None),
        P("section", None, None, None),
        P("section", None, None),
    )
    return jax.shard_map(
        on_device, mesh=mesh, in_specs=in_specs, out_specs=out_specs, check_vma=False
    )
```

```python
from functools import partial

import jax
import jax.numpy as jnp
from jax import lax
from jax.experimental import pallas as pl
from jax.experimental.pallas import tpu as pltpu
from jax.sharding import PartitionSpec as P

HEAD = 64
PAIR = 2 * HEAD
MESH = pl.DeviceIdType.MESH
bf16 = jnp.bfloat16
f32 = jnp.float32


def dot(a, b):
    return lax.dot_general(a, b, (((1,), (0,)), ((), ())), preferred_element_type=f32)


def dot_t(a, b):
    return lax.dot_general(a, b, (((1,), (1,)), ((), ())), preferred_element_type=f32)


def t_dot(a, b):
    return lax.dot_general(a, b, (((0,), (0,)), ((), ())), preferred_element_type=f32)


def row_mean(x):
    return jnp.sum(x, axis=-1, keepdims=True) * (1.0 / x.shape[-1])


def normalize(h):
    center = h - row_mean(h)
    scale = lax.rsqrt(row_mean(center * center) + 1e-06)
    return center * scale, scale


def normalize_back(grad, unit, scale, gain):
    inner = grad * gain
    return scale * (inner - row_mean(inner) - unit * row_mean(inner * unit))


def gelu_parts(a):
    cdf = 0.5 * (1.0 + lax.erf(a * (0.5**0.5)))
    pdf = jnp.exp(a * a * (-0.5)) * 0.3989422804014327
    return a * cdf, cdf + a * pdf


def halves(x):
    low = lax.broadcasted_iota(jnp.int32, x.shape, 1) < HEAD
    zero = jnp.zeros_like(x)
    return jnp.concatenate([jnp.where(low, x, zero), jnp.where(low, zero, x)], axis=0)


def attend(queries, keys, values, allowed):
    n = keys[0].shape[0]
    scores = [dot_t(q, halves(k)) for q, k in zip(queries, keys)]
    split = [[jnp.where(allowed, x[:, h : h + n], -1000000000.0) for h in (0, n)] for x in scores]
    peaks = [[jnp.max(x, axis=-1, keepdims=True) for x in pair] for pair in split]
    raised = [[jnp.exp(x - m) for x, m in zip(*both)] for both in zip(split, peaks)]
    shares = [[1.0 / jnp.sum(x, axis=-1, keepdims=True) for x in pair] for pair in raised]
    weights = [
        jnp.concatenate([x * m for x, m in zip(*both)], axis=1) for both in zip(raised, shares)
    ]
    outs = [dot(x.astype(bf16), halves(v)) for x, v in zip(weights, values)]
    return outs, weights


def score_grads(values, weights, grads):
    n = values[0].shape[0]
    grad_weights = [dot_t(x, halves(v)) for x, v in zip(grads, values)]
    products = [x * y for x, y in zip(weights, grad_weights)]
    totals = [
        [jnp.sum(x[:, h : h + n], axis=-1, keepdims=True) for h in (0, n)] for x in products
    ]
    return [
        jnp.concatenate(
            [
                (x[:, h : h + n] - y[:, h : h + n] * total).astype(bf16)
                for h, total in zip((0, n), pair)
            ],
            axis=1,
        )
        for x, y, pair in zip(products, weights, totals)
    ]


def query_grads(keys, grad_scores):
    return [dot(x, halves(k)) * (HEAD**-0.5) for x, k in zip(grad_scores, keys)]


def stacked(x):
    n = x.shape[1] // 2
    return jnp.concatenate([x[:, :n], x[:, n:]], axis=0)


def key_grads(queries, weights, grads, grad_scores):
    grad_k = [t_dot(stacked(x), halves(q)) for x, q in zip(grad_scores, queries)]
    grad_v = [t_dot(stacked(x.astype(bf16)), halves(y)) for x, y in zip(weights, grads)]
    return grad_k, grad_v


def column_sum(x):
    return jnp.sum(x.astype(f32), axis=0, keepdims=True)


def kernel(names, fused, *refs):
    R = dict(zip(names, refs))
    inputs, other_view, mats, vec = (R[k] for k in ("inputs", "other_view", "mats", "vec"))
    mixing, partner, cot = R["mixing"], R["partner"], R["gin"]
    segments, seg_q, seg_v = R["segments"], R["seg_q"], R["seg_v"]
    records, in_grad, view_grad = R["records"], R["in_grad"], R["view_grad"]
    G, gv, w = R["G"], R["gv"], R["w"]
    wt = G
    hin, gin, gout = R["hin"], R["gin"], R["gout"]
    B, TS, D = inputs.shape
    VS = other_view.shape[1]
    T = segments.shape[1]
    V = seg_v.shape[2]
    S = lax.axis_size("section")
    n_dp = lax.axis_size("dp")
    z = lax.axis_index("section")
    d = lax.axis_index("dp")
    far = {"dp": lax.rem(d + n_dp // 2, n_dp)}
    pairs = D // PAIR
    CH = T // 2
    chunks = B * 2
    core, x_bit, y_bit = lax.rem(d, 2), lax.rem(d // 2, 2), d // 4
    beside = {"dp": d + 1 - 2 * core}
    x_next = {"dp": d + 2 - 4 * x_bit}

    def remote(src, dst, send, recv, device):
        return pltpu.make_async_remote_copy(
            src_ref=src,
            dst_ref=dst,
            send_sem=send,
            recv_sem=recv,
            device_id=device,
            device_id_type=MESH,
        )

    def block_columns(b):
        return pl.ds(b * D, D)

    def table(b):
        return pltpu.make_async_copy(
            mats.at[0, b // 4, :, block_columns(b % 4)], w.at[b], R["w_sem"].at[b]
        )

    def local(src, dst, k):
        return pltpu.make_async_copy(src, dst, R["l_sem"].at[k])

    def at(i, length):
        return pl.ds(pl.multiple_of(i * length, length), length)

    own_i = local(inputs, R["own_i"], 0)
    own_v = local(other_view, R["own_v"], 1)
    own_cot = local(R["cot"], gin, 2)
    barrier = pltpu.get_barrier_semaphore()
    others = [far] + [{"section": lax.rem(z + o, S)} for o in range(1, S)]
    if fused:
        others += [beside, x_next]
    for other in others:
        pl.semaphore_signal(barrier, inc=1, device_id=other, device_id_type=MESH)
    own_i.start()
    own_v.start()
    for b in range(8):
        table(b).start()

    @pl.when(z == S - 1)
    def _():
        own_cot.start()

    gv[...] = jnp.zeros_like(gv)
    pick = [[(partner[r] == j).astype(f32) for j in range(B)] for r in range(B)]
    mix = [mixing[r] for r in range(B)]
    pl.semaphore_wait(barrier, len(others))

    ex = R["ex_sem"]
    far_i = remote(inputs, R["far_i"], ex.at[0], ex.at[1], far)
    far_v = remote(other_view, R["far_v"], ex.at[2], ex.at[3], far)
    far_i.start()

    @pl.when(z == 0)
    def _():
        far_v.start()

    across = lax.broadcasted_iota(jnp.int32, (T, T), 1)
    down = lax.broadcasted_iota(jnp.int32, (T, T), 0)
    wide_across = lax.broadcasted_iota(jnp.int32, (T, V), 1)
    wide_down = lax.broadcasted_iota(jnp.int32, (T, V), 0)
    spread = (wide_across // (V // T) == wide_down).astype(f32)
    for r in range(B):
        ids = segments[r : r + 1].astype(f32)
        column = jnp.sum(jnp.where(across == down, ids, 0.0), axis=1, keepdims=True)
        seg_q[r] = column
        seg_v[r] = jnp.sum(spread * column, axis=0, keepdims=True)

    def blend(own, other, r):
        chosen = sum(pick[r][j] * other[j].astype(f32) for j in range(B))
        return (mix[r] * own[r].astype(f32) + (1.0 - mix[r]) * chosen).astype(bf16)

    def gather_i(r, source):
        return remote(
            R["stage_i"].at[r],
            hin.at[pl.ds(pl.multiple_of(r * T + source * TS, TS), TS)],
            R["gi_send"].at[r],
            R["gi_recv"].at[r, source],
            {"section": 0},
        )

    def gather_v(r, source):
        return remote(
            R["stage_v"].at[r],
            R["view"].at[pl.ds(pl.multiple_of(r * V + source * VS, VS), VS)],
            R["gv_send"].at[r],
            R["gv_recv"].at[r, source],
            {"section": 2},
        )

    own_i.wait()
    far_i.wait_recv()
    for r in range(B):
        mixed = blend(R["own_i"], R["far_i"], r)

        @pl.when(z == 0)
        def _():
            hin[r * T : r * T + TS] = mixed

        @pl.when(z != 0)
        def _():
            R["stage_i"][r] = mixed
            gather_i(r, z).start()

    @pl.when(z != 0)
    def _():
        far_v.start()

    own_v.wait()
    far_v.wait_recv()
    for r in range(B):
        mixed_view = blend(R["own_v"], R["far_v"], r)

        @pl.when(z == 2)
        def _():
            R["view"][r * V + 2 * VS : r * V + 3 * VS] = mixed_view

        @pl.when(z != 2)
        def _():
            R["stage_v"][r] = mixed_view
            gather_v(r, z).start()

    far_i.wait_send()
    far_v.wait_send()

    def forward_hop(i):
        part = at(i, CH)
        return remote(
            records.at[part],
            hin.at[part],
            R["f_send"].at[i],
            R["f_recv"].at[i],
            {"section": z + 1},
        )

    def backward_hop(i):
        part = at(i, CH)
        return remote(
            gout.at[part], gin.at[part], R["b_send"].at[i], R["b_recv"].at[i], {"section": z - 1}
        )

    def entered(i):
        part = hin.at[at(i, CH)]
        remote(
            part, part, R["f_send"].at[i], R["f_recv"].at[i], {"section": z - 1}
        ).wait_recv()

    def returned(i):
        part = gin.at[at(i, CH)]
        remote(
            part, part, R["b_send"].at[i], R["b_recv"].at[i], {"section": z + 1}
        ).wait_recv()

    def both(step, r):
        step(2 * r)
        step(2 * r + 1)

    def forward_hops(r):
        forward_hop(2 * r).start()
        forward_hop(2 * r + 1).start()

    def backward_hops(r):
        backward_hop(2 * r).start()
        backward_hop(2 * r + 1).start()

    def each_row(step):
        lax.fori_loop(0, B, lambda r, c: (step(r), c)[1], 0)

    def each_chunk(step):
        lax.fori_loop(0, chunks, lambda i, c: (step(i), c)[1], 0)

    def cols(b, width=D):
        return slice(b * width, (b + 1) * width)

    def tables_ready():
        for b in range(8):
            table(b).wait()

    def turned(first, last):
        def one(b, c):
            wt[b] = jnp.transpose(w[b])
            return c

        lax.fori_loop(first, last, one, 0)

    def norm_in(h, rows, unit, scale, normed, gain, shift):
        unit_value, scale_value = normalize(h)
        unit[rows] = unit_value
        scale[rows] = scale_value
        value = (unit_value * vec[gain] + vec[shift]).astype(bf16)
        normed[rows] = value
        return value

    def norm_out(grad, rows, unit, scale, gain):
        return normalize_back(grad, unit[rows], scale[rows], vec[gain])

    def norm_sums(grad, unit, gain, shift):
        gv[gain : gain + 1] = column_sum(grad[...] * unit[...])
        gv[shift : shift + 1] = column_sum(grad[...])

    def heads(ref, rows, start=0):
        return [ref[rows, start + p * PAIR : start + (p + 1) * PAIR] for p in range(pairs)]

    def put(ref, rows, values, start=0):
        width = values[0].shape[1]
        for p, value in enumerate(values):
            ref[rows, start + p * width : start + (p + 1) * width] = value.astype(ref.dtype)

    def self_attend(r, rows, qkv, weights, attended):
        allowed = seg_q[r] == segments[pl.ds(r, 1)].astype(f32)
        q, k, v = (heads(qkv, rows, start) for start in (0, D, 2 * D))
        out, kept = attend(q, k, v, allowed)
        put(attended, rows, out)
        put(weights, rows, kept)

    def held(weights, rows, n):
        return [weights[rows, cols(p, 2 * n)] for p in range(pairs)]

    def self_attend_back(r, rows, qkv, weights, grad, dqkv):
        q, k, v = (heads(qkv, rows, start) for start in (0, D, 2 * D))
        kept, do = held(weights, rows, T), heads(grad, rows)
        ds = score_grads(v, kept, do)
        dk, dv = key_grads(q, kept, do, ds)
        put(dqkv, rows, query_grads(k, ds))
        put(dqkv, rows, dk, D)
        put(dqkv, rows, dv, 2 * D)

    half = D // 2

    def sems(kind, b):
        return R["r_send"].at[kind, b], R["r_recv"].at[kind, b]

    def core_send(b):
        rows = pl.ds(pl.multiple_of((1 - core) * half, half), half)
        return remote(G.at[b, rows], R["core_in"].at[b], *sems(0, b), beside)

    def produce(b, value):
        G[b] = value.astype(bf16)
        if fused:
            core_send(b).start()

    def follow(b):
        if fused:
            sum_core(b)

    part_v = R["part_v"]

    VH = 2 * VS

    def part_copy(r, k):
        return remote(
            R["dw"].at[pl.ds(pl.multiple_of(r * V + k * VH, VH), VH)],
            part_v.at[r],
            R["sv_send"].at[r, k],
            R["sv_recv"].at[r],
            {"section": 3 * k},
        )

    def scatter_v(r):
        for k in range(2):
            part_copy(r, k).start()

    def hand_i(r, k):
        return remote(
            R["fin_i"].at[pl.ds(r * T + k * TS, TS)],
            in_grad.at[r],
            R["hi_send"].at[r, k],
            R["hi_recv"].at[r],
            {"section": k},
        )

    def hand_v(r, k):
        return remote(
            R["fin_v"].at[r, pl.ds((1 - k) * VS, VS)],
            view_grad.at[r],
            R["hv_send"].at[r, k],
            R["hv_recv"].at[r],
            {"section": 1 + k},
        )

    owed_i, owed_v = R["owed_i"], R["owed_v"]

    def owed_i_copy(r):
        rows = pl.ds(r * T, T)
        return remote(
            owed_i.at[rows], R["arr_i"].at[rows], R["oi_send"].at[r], R["oi_recv"].at[r], far
        )

    def owed_v_copy(r):
        return remote(
            owed_v.at[r], R["arr_v"].at[r], R["ov_send"].at[r], R["ov_recv"].at[r], far
        )

    def owed(t, rows):
        return sum(
            pick[r][t] * (1.0 - mix[r]) * rows[r].astype(f32) for r in range(B)
        ).astype(bf16)

    def combined(r, own, arrived):
        return (mix[r] * own.astype(f32) + arrived.astype(f32)).astype(bf16)

    def mixup_i():
        rows = [gout[r * T : (r + 1) * T] for r in range(B)]
        for t in range(B):
            owed_i[t * T : (t + 1) * T] = owed(t, rows)

    rx, ry, rx2, ry2, core_in = (R[k] for k in ("rx", "ry", "rx2", "ry2", "core_in"))
    quarter, eighth = half // 4, half // 8
    own = core * half
    a0, b0 = own, own + half // 2
    a_own, a_far = a0 + x_bit * quarter, a0 + (1 - x_bit) * quarter
    a_end, a_out = a_own + y_bit * eighth, a_own + (1 - y_bit) * eighth

    def turned_round(b):
        return jnp.where(b < jnp.where(z == 0, 2, jnp.where(z == 3, 1, 0)), 1, 0)

    def second_half(b):
        flip = turned_round(b)
        first = y_bit + flip * (x_bit - y_bit)
        then = x_bit + flip * (y_bit - x_bit)
        mine, other = b0 + first * quarter, b0 + (1 - first) * quarter
        return mine, other, mine + then * eighth, mine + (1 - then) * eighth

    def first_way(b):
        flip = turned_round(b)
        return {"dp": (1 - flip) * far["dp"] + flip * x_next["dp"]}

    def second_way(b):
        flip = turned_round(b)
        return {"dp": flip * far["dp"] + (1 - flip) * x_next["dp"]}
    LENT, TAKEN = 0, 4
    own_blocks = jnp.where(z == 0, 4, 8)
    blocks = jnp.where(z == 0, 5, jnp.where(z == 1, 7, 8))
    wrap = jnp.where(z == 0, 5, 8)
    shift = jnp.where(z == 2, 4, jnp.where(z == 1, 1, 0))
    shift_back = jnp.where(z == 0, TAKEN, shift)

    def lend():
        rows = part(own, half)
        return remote(
            G.at[LENT, rows], G.at[TAKEN, rows], R["lend_send"], R["lend_recv"], {"section": 0}
        )

    def give_back():
        rows = part(own, half)
        return remote(
            w.at[TAKEN, rows], w.at[LENT, rows], R["back_send"], R["back_recv"], {"section": 1}
        )

    def part(start, length):
        return pl.ds(pl.multiple_of(start, eighth), length)

    def final(b, start, length):
        return w.at[b, part(start, length)]

    def scatter_x(b):
        return remote(G.at[b, part(a_far, quarter)], rx.at[b], *sems(1, b), x_next)

    def scatter_y(b):
        rows = part(second_half(b)[1], quarter)
        return remote(G.at[b, rows], ry.at[b], *sems(2, b), first_way(b))

    def scatter_xy(b):
        return remote(G.at[b, part(a_out, eighth)], ry2.at[b], *sems(3, b), far)

    def scatter_yx(b):
        rows = part(second_half(b)[3], eighth)
        return remote(G.at[b, rows], rx2.at[b], *sems(4, b), second_way(b))

    def spread_y(b):
        return remote(final(b, a_end, eighth), final(b, a_end, eighth), *sems(5, b), far)

    def spread_x(b):
        rows = final(b, second_half(b)[2], eighth)
        return remote(rows, rows, *sems(6, b), second_way(b))

    def spread_yx(b):
        return remote(final(b, a_own, quarter), final(b, a_own, quarter), *sems(7, b), x_next)

    def spread_xy(b):
        rows = final(b, second_half(b)[0], quarter)
        return remote(rows, rows, *sems(8, b), first_way(b))

    def spread_core(b):
        return remote(final(b, own, half), final(b, own, half), *sems(9, b), beside)

    def add(b, start, length, arrived):
        rows = part(start, length)
        G[b, rows] = (G[b, rows].astype(f32) + arrived[b].astype(f32)).astype(bf16)

    def finish(b, start, arrived):
        rows = part(start, eighth)
        total = (G[b, rows].astype(f32) + arrived[b].astype(f32)).astype(bf16)
        w[b, rows] = total

    def sum_core(b):
        core_send(b).wait_recv()
        add(b, own, half, core_in)
        lent = (z == 1) & (b == LENT)

        @pl.when(lent)
        def _():
            lend().start()

        @pl.when(jnp.logical_not(lent))
        def _():
            scatter_x(b).start()
            scatter_y(b).start()

    def take():
        lend().wait_recv()
        scatter_x(TAKEN).start()
        scatter_y(TAKEN).start()

    n1, u1, s1, p1, a1 = R["n1"], R["u1"], R["s1"], R["p1"], R["a1"]
    qkv1, dqkv1, do1, dn1 = R["qkv1"], R["dqkv1"], R["do1"], R["dn1"]
    n2, u2, s2, a2 = R["n2"], R["u2"], R["s2"], R["a2"]
    q2, dq2, kv2, dkv2, do2, dn2 = (R[k] for k in ("q2", "dq2", "kv2", "dkv2", "do2", "dn2"))
    view, dm = R["view"], R["dm"]
    g, gp, da = R["g"], R["gp"], R["da"]
    p2, ds2 = gp, da
    SCALE = HEAD**-0.5

    def wide_t(first, count):
        return wt[first : first + count].reshape(count * D, D)

    @pl.when(z == 0)
    def _():
        tables_ready()

        def forward(r):
            rows = at(r, T)
            for k in range(1, S):
                gather_i(r, k).wait_recv()
            h = hin[rows].astype(f32)
            n = norm_in(h, rows, u1, s1, n1, 0, 1)
            q = (dot(n, w[0]) + vec[5]).astype(bf16)
            qkv1[rows, cols(0)] = q * SCALE
            qkv1[rows, cols(1)] = dot(n, w[1]).astype(bf16)
            qkv1[rows, cols(2)] = (dot(n, w[2]) + vec[2]).astype(bf16)
            self_attend(r, rows, qkv1, p1, a1)
            out = h + dot(a1[rows], w[3]) + vec[4]
            records[rows] = out.astype(bf16)
            forward_hops(r)

        each_row(forward)
        turned(0, 4)

        def backward(r):
            rows = at(r, T)
            both(returned, r)
            e = gin[rows]
            do1[rows] = dot(e, wt[3]).astype(bf16)
            self_attend_back(r, rows, qkv1, p1, do1, dqkv1)
            dn = dot(dqkv1[rows], wide_t(0, 3))
            dn1[rows] = dn
            gout[rows] = (e.astype(f32) + norm_out(dn, rows, u1, s1, 0)).astype(bf16)

        each_row(backward)
        for b in range(3):
            produce(b, t_dot(n1[...], dqkv1[:, cols(b)]))
        mixup_i()
        follow(0)
        owed_i_copy(0).start()
        produce(3, t_dot(a1[...], gin[...]))
        follow(1)
        for r in range(1, B):
            owed_i_copy(r).start()
        for b in range(2, 4):
            follow(b)
        norm_sums(dn1, u1, 0, 1)
        gv[2:3] = column_sum(dqkv1[:, cols(2)])
        gv[4:5] = column_sum(gin[...])
        gv[5:6] = column_sum(dqkv1[:, cols(0)])
        if fused:
            for b in range(5, 8):
                w[b] = jnp.zeros((D, D), bf16)
        else:
            for b in range(4, 8):
                G[b] = jnp.zeros((D, D), bf16)

    def feed_hidden(n, c):
        a = dot(n, w[c]) + vec[2 + c]
        return gelu_parts(a)

    def feed_grads(first, last, left, right, start):
        def one(c, _):
            produce(first + c, t_dot(left[...], right[:, at(c, D)]))
            pl.when(first + c >= 2)(lambda: follow(first + c - 2))
            return 0

        lax.fori_loop(0, last - first, one, 0)

    def feed_sums():
        norm_sums(dn1, u1, 0, 1)
        for c in range(4):
            gv[2 + c : 3 + c] = column_sum(da[:, cols(c)])
        gv[6:7] = column_sum(gin[...])

    @pl.when(z == 1)
    def _():
        tables_ready()
        turned(0, 8)

        def forward(i):
            rows = at(i, CH)
            entered(i)
            h = hin[rows].astype(f32)
            n = norm_in(h, rows, u1, s1, n1, 0, 1)
            out = h + vec[6]
            for c in range(4):
                active, slope = feed_hidden(n, c)
                active = active.astype(bf16)
                g[rows, cols(c)] = active
                gp[rows, cols(c)] = slope
                out += dot(active, wt[4 + c])
            records[rows] = out.astype(bf16)
            forward_hop(i).start()

        each_chunk(forward)

        def backward(i):
            rows = at(i, CH)
            returned(i)
            e = gin[rows]
            dn = jnp.zeros((CH, D), f32)
            for c in range(4):
                dg = dot(e, w[4 + c])
                dc = (dg * gp[rows, cols(c)]).astype(bf16)
                da[rows, cols(c)] = dc
                dn += dot(dc, wt[c])
            dn1[rows] = dn
            gout[rows] = (e.astype(f32) + norm_out(dn, rows, u1, s1, 0)).astype(bf16)
            backward_hop(i).start()

        each_chunk(backward)
        feed_grads(0, 4, n1, da, 0)
        feed_grads(4, 8, gin, g, 4)
        follow(6)
        follow(7)
        feed_sums()

    @pl.when(z == 3)
    def _():
        tables_ready()
        turned(0, 4)
        own_cot.wait()

        def ahead(r):
            rows = at(r, T)
            e = cot[rows]
            for c in range(4):
                gp[rows, cols(c)] = dot(e, w[4 + c])

        each_row(ahead)

        def turn(i):
            rows = at(i, CH)
            entered(i)
            e = cot[rows]
            n = norm_in(hin[rows].astype(f32), rows, u1, s1, n1, 0, 1)
            dn = jnp.zeros((CH, D), f32)
            for c in range(4):
                active, slope = feed_hidden(n, c)
                g[rows, cols(c)] = active.astype(bf16)
                dc = (gp[rows, cols(c)] * slope).astype(bf16)
                da[rows, cols(c)] = dc
                dn += dot(dc, wt[c])
            dn1[rows] = dn
            gout[rows] = (e.astype(f32) + norm_out(dn, rows, u1, s1, 0)).astype(bf16)
            backward_hop(i).start()

        each_chunk(turn)
        feed_grads(0, 4, n1, da, 0)

        def output(r):
            rows = at(r, T)
            out = hin[rows].astype(f32) + vec[6]
            for c in range(4):
                out += dot_t(g[rows, cols(c)], w[4 + c])
            records[rows] = out.astype(bf16)

        each_row(output)
        feed_grads(4, 8, cot, g, 4)
        follow(6)
        follow(7)
        feed_sums()

    @pl.when(z == 2)
    def _():
        tables_ready()

        def ahead(r):
            wide = at(r, V)
            for k in (0, 1, 3):
                gather_v(r, k).wait_recv()
            for b in range(2):
                kv2[wide, cols(b)] = dot(view[wide], w[1 + b]).astype(bf16)

        each_row(ahead)
        turned(3, 8)
        wt[0] = jnp.transpose(w[0])

        def forward(r):
            rows, wide = at(r, T), at(r, V)
            both(entered, r)
            h = hin[rows].astype(f32)
            n = norm_in(h, rows, u2, s2, n2, 0, 1)
            q2[rows] = dot(n, w[0]).astype(bf16) * SCALE
            keys, values = heads(kv2, wide), heads(kv2, wide, D)
            out, kept = attend(heads(q2, rows), keys, values, seg_q[r] == seg_v[r])
            put(a2, rows, out)
            put(p2, rows, kept)
            m = h + dot(a2[rows], w[3]) + vec[4]
            n = norm_in(m, rows, u1, s1, n1, 2, 3)
            q = (dot(n, w[4]) + vec[5]).astype(bf16)
            qkv1[rows, cols(0)] = q * SCALE
            qkv1[rows, cols(1)] = dot(n, w[5]).astype(bf16)
            qkv1[rows, cols(2)] = dot(n, w[6]).astype(bf16)
            self_attend(r, rows, qkv1, p1, a1)
            out = m + dot(a1[rows], w[7]) + vec[6]
            records[rows] = out.astype(bf16)
            forward_hops(r)

        each_row(forward)

        def backward(r):
            rows, wide = at(r, T), at(r, V)
            both(returned, r)
            e = gin[rows]
            do1[rows] = dot(e, wt[7]).astype(bf16)
            self_attend_back(r, rows, qkv1, p1, do1, dqkv1)
            dn = dot(dqkv1[rows], wide_t(4, 3))
            dn1[rows] = dn
            dmid = e.astype(f32) + norm_out(dn, rows, u1, s1, 2)
            dm[rows] = dmid
            do2[rows] = dot(dmid.astype(bf16), wt[3]).astype(bf16)
            ds = score_grads(heads(kv2, wide, D), held(p2, rows, V), heads(do2, rows))
            put(ds2, rows, ds)
            put(dq2, rows, query_grads(heads(kv2, wide), ds))
            dn = dot(dq2[rows], wt[0])
            dn2[rows] = dn
            gout[rows] = (dmid + norm_out(dn, rows, u2, s2, 0)).astype(bf16)
            backward_hops(r)

        each_row(backward)
        for b in range(3):
            produce(4 + b, t_dot(n1[...], dqkv1[:, cols(b)]))
        follow(4)
        produce(7, t_dot(a1[...], gin[...]))
        follow(5)

        def source_grad(r):
            rows, wide = at(r, T), at(r, V)
            dk, dv = key_grads(
                heads(q2, rows), held(p2, rows, V), heads(do2, rows), held(ds2, rows, V)
            )
            put(dkv2, wide, dk)
            put(dkv2, wide, dv, D)
            dw = dot_t(dkv2[wide, cols(0)], w[1]) + dot_t(dkv2[wide, cols(1)], w[2])
            R["dw"][wide] = dw.astype(bf16)

        each_row(source_grad)
        for b in range(2):
            produce(b, t_dot(n2[...], dq2[...]) if b == 0 else t_dot(view[...], dkv2[:, cols(0)]))
            follow(6 + b)
        produce(2, t_dot(view[...], dkv2[:, cols(1)]))
        follow(0)
        produce(3, t_dot(a2[...], dm[...].astype(bf16)))
        for b in range(1, 4):
            follow(b)
        norm_sums(dn1, u1, 2, 3)
        norm_sums(dn2, u2, 0, 1)
        each_row(scatter_v)
        gv[4:5] = column_sum(dm[...])
        gv[5:6] = column_sum(dqkv1[:, cols(0)])
        gv[6:7] = column_sum(gin[...])

    def mixup_v():
        for r in range(B):
            part_copy(r, 0).wait_recv()
        rows = [part_v[r] for r in range(B)]
        for t in range(B):
            owed_v[t] = owed(t, rows)

    def mixup_i_end():
        for r in range(B):
            owed_i_copy(r).wait()
        for r in range(B):
            rows = slice(r * T, (r + 1) * T)
            R["fin_i"][rows] = combined(r, gout[rows], R["arr_i"][rows])
        for r in range(B):
            for k in range(1, S):
                hand_i(r, k).start()
            in_grad[r] = R["fin_i"][r * T : r * T + TS]

    def mixup_v_end(k):
        for r in range(B):
            owed_v_copy(r).wait()
        for r in range(B):
            R["fin_v"][r] = combined(r, part_v[r], R["arr_v"][r])
        for r in range(B):
            hand_v(r, k).start()
            view_grad[r] = R["fin_v"][r, k * VS : (k + 1) * VS]

    def mixup_handed():
        for r in range(B):

            @pl.when(z != 0)
            def _():
                hand_i(r, 1).wait_recv()

            @pl.when((z == 1) | (z == 2))
            def _():
                hand_v(r, 0).wait_recv()

            @pl.when(z == 0)
            def _():
                for k in range(1, S):
                    hand_i(r, k).wait_send()

            for end, k in ((0, 0), (3, 1)):

                @pl.when(z == end)
                def _():
                    hand_v(r, k).wait_send()

    def sum_first(b):
        scatter_x(b).wait_recv()
        add(b, a_own, quarter, rx)
        scatter_xy(b).start()
        scatter_y(b).wait_recv()
        add(b, second_half(b)[0], quarter, ry)
        scatter_yx(b).start()

    def sum_second(b):
        scatter_xy(b).wait_recv()
        finish(b, a_end, ry2)
        spread_y(b).start()
        scatter_yx(b).wait_recv()
        finish(b, second_half(b)[2], rx2)
        spread_x(b).start()

        @pl.when((z == 3) & (b < B))
        def _():
            owed_v_copy(b).start()

    def pass_on(b):
        spread_y(b).wait_recv()
        spread_yx(b).start()
        spread_x(b).wait_recv()
        spread_xy(b).start()

        @pl.when((z == 0) & (b < B))
        def _():
            owed_v_copy(b).start()

    def pass_core(b):
        spread_yx(b).wait_recv()
        spread_xy(b).wait_recv()
        taken = (z == 0) & (b == TAKEN)

        @pl.when(taken)
        def _():
            give_back().start()

        @pl.when(jnp.logical_not(taken))
        def _():
            spread_core(b).start()

    def arrive(b):
        spread_core(b).wait_recv()

    def sent(b):
        for copy in (scatter_x, scatter_y, scatter_xy, scatter_yx, spread_y, spread_x):
            copy(b).wait_send()
        for copy in (spread_yx, spread_xy):
            copy(b).wait_send()

    def core_sent(b):
        core_send(b).wait_send()
        spread_core(b).wait_send()

    def vector_round(k, device):
        return remote(gv, R["gv_in"].at[k], R["v_send"].at[k], R["v_recv"].at[k], device)

    def vector_sum(k, device):
        copy = vector_round(k, device)
        copy.wait()
        gv[...] += R["gv_in"][k]

    def loop(first, last, step):
        lax.fori_loop(first, last, lambda i, c: (step(i), c)[1], 0)

    def each_block(step):
        loop(0, blocks, lambda i: step(lax.rem(i + shift, wrap)))

    def each_back(step):
        loop(0, blocks, lambda i: step(lax.rem(i + shift_back, wrap)))

    if fused:
        vector_round(0, beside).start()
        vector_sum(0, beside)
        vector_round(1, x_next).start()

        @pl.when(z == 0)
        def _():
            take()

        each_block(sum_first)
        vector_sum(1, x_next)
        vector_round(2, far).start()

        @pl.when(z == 3)
        def _():
            mixup_v()

        each_back(sum_second)
        vector_sum(2, far)

        @pl.when(z == 0)
        def _():
            mixup_i_end()
            mixup_v()

        each_back(pass_on)

        @pl.when(z == 3)
        def _():
            mixup_v_end(1)

        each_back(pass_core)

        @pl.when(z == 0)
        def _():
            mixup_v_end(0)


        @pl.when(z == 1)
        def _():
            give_back().wait_recv()
            spread_core(LENT).start()

        loop(0, own_blocks, arrive)
        mixup_handed()
        each_block(sent)
        loop(0, own_blocks, core_sent)

        @pl.when(z == 1)
        def _():
            lend().wait_send()

        @pl.when(z == 0)
        def _():
            give_back().wait_send()
            w[TAKEN] = jnp.zeros((D, D), bf16)

    else:
        @pl.when(z == 0)
        def _():
            mixup_i_end()

        @pl.when((z == 0) | (z == 3))
        def _():
            mixup_v()
            for r in range(B):
                owed_v_copy(r).start()

        for end, k in ((0, 0), (3, 1)):
            pl.when(z == end)(partial(mixup_v_end, k))
        mixup_handed()
        for b in range(8):
            w[b] = G[b]

    for i in range(vec.shape[0]):
        R["gv_out"][i] = gv[i : i + 1]

    @pl.when(z == 2)
    def _():
        for r in range(B):
            for k in range(2):
                part_copy(r, k).wait_send()

    for r in range(B):

        @pl.when(z != 0)
        def _():
            gather_i(r, z).wait_send()

        @pl.when(z != 2)
        def _():
            gather_v(r, z).wait_send()

    for i in range(chunks):

        @pl.when(z != 0)
        def _():
            backward_hop(i).wait_send()

        @pl.when(z != S - 1)
        def _():
            forward_hop(i).wait_send()


def on_device(inputs, other_view, mats, vectors, mixing, partner, segments, cotangent):
    B, TS, D = inputs.shape
    VS = other_view.shape[1]
    T = segments.shape[1]
    S = lax.axis_size("section")
    V = VS * S
    H = mats.shape[3]
    pairs = D // PAIR
    vmem = pl.BlockSpec(memory_space=pltpu.VMEM)
    smem = pl.BlockSpec(memory_space=pltpu.SMEM)
    hbm = pl.BlockSpec(memory_space=pl.ANY)
    args = {
        "inputs": (inputs, hbm),
        "other_view": (other_view, hbm),
        "mats": (mats, hbm),
        "vec": (jnp.swapaxes(vectors, 0, 1), vmem),
        "mixing": (mixing, smem),
        "partner": (partner, smem),
        "segments": (segments, vmem),
        "cot": (cotangent.reshape(B * T, D), hbm),
    }
    outs = {
        "records": (B * T, D, bf16),
        "in_grad": (B, TS, D, bf16),
        "view_grad": (B, VS, D, bf16),
        "gv_out": (vectors.shape[1], 1, D, f32),
        "w": (8, D, D, bf16),
    }
    dma = pltpu.SemaphoreType.DMA

    def buf(*shape, dtype=bf16):
        return pltpu.VMEM(shape, dtype)

    scratch = {"G": buf(8, D, D), "core_in": buf(8, D // 2, D)}
    scratch |= {k: buf(8, D // 8, D) for k in ("rx", "ry")}
    scratch |= {k: buf(8, D // 16, D) for k in ("rx2", "ry2")}
    scratch |= {"gv": buf(8, D, dtype=f32), "gv_in": buf(3, 8, D, dtype=f32)}
    scratch |= {"seg_q": buf(B, T, 1, dtype=f32), "seg_v": buf(B, 1, V, dtype=f32)}
    for k in ("own", "far", "stage"):
        scratch |= {k + "_i": buf(B, TS, D), k + "_v": buf(B, VS, D)}
    for k in ("owed", "arr", "fin"):
        scratch |= {k + "_i": buf(B * T, D), k + "_v": buf(B, 2 * VS, D)}
    scratch["part_v"] = buf(B, 2 * VS, D)
    scratch |= {k: buf(B * V, D) for k in ("view", "dw")}
    for k in ("hin", "gin", "gout", "n1", "a1", "do1", "n2", "a2", "q2", "dq2", "do2"):
        scratch[k] = buf(B * T, D)
    scratch |= {k: buf(B * T, D, dtype=f32) for k in ("u1", "u2", "dn1", "dn2", "dm")}
    scratch |= {k: buf(B * T, 1, dtype=f32) for k in ("s1", "s2")}
    scratch |= {k: buf(B * T, 3 * D) for k in ("qkv1", "dqkv1")}
    scratch |= {k: buf(B * V, 2 * D) for k in ("kv2", "dkv2")}
    scratch["p1"] = buf(B * T, 2 * T * pairs, dtype=f32)
    W = max(H, 2 * V * pairs)
    scratch |= {"g": buf(B * T, H), "da": buf(B * T, W), "gp": buf(B * T, W, dtype=f32)}
    scratch |= {
        "w_sem": dma((8,)),
        "ex_sem": dma((4,)),
        "oi_send": dma((B,)),
        "oi_recv": dma((B,)),
        "ov_send": dma((B,)),
        "ov_recv": dma((B,)),
        "l_sem": dma((3,)),
        "gi_send": dma((B,)),
        "gi_recv": dma((B, S)),
        "gv_send": dma((B,)),
        "gv_recv": dma((B, S)),
        "f_send": dma((2 * B,)),
        "f_recv": dma((2 * B,)),
        "b_send": dma((2 * B,)),
        "b_recv": dma((2 * B,)),
        "sv_send": dma((B, 2)),
        "sv_recv": dma((B,)),
        "hi_send": dma((B, S)),
        "hi_recv": dma((B,)),
        "hv_send": dma((B, 2)),
        "hv_recv": dma((B,)),
        "lend_send": dma,
        "lend_recv": dma,
        "back_send": dma,
        "back_recv": dma,
        "r_send": dma((10, 8)),
        "r_recv": dma((10, 8)),
        "v_send": dma((3,)),
        "v_recv": dma((3,)),
    }
    names = list(args) + list(outs) + list(scratch)
    fused = lax.axis_size("dp") == 8
    *small, total = pl.pallas_call(
        partial(kernel, names, fused),
        out_shape=[pltpu.VMEM(s[:-1], s[-1]) for s in outs.values()],
        in_specs=[spec for _, spec in args.values()],
        out_specs=[vmem] * len(outs),
        scratch_shapes=list(scratch.values()),
        compiler_params=pltpu.CompilerParams(
            collective_id=0, has_side_effects=True, vmem_limit_bytes=50 << 20
        ),
        name="relay",
    )(*[value for value, _ in args.values()])
    if not fused:
        total, small[-1] = lax.psum((total, small[-1]), "dp")
    piece = D // 4
    wide, records, in_grad, view_grad, vector_grad = pl.pallas_call(
        widen,
        out_shape=[jax.ShapeDtypeStruct(mats.shape, f32)]
        + [jax.ShapeDtypeStruct(x.shape, x.dtype) for x in small],
        in_specs=[vmem] * 5,
        out_specs=[hbm] * 5,
        scratch_shapes=[pltpu.VMEM((4, piece, H), f32), dma((4,)), dma((4,))],
        compiler_params=pltpu.CompilerParams(vmem_limit_bytes=16 << 20),
        name="widen",
    )(total, *small)
    records = records.reshape(1, B, T, D)
    return records, in_grad, view_grad, wide, jnp.swapaxes(vector_grad, 0, 1)


def widen(total, *refs):
    small, wide, outs, slots, sems, small_sems = refs[:4], refs[4], refs[5:9], *refs[9:]
    held, piece, H = slots.shape
    D = total.shape[1]
    copies = [
        pltpu.make_async_copy(a, b, small_sems.at[i]) for i, (a, b) in enumerate(zip(small, outs))
    ]
    for copy in copies:
        copy.start()

    def write(i):
        t, rows = i * piece // D, pl.ds(i * piece % D, piece)
        return pltpu.make_async_copy(slots.at[i % held], wide.at[0, t, rows], sems.at[i % held])

    steps = 2 * D // piece
    for i in range(steps):
        if i >= held:
            write(i - held).wait()
        t, start = i * piece // D, i * piece % D
        for c in range(H // D):
            values = total[t * (H // D) + c, start : start + piece].astype(f32)
            slots[i % held, :, c * D : (c + 1) * D] = values
        write(i).start()
    for i in range(steps - held, steps):
        write(i).wait()
    for copy in copies:
        copy.wait()


def solution(mesh):
    in_specs = (
        P("dp", "section", None),
        P("dp", "section", None),
        P("section", None, None, None),
        P("section", None, None),
        P("dp"),
        P("dp"),
        P("dp", None),
        P("dp", None, None),
    )
    out_specs = (
        P("section", "dp", None, None),
        P("dp", "section", None),
        P("dp", "section", None),
        P("section", None, None, None),
        P("section", None, None),
    )
    return jax.shard_map(
        on_device, mesh=mesh, in_specs=in_specs, out_specs=out_specs, check_vma=False
    )
```

```python
from functools import partial

import jax
import jax.numpy as jnp
from jax import lax
from jax.experimental import pallas as pl
from jax.experimental.pallas import tpu as pltpu
from jax.sharding import PartitionSpec as P

HEAD = 64
PAIR = 2 * HEAD
MESH = pl.DeviceIdType.MESH
bf16 = jnp.bfloat16
f32 = jnp.float32


def dot(a, b):
    return lax.dot_general(a, b, (((1,), (0,)), ((), ())), preferred_element_type=f32)


def dot_t(a, b):
    return lax.dot_general(a, b, (((1,), (1,)), ((), ())), preferred_element_type=f32)


def t_dot(a, b):
    return lax.dot_general(a, b, (((0,), (0,)), ((), ())), preferred_element_type=f32)


def row_mean(x):
    return jnp.sum(x, axis=-1, keepdims=True) * (1.0 / x.shape[-1])


def normalize(h):
    center = h - row_mean(h)
    scale = lax.rsqrt(row_mean(center * center) + 1e-06)
    return center * scale, scale


def normalize_back(grad, unit, scale, gain):
    inner = grad * gain
    return scale * (inner - row_mean(inner) - unit * row_mean(inner * unit))


def gelu_parts(a):
    cdf = 0.5 * (1.0 + lax.erf(a * (0.5**0.5)))
    pdf = jnp.exp(a * a * (-0.5)) * 0.3989422804014327
    return a * cdf, cdf + a * pdf


def halves(x):
    low = lax.broadcasted_iota(jnp.int32, x.shape, 1) < HEAD
    zero = jnp.zeros_like(x)
    return jnp.concatenate([jnp.where(low, x, zero), jnp.where(low, zero, x)], axis=0)


def attend(queries, keys, values, allowed):
    n = keys[0].shape[0]
    scores = [dot_t(q, halves(k)) for q, k in zip(queries, keys)]
    split = [[jnp.where(allowed, x[:, h : h + n], -1000000000.0) for h in (0, n)] for x in scores]
    peaks = [[jnp.max(x, axis=-1, keepdims=True) for x in pair] for pair in split]
    raised = [[jnp.exp(x - m) for x, m in zip(*both)] for both in zip(split, peaks)]
    shares = [[1.0 / jnp.sum(x, axis=-1, keepdims=True) for x in pair] for pair in raised]
    weights = [
        jnp.concatenate([x * m for x, m in zip(*both)], axis=1) for both in zip(raised, shares)
    ]
    outs = [dot(x.astype(bf16), halves(v)) for x, v in zip(weights, values)]
    return outs, weights


def score_grads(values, weights, grads):
    n = values[0].shape[0]
    grad_weights = [dot_t(x, halves(v)) for x, v in zip(grads, values)]
    products = [x * y for x, y in zip(weights, grad_weights)]
    totals = [
        [jnp.sum(x[:, h : h + n], axis=-1, keepdims=True) for h in (0, n)] for x in products
    ]
    return [
        jnp.concatenate(
            [
                (x[:, h : h + n] - y[:, h : h + n] * total).astype(bf16)
                for h, total in zip((0, n), pair)
            ],
            axis=1,
        )
        for x, y, pair in zip(products, weights, totals)
    ]


def query_grads(keys, grad_scores):
    return [dot(x, halves(k)) * (HEAD**-0.5) for x, k in zip(grad_scores, keys)]


def stacked(x):
    n = x.shape[1] // 2
    return jnp.concatenate([x[:, :n], x[:, n:]], axis=0)


def key_grads(queries, weights, grads, grad_scores):
    grad_k = [t_dot(stacked(x), halves(q)) for x, q in zip(grad_scores, queries)]
    grad_v = [t_dot(stacked(x.astype(bf16)), halves(y)) for x, y in zip(weights, grads)]
    return grad_k, grad_v


def column_sum(x):
    return jnp.sum(x.astype(f32), axis=0, keepdims=True)


def kernel(names, fused, *refs):
    R = dict(zip(names, refs))
    inputs, other_view, mats, vec = (R[k] for k in ("inputs", "other_view", "mats", "vec"))
    mixing, partner, cot = R["mixing"], R["partner"], R["gin"]
    segments, seg_q, seg_v = R["segments"], R["seg_q"], R["seg_v"]
    records, in_grad, view_grad = R["records"], R["in_grad"], R["view_grad"]
    G, gv, w = R["G"], R["gv"], R["w"]
    wt = G
    hin, gin, gout = R["hin"], R["gin"], R["gout"]
    B, TS, D = inputs.shape
    VS = other_view.shape[1]
    T = segments.shape[1]
    V = seg_v.shape[2]
    S = lax.axis_size("section")
    n_dp = lax.axis_size("dp")
    z = lax.axis_index("section")
    d = lax.axis_index("dp")
    far = {"dp": lax.rem(d + n_dp // 2, n_dp)}
    pairs = D // PAIR
    CH = T // 2
    chunks = B * 2
    core, x_bit, y_bit = lax.rem(d, 2), lax.rem(d // 2, 2), d // 4
    beside = {"dp": d + 1 - 2 * core}
    x_next = {"dp": d + 2 - 4 * x_bit}

    def remote(src, dst, send, recv, device):
        return pltpu.make_async_remote_copy(
            src_ref=src,
            dst_ref=dst,
            send_sem=send,
            recv_sem=recv,
            device_id=device,
            device_id_type=MESH,
        )

    def block_columns(b):
        return pl.ds(b * D, D)

    def table(b):
        return pltpu.make_async_copy(
            mats.at[0, b // 4, :, block_columns(b % 4)], w.at[b], R["w_sem"].at[b]
        )

    def local(src, dst, k):
        return pltpu.make_async_copy(src, dst, R["l_sem"].at[k])

    def at(i, length):
        return pl.ds(pl.multiple_of(i * length, length), length)

    own_i = local(inputs, R["own_i"], 0)
    own_v = local(other_view, R["own_v"], 1)
    own_cot = local(R["cot"], gin, 2)
    barrier = pltpu.get_barrier_semaphore()
    others = [far] + [{"section": lax.rem(z + o, S)} for o in range(1, S)]
    if fused:
        others += [beside, x_next]
    for other in others:
        pl.semaphore_signal(barrier, inc=1, device_id=other, device_id_type=MESH)
    own_i.start()
    own_v.start()

    gv[...] = jnp.zeros_like(gv)
    pick = [[(partner[r] == j).astype(f32) for j in range(B)] for r in range(B)]
    mix = [mixing[r] for r in range(B)]
    pl.semaphore_wait(barrier, len(others))

    ex = R["ex_sem"]
    far_i = remote(inputs, R["far_i"], ex.at[0], ex.at[1], far)
    far_v = remote(other_view, R["far_v"], ex.at[2], ex.at[3], far)
    far_i.start()

    @pl.when(z == 0)
    def _():
        far_v.start()

    across = lax.broadcasted_iota(jnp.int32, (T, T), 1)
    down = lax.broadcasted_iota(jnp.int32, (T, T), 0)
    wide_across = lax.broadcasted_iota(jnp.int32, (T, V), 1)
    wide_down = lax.broadcasted_iota(jnp.int32, (T, V), 0)
    spread = (wide_across // (V // T) == wide_down).astype(f32)
    for r in range(B):
        ids = segments[r : r + 1].astype(f32)
        column = jnp.sum(jnp.where(across == down, ids, 0.0), axis=1, keepdims=True)
        seg_q[r] = column
        seg_v[r] = jnp.sum(spread * column, axis=0, keepdims=True)

    def blend(own, other, r):
        chosen = sum(pick[r][j] * other[j].astype(f32) for j in range(B))
        return (mix[r] * own[r].astype(f32) + (1.0 - mix[r]) * chosen).astype(bf16)

    def gather_i(r, source):
        return remote(
            R["stage_i"].at[r],
            hin.at[pl.ds(pl.multiple_of(r * T + source * TS, TS), TS)],
            R["gi_send"].at[r],
            R["gi_recv"].at[r, source],
            {"section": 0},
        )

    def gather_v(r, source):
        return remote(
            R["stage_v"].at[r],
            R["view"].at[pl.ds(pl.multiple_of(r * V + source * VS, VS), VS)],
            R["gv_send"].at[r],
            R["gv_recv"].at[r, source],
            {"section": 2},
        )

    own_i.wait()
    far_i.wait_recv()
    for r in range(B):
        mixed = blend(R["own_i"], R["far_i"], r)

        @pl.when(z == 0)
        def _():
            hin[r * T : r * T + TS] = mixed

        @pl.when(z != 0)
        def _():
            R["stage_i"][r] = mixed
            gather_i(r, z).start()

    for b in range(8):
        table(b).start()

    @pl.when(z == S - 1)
    def _():
        own_cot.start()

    @pl.when(z != 0)
    def _():
        far_v.start()

    own_v.wait()
    far_v.wait_recv()
    for r in range(B):
        mixed_view = blend(R["own_v"], R["far_v"], r)

        @pl.when(z == 2)
        def _():
            R["view"][r * V + 2 * VS : r * V + 3 * VS] = mixed_view

        @pl.when(z != 2)
        def _():
            R["stage_v"][r] = mixed_view
            gather_v(r, z).start()

    far_i.wait_send()
    far_v.wait_send()

    def forward_hop(i):
        part = at(i, CH)
        return remote(
            records.at[part],
            hin.at[part],
            R["f_send"].at[i],
            R["f_recv"].at[i],
            {"section": z + 1},
        )

    def backward_hop(i):
        part = at(i, CH)
        return remote(
            gout.at[part], gin.at[part], R["b_send"].at[i], R["b_recv"].at[i], {"section": z - 1}
        )

    def entered(i):
        part = hin.at[at(i, CH)]
        remote(
            part, part, R["f_send"].at[i], R["f_recv"].at[i], {"section": z - 1}
        ).wait_recv()

    def returned(i):
        part = gin.at[at(i, CH)]
        remote(
            part, part, R["b_send"].at[i], R["b_recv"].at[i], {"section": z + 1}
        ).wait_recv()

    def both(step, r):
        step(2 * r)
        step(2 * r + 1)

    def forward_hops(r):
        forward_hop(2 * r).start()
        forward_hop(2 * r + 1).start()

    def backward_hops(r):
        backward_hop(2 * r).start()
        backward_hop(2 * r + 1).start()

    def each_row(step):
        lax.fori_loop(0, B, lambda r, c: (step(r), c)[1], 0)

    def each_chunk(step):
        lax.fori_loop(0, chunks, lambda i, c: (step(i), c)[1], 0)

    def cols(b, width=D):
        return slice(b * width, (b + 1) * width)

    def tables_ready():
        for b in range(8):
            table(b).wait()

    def turned(first, last):
        def one(b, c):
            wt[b] = jnp.transpose(w[b])
            return c

        lax.fori_loop(first, last, one, 0)

    def norm_in(h, rows, unit, scale, normed, gain, shift):
        unit_value, scale_value = normalize(h)
        unit[rows] = unit_value
        scale[rows] = scale_value
        value = (unit_value * vec[gain] + vec[shift]).astype(bf16)
        normed[rows] = value
        return value

    def norm_out(grad, rows, unit, scale, gain):
        return normalize_back(grad, unit[rows], scale[rows], vec[gain])

    def norm_sums(grad, unit, gain, shift):
        gv[gain : gain + 1] = column_sum(grad[...] * unit[...])
        gv[shift : shift + 1] = column_sum(grad[...])

    def heads(ref, rows, start=0):
        return [ref[rows, start + p * PAIR : start + (p + 1) * PAIR] for p in range(pairs)]

    def put(ref, rows, values, start=0):
        width = values[0].shape[1]
        for p, value in enumerate(values):
            ref[rows, start + p * width : start + (p + 1) * width] = value.astype(ref.dtype)

    def self_attend(r, rows, qkv, weights, attended):
        allowed = seg_q[r] == segments[pl.ds(r, 1)].astype(f32)
        q, k, v = (heads(qkv, rows, start) for start in (0, D, 2 * D))
        out, kept = attend(q, k, v, allowed)
        put(attended, rows, out)
        put(weights, rows, kept)

    def held(weights, rows, n):
        return [weights[rows, cols(p, 2 * n)] for p in range(pairs)]

    def self_attend_back(r, rows, qkv, weights, grad, dqkv):
        q, k, v = (heads(qkv, rows, start) for start in (0, D, 2 * D))
        kept, do = held(weights, rows, T), heads(grad, rows)
        ds = score_grads(v, kept, do)
        dk, dv = key_grads(q, kept, do, ds)
        put(dqkv, rows, query_grads(k, ds))
        put(dqkv, rows, dk, D)
        put(dqkv, rows, dv, 2 * D)

    half = D // 2

    def sems(kind, b):
        return R["r_send"].at[kind, b], R["r_recv"].at[kind, b]

    def core_send(b):
        rows = pl.ds(pl.multiple_of((1 - core) * half, half), half)
        return remote(G.at[b, rows], R["core_in"].at[b], *sems(0, b), beside)

    def produce(b, value):
        G[b] = value.astype(bf16)
        if fused:
            core_send(b).start()

    def follow(b):
        if fused:
            sum_core(b)

    part_v = R["part_v"]

    VH = 2 * VS

    def part_copy(r, k):
        return remote(
            R["dw"].at[pl.ds(pl.multiple_of(r * V + k * VH, VH), VH)],
            part_v.at[r],
            R["sv_send"].at[r, k],
            R["sv_recv"].at[r],
            {"section": 3 * k},
        )

    def scatter_v(r):
        for k in range(2):
            part_copy(r, k).start()

    def hand_i(r, k):
        return remote(
            R["fin_i"].at[pl.ds(r * T + k * TS, TS)],
            in_grad.at[r],
            R["hi_send"].at[r, k],
            R["hi_recv"].at[r],
            {"section": k},
        )

    def hand_v(r, k):
        return remote(
            R["fin_v"].at[r, pl.ds((1 - k) * VS, VS)],
            view_grad.at[r],
            R["hv_send"].at[r, k],
            R["hv_recv"].at[r],
            {"section": 1 + k},
        )

    owed_i, owed_v = R["owed_i"], R["owed_v"]

    def owed_i_copy(r):
        rows = pl.ds(r * T, T)
        return remote(
            owed_i.at[rows], R["arr_i"].at[rows], R["oi_send"].at[r], R["oi_recv"].at[r], far
        )

    def owed_v_copy(r):
        return remote(
            owed_v.at[r], R["arr_v"].at[r], R["ov_send"].at[r], R["ov_recv"].at[r], far
        )

    def owed(t, rows):
        return sum(
            pick[r][t] * (1.0 - mix[r]) * rows[r].astype(f32) for r in range(B)
        ).astype(bf16)

    def combined(r, own, arrived):
        return (mix[r] * own.astype(f32) + arrived.astype(f32)).astype(bf16)

    def mixup_i():
        rows = [gout[r * T : (r + 1) * T] for r in range(B)]
        for t in range(B):
            owed_i[t * T : (t + 1) * T] = owed(t, rows)

    rx, ry, rx2, ry2, core_in = (R[k] for k in ("rx", "ry", "rx2", "ry2", "core_in"))
    quarter, eighth = half // 4, half // 8
    own = core * half
    a0, b0 = own, own + half // 2
    a_own, a_far = a0 + x_bit * quarter, a0 + (1 - x_bit) * quarter
    a_end, a_out = a_own + y_bit * eighth, a_own + (1 - y_bit) * eighth

    def turned_round(b):
        return jnp.where(b < jnp.where(z == 0, 2, jnp.where(z == 3, 1, 0)), 1, 0)

    def second_half(b):
        flip = turned_round(b)
        first = y_bit + flip * (x_bit - y_bit)
        then = x_bit + flip * (y_bit - x_bit)
        mine, other = b0 + first * quarter, b0 + (1 - first) * quarter
        return mine, other, mine + then * eighth, mine + (1 - then) * eighth

    def first_way(b):
        flip = turned_round(b)
        return {"dp": (1 - flip) * far["dp"] + flip * x_next["dp"]}

    def second_way(b):
        flip = turned_round(b)
        return {"dp": flip * far["dp"] + (1 - flip) * x_next["dp"]}
    LENT, TAKEN = 0, 4
    own_blocks = jnp.where(z == 0, 4, 8)
    blocks = jnp.where(z == 0, 5, jnp.where(z == 1, 7, 8))
    wrap = jnp.where(z == 0, 5, 8)
    shift = jnp.where(z == 2, 4, jnp.where(z == 1, 1, 0))
    shift_back = jnp.where(z == 0, TAKEN, shift)

    def lend():
        rows = part(own, half)
        return remote(
            G.at[LENT, rows], G.at[TAKEN, rows], R["lend_send"], R["lend_recv"], {"section": 0}
        )

    def give_back():
        rows = part(own, half)
        return remote(
            w.at[TAKEN, rows], w.at[LENT, rows], R["back_send"], R["back_recv"], {"section": 1}
        )

    def part(start, length):
        return pl.ds(pl.multiple_of(start, eighth), length)

    def final(b, start, length):
        return w.at[b, part(start, length)]

    def scatter_x(b):
        return remote(G.at[b, part(a_far, quarter)], rx.at[b], *sems(1, b), x_next)

    def scatter_y(b):
        rows = part(second_half(b)[1], quarter)
        return remote(G.at[b, rows], ry.at[b], *sems(2, b), first_way(b))

    def scatter_xy(b):
        return remote(G.at[b, part(a_out, eighth)], ry2.at[b], *sems(3, b), far)

    def scatter_yx(b):
        rows = part(second_half(b)[3], eighth)
        return remote(G.at[b, rows], rx2.at[b], *sems(4, b), second_way(b))

    def spread_y(b):
        return remote(final(b, a_end, eighth), final(b, a_end, eighth), *sems(5, b), far)

    def spread_x(b):
        rows = final(b, second_half(b)[2], eighth)
        return remote(rows, rows, *sems(6, b), second_way(b))

    def spread_yx(b):
        return remote(final(b, a_own, quarter), final(b, a_own, quarter), *sems(7, b), x_next)

    def spread_xy(b):
        rows = final(b, second_half(b)[0], quarter)
        return remote(rows, rows, *sems(8, b), first_way(b))

    def spread_core(b, k):
        rows = final(b, own + k * (half // 2), half // 2)
        return remote(rows, rows, *sems(9 + k, b), beside)

    def add(b, start, length, arrived):
        rows = part(start, length)
        G[b, rows] = (G[b, rows].astype(f32) + arrived[b].astype(f32)).astype(bf16)

    def finish(b, start, arrived):
        rows = part(start, eighth)
        total = (G[b, rows].astype(f32) + arrived[b].astype(f32)).astype(bf16)
        w[b, rows] = total

    def sum_core(b):
        core_send(b).wait_recv()
        add(b, own, half, core_in)
        lent = (z == 1) & (b == LENT)

        @pl.when(lent)
        def _():
            lend().start()

        @pl.when(jnp.logical_not(lent))
        def _():
            scatter_x(b).start()
            scatter_y(b).start()

    def take():
        lend().wait_recv()
        scatter_x(TAKEN).start()
        scatter_y(TAKEN).start()

    n1, u1, s1, p1, a1 = R["n1"], R["u1"], R["s1"], R["p1"], R["a1"]
    qkv1, dqkv1, do1, dn1 = R["qkv1"], R["dqkv1"], R["do1"], R["dn1"]
    n2, u2, s2, a2 = R["n2"], R["u2"], R["s2"], R["a2"]
    q2, dq2, kv2, dkv2, do2, dn2 = (R[k] for k in ("q2", "dq2", "kv2", "dkv2", "do2", "dn2"))
    view, dm = R["view"], R["dm"]
    g, gp, da = R["g"], R["gp"], R["da"]
    p2, ds2 = gp, da
    SCALE = HEAD**-0.5

    def wide_t(first, count):
        return wt[first : first + count].reshape(count * D, D)

    @pl.when(z == 0)
    def _():
        tables_ready()

        def forward(r):
            rows = at(r, T)
            for k in range(1, S):
                gather_i(r, k).wait_recv()
            h = hin[rows].astype(f32)
            n = norm_in(h, rows, u1, s1, n1, 0, 1)
            q = (dot(n, w[0]) + vec[5]).astype(bf16)
            qkv1[rows, cols(0)] = q * SCALE
            qkv1[rows, cols(1)] = dot(n, w[1]).astype(bf16)
            qkv1[rows, cols(2)] = (dot(n, w[2]) + vec[2]).astype(bf16)
            self_attend(r, rows, qkv1, p1, a1)
            out = h + dot(a1[rows], w[3]) + vec[4]
            records[rows] = out.astype(bf16)
            forward_hops(r)

        each_row(forward)
        turned(0, 4)

        def backward(r):
            rows = at(r, T)
            both(returned, r)
            e = gin[rows]
            do1[rows] = dot(e, wt[3]).astype(bf16)
            self_attend_back(r, rows, qkv1, p1, do1, dqkv1)
            dn = dot(dqkv1[rows], wide_t(0, 3))
            dn1[rows] = dn
            gout[rows] = (e.astype(f32) + norm_out(dn, rows, u1, s1, 0)).astype(bf16)

        each_row(backward)
        for b in range(3):
            produce(b, t_dot(n1[...], dqkv1[:, cols(b)]))
        mixup_i()
        follow(0)
        owed_i_copy(0).start()
        produce(3, t_dot(a1[...], gin[...]))
        follow(1)
        for r in range(1, B):
            owed_i_copy(r).start()
        for b in range(2, 4):
            follow(b)
        norm_sums(dn1, u1, 0, 1)
        gv[2:3] = column_sum(dqkv1[:, cols(2)])
        gv[4:5] = column_sum(gin[...])
        gv[5:6] = column_sum(dqkv1[:, cols(0)])
        if fused:
            for b in range(5, 8):
                w[b] = jnp.zeros((D, D), bf16)
        else:
            for b in range(4, 8):
                G[b] = jnp.zeros((D, D), bf16)

    def feed_grads(first, last, left, right, start):
        def one(c, _):
            produce(first + c, t_dot(left[...], right[:, at(c, D)]))
            pl.when(first + c >= 2)(lambda: follow(first + c - 2))
            return 0

        lax.fori_loop(0, last - first, one, 0)

    def feed_sums():
        norm_sums(dn1, u1, 0, 1)
        for c in range(4):
            gv[2 + c : 3 + c] = column_sum(da[:, cols(c)])
        gv[6:7] = column_sum(gin[...])

    @pl.when(z == 1)
    def _():
        tables_ready()
        turned(0, 8)

        def forward(i):
            rows = at(i, CH)
            entered(i)
            h = hin[rows].astype(f32)
            n = norm_in(h, rows, u1, s1, n1, 0, 1)
            hidden = [dot(n, w[c]) + vec[2 + c] for c in range(4)]
            parts = [gelu_parts(a) for a in hidden]
            actives = [active.astype(bf16) for active, _ in parts]
            out = sum([dot(active, wt[4 + c]) for c, active in enumerate(actives)], h + vec[6])
            records[rows] = out.astype(bf16)
            forward_hop(i).start()
            for c in range(4):
                g[rows, cols(c)] = actives[c]
                gp[rows, cols(c)] = parts[c][1]

        each_chunk(forward)

        def backward(i):
            rows = at(i, CH)
            returned(i)
            e = gin[rows]
            dgs = [dot(e, w[4 + c]) for c in range(4)]
            dcs = [(dg * gp[rows, cols(c)]).astype(bf16) for c, dg in enumerate(dgs)]
            dn = sum([dot(dc, wt[c]) for c, dc in enumerate(dcs)])
            for c in range(4):
                da[rows, cols(c)] = dcs[c]
            dn1[rows] = dn
            gout[rows] = (e.astype(f32) + norm_out(dn, rows, u1, s1, 0)).astype(bf16)
            backward_hop(i).start()

        each_chunk(backward)
        feed_grads(0, 4, n1, da, 0)
        feed_grads(4, 8, gin, g, 4)
        follow(6)
        follow(7)
        feed_sums()

    @pl.when(z == 3)
    def _():
        tables_ready()
        turned(0, 4)
        own_cot.wait()

        def ahead(r):
            rows = at(r, T)
            e = cot[rows]
            for c in range(4):
                gp[rows, cols(c)] = dot(e, w[4 + c])

        each_row(ahead)

        def turn(i):
            rows = at(i, CH)
            entered(i)
            e = cot[rows]
            n = norm_in(hin[rows].astype(f32), rows, u1, s1, n1, 0, 1)
            hidden = [dot(n, w[c]) + vec[2 + c] for c in range(4)]
            parts = [gelu_parts(a) for a in hidden]
            dcs = [(gp[rows, cols(c)] * parts[c][1]).astype(bf16) for c in range(4)]
            dn = sum([dot(dc, wt[c]) for c, dc in enumerate(dcs)])
            for c in range(4):
                g[rows, cols(c)] = parts[c][0].astype(bf16)
                da[rows, cols(c)] = dcs[c]
            dn1[rows] = dn
            gout[rows] = (e.astype(f32) + norm_out(dn, rows, u1, s1, 0)).astype(bf16)
            backward_hop(i).start()

        each_chunk(turn)
        feed_grads(0, 4, n1, da, 0)

        def output(r):
            rows = at(r, T)
            out = hin[rows].astype(f32) + vec[6]
            for c in range(4):
                out += dot_t(g[rows, cols(c)], w[4 + c])
            records[rows] = out.astype(bf16)

        each_row(output)
        feed_grads(4, 8, cot, g, 4)
        follow(6)
        follow(7)
        feed_sums()

    @pl.when(z == 2)
    def _():
        tables_ready()

        def ahead(r):
            wide = at(r, V)
            for k in (0, 1, 3):
                gather_v(r, k).wait_recv()
            for b in range(2):
                kv2[wide, cols(b)] = dot(view[wide], w[1 + b]).astype(bf16)

        each_row(ahead)
        turned(3, 8)
        wt[0] = jnp.transpose(w[0])

        def forward(r):
            rows, wide = at(r, T), at(r, V)
            both(entered, r)
            h = hin[rows].astype(f32)
            n = norm_in(h, rows, u2, s2, n2, 0, 1)
            q2[rows] = dot(n, w[0]).astype(bf16) * SCALE
            keys, values = heads(kv2, wide), heads(kv2, wide, D)
            out, kept = attend(heads(q2, rows), keys, values, seg_q[r] == seg_v[r])
            put(a2, rows, out)
            put(p2, rows, kept)
            m = h + dot(a2[rows], w[3]) + vec[4]
            n = norm_in(m, rows, u1, s1, n1, 2, 3)
            q = (dot(n, w[4]) + vec[5]).astype(bf16)
            qkv1[rows, cols(0)] = q * SCALE
            qkv1[rows, cols(1)] = dot(n, w[5]).astype(bf16)
            qkv1[rows, cols(2)] = dot(n, w[6]).astype(bf16)
            self_attend(r, rows, qkv1, p1, a1)
            out = m + dot(a1[rows], w[7]) + vec[6]
            records[rows] = out.astype(bf16)
            forward_hops(r)

        each_row(forward)

        def backward(r):
            rows, wide = at(r, T), at(r, V)
            both(returned, r)
            e = gin[rows]
            do1[rows] = dot(e, wt[7]).astype(bf16)
            self_attend_back(r, rows, qkv1, p1, do1, dqkv1)
            dn = dot(dqkv1[rows], wide_t(4, 3))
            dn1[rows] = dn
            dmid = e.astype(f32) + norm_out(dn, rows, u1, s1, 2)
            dm[rows] = dmid
            do2[rows] = dot(dmid.astype(bf16), wt[3]).astype(bf16)
            ds = score_grads(heads(kv2, wide, D), held(p2, rows, V), heads(do2, rows))
            put(ds2, rows, ds)
            put(dq2, rows, query_grads(heads(kv2, wide), ds))
            dn = dot(dq2[rows], wt[0])
            dn2[rows] = dn
            gout[rows] = (dmid + norm_out(dn, rows, u2, s2, 0)).astype(bf16)
            backward_hops(r)

        each_row(backward)
        for b in range(3):
            produce(4 + b, t_dot(n1[...], dqkv1[:, cols(b)]))
        follow(4)
        produce(7, t_dot(a1[...], gin[...]))
        follow(5)

        def source_grad(r):
            rows, wide = at(r, T), at(r, V)
            dk, dv = key_grads(
                heads(q2, rows), held(p2, rows, V), heads(do2, rows), held(ds2, rows, V)
            )
            put(dkv2, wide, dk)
            put(dkv2, wide, dv, D)
            dw = dot_t(dkv2[wide, cols(0)], w[1]) + dot_t(dkv2[wide, cols(1)], w[2])
            R["dw"][wide] = dw.astype(bf16)

        each_row(source_grad)
        for b in range(2):
            produce(b, t_dot(n2[...], dq2[...]) if b == 0 else t_dot(view[...], dkv2[:, cols(0)]))
            follow(6 + b)
        produce(2, t_dot(view[...], dkv2[:, cols(1)]))
        follow(0)
        produce(3, t_dot(a2[...], dm[...].astype(bf16)))
        for b in range(1, 4):
            follow(b)
        norm_sums(dn1, u1, 2, 3)
        norm_sums(dn2, u2, 0, 1)
        each_row(scatter_v)
        gv[4:5] = column_sum(dm[...])
        gv[5:6] = column_sum(dqkv1[:, cols(0)])
        gv[6:7] = column_sum(gin[...])

    def mixup_v():
        for r in range(B):
            part_copy(r, 0).wait_recv()
        rows = [part_v[r] for r in range(B)]
        for t in range(B):
            owed_v[t] = owed(t, rows)

    def mixup_i_end():
        for r in range(B):
            owed_i_copy(r).wait()
        for r in range(B):
            rows = slice(r * T, (r + 1) * T)
            R["fin_i"][rows] = combined(r, gout[rows], R["arr_i"][rows])
        for r in range(B):
            for k in range(1, S):
                hand_i(r, k).start()
            in_grad[r] = R["fin_i"][r * T : r * T + TS]

    def mixup_v_end(k):
        for r in range(B):
            owed_v_copy(r).wait()
        for r in range(B):
            R["fin_v"][r] = combined(r, part_v[r], R["arr_v"][r])
        for r in range(B):
            hand_v(r, k).start()
            view_grad[r] = R["fin_v"][r, k * VS : (k + 1) * VS]

    def mixup_handed():
        for r in range(B):

            @pl.when(z != 0)
            def _():
                hand_i(r, 1).wait_recv()

            @pl.when((z == 1) | (z == 2))
            def _():
                hand_v(r, 0).wait_recv()

            @pl.when(z == 0)
            def _():
                for k in range(1, S):
                    hand_i(r, k).wait_send()

            for end, k in ((0, 0), (3, 1)):

                @pl.when(z == end)
                def _():
                    hand_v(r, k).wait_send()

    def sum_first(b):
        scatter_x(b).wait_recv()
        add(b, a_own, quarter, rx)
        scatter_xy(b).start()
        scatter_y(b).wait_recv()
        add(b, second_half(b)[0], quarter, ry)
        scatter_yx(b).start()

    def sum_second(b):
        scatter_xy(b).wait_recv()
        finish(b, a_end, ry2)
        spread_y(b).start()
        scatter_yx(b).wait_recv()
        finish(b, second_half(b)[2], rx2)
        spread_x(b).start()

        @pl.when((z == 3) & (b < B))
        def _():
            owed_v_copy(b).start()

    def pass_on(b):
        spread_y(b).wait_recv()
        spread_yx(b).start()
        spread_x(b).wait_recv()
        spread_xy(b).start()

        @pl.when((z == 0) & (b < B))
        def _():
            owed_v_copy(b).start()

    def pass_core(b):
        taken = (z == 0) & (b == TAKEN)
        spread_yx(b).wait_recv()

        @pl.when(jnp.logical_not(taken))
        def _():
            spread_core(b, 0).start()

        spread_xy(b).wait_recv()

        @pl.when(taken)
        def _():
            give_back().start()

        @pl.when(jnp.logical_not(taken))
        def _():
            spread_core(b, 1).start()

    def arrive(b):
        spread_core(b, 0).wait_recv()
        spread_core(b, 1).wait_recv()

    def sent(b):
        for copy in (scatter_x, scatter_y, scatter_xy, scatter_yx, spread_y, spread_x):
            copy(b).wait_send()
        for copy in (spread_yx, spread_xy):
            copy(b).wait_send()

    def core_sent(b):
        core_send(b).wait_send()
        spread_core(b, 0).wait_send()
        spread_core(b, 1).wait_send()

    def vector_round(k, device):
        return remote(gv, R["gv_in"].at[k], R["v_send"].at[k], R["v_recv"].at[k], device)

    def vector_sum(k, device):
        copy = vector_round(k, device)
        copy.wait()
        gv[...] += R["gv_in"][k]

    def loop(first, last, step):
        lax.fori_loop(first, last, lambda i, c: (step(i), c)[1], 0)

    def each_block(step):
        loop(0, blocks, lambda i: step(lax.rem(i + shift, wrap)))

    def each_back(step):
        loop(0, blocks, lambda i: step(lax.rem(i + shift_back, wrap)))

    if fused:
        vector_round(0, beside).start()
        vector_sum(0, beside)
        vector_round(1, x_next).start()

        @pl.when(z == 0)
        def _():
            take()

        each_block(sum_first)
        vector_sum(1, x_next)
        vector_round(2, far).start()

        @pl.when(z == 3)
        def _():
            mixup_v()

        each_back(sum_second)
        vector_sum(2, far)

        @pl.when(z == 0)
        def _():
            mixup_i_end()
            mixup_v()

        each_back(pass_on)

        @pl.when(z == 3)
        def _():
            mixup_v_end(1)

        most = blocks - 2
        loop(0, most, lambda i: pass_core(lax.rem(i + shift_back, wrap)))

        @pl.when(z == 0)
        def _():
            mixup_v_end(0)

        loop(most, blocks, lambda i: pass_core(lax.rem(i + shift_back, wrap)))


        @pl.when(z == 1)
        def _():
            give_back().wait_recv()
            spread_core(LENT, 0).start()
            spread_core(LENT, 1).start()

        loop(0, own_blocks, arrive)
        mixup_handed()
        each_block(sent)
        loop(0, own_blocks, core_sent)

        @pl.when(z == 1)
        def _():
            lend().wait_send()

        @pl.when(z == 0)
        def _():
            give_back().wait_send()
            w[TAKEN] = jnp.zeros((D, D), bf16)

    else:
        @pl.when(z == 0)
        def _():
            mixup_i_end()

        @pl.when((z == 0) | (z == 3))
        def _():
            mixup_v()
            for r in range(B):
                owed_v_copy(r).start()

        for end, k in ((0, 0), (3, 1)):
            pl.when(z == end)(partial(mixup_v_end, k))
        mixup_handed()
        for b in range(8):
            w[b] = G[b]

    for i in range(vec.shape[0]):
        R["gv_out"][i] = gv[i : i + 1]

    @pl.when(z == 2)
    def _():
        for r in range(B):
            for k in range(2):
                part_copy(r, k).wait_send()

    for r in range(B):

        @pl.when(z != 0)
        def _():
            gather_i(r, z).wait_send()

        @pl.when(z != 2)
        def _():
            gather_v(r, z).wait_send()

    for i in range(chunks):

        @pl.when(z != 0)
        def _():
            backward_hop(i).wait_send()

        @pl.when(z != S - 1)
        def _():
            forward_hop(i).wait_send()


def on_device(inputs, other_view, mats, vectors, mixing, partner, segments, cotangent):
    B, TS, D = inputs.shape
    VS = other_view.shape[1]
    T = segments.shape[1]
    S = lax.axis_size("section")
    V = VS * S
    H = mats.shape[3]
    pairs = D // PAIR
    vmem = pl.BlockSpec(memory_space=pltpu.VMEM)
    smem = pl.BlockSpec(memory_space=pltpu.SMEM)
    hbm = pl.BlockSpec(memory_space=pl.ANY)
    args = {
        "inputs": (inputs, hbm),
        "other_view": (other_view, hbm),
        "mats": (mats, hbm),
        "vec": (jnp.swapaxes(vectors, 0, 1), vmem),
        "mixing": (mixing, smem),
        "partner": (partner, smem),
        "segments": (segments, vmem),
        "cot": (cotangent.reshape(B * T, D), hbm),
    }
    outs = {
        "records": (B * T, D, bf16),
        "in_grad": (B, TS, D, bf16),
        "view_grad": (B, VS, D, bf16),
        "gv_out": (vectors.shape[1], 1, D, f32),
        "w": (8, D, D, bf16),
    }
    dma = pltpu.SemaphoreType.DMA

    def buf(*shape, dtype=bf16):
        return pltpu.VMEM(shape, dtype)

    scratch = {"G": buf(8, D, D), "core_in": buf(8, D // 2, D)}
    scratch |= {k: buf(8, D // 8, D) for k in ("rx", "ry")}
    scratch |= {k: buf(8, D // 16, D) for k in ("rx2", "ry2")}
    scratch |= {"gv": buf(8, D, dtype=f32), "gv_in": buf(3, 8, D, dtype=f32)}
    scratch |= {"seg_q": buf(B, T, 1, dtype=f32), "seg_v": buf(B, 1, V, dtype=f32)}
    for k in ("own", "far", "stage"):
        scratch |= {k + "_i": buf(B, TS, D), k + "_v": buf(B, VS, D)}
    for k in ("owed", "arr", "fin"):
        scratch |= {k + "_i": buf(B * T, D), k + "_v": buf(B, 2 * VS, D)}
    scratch["part_v"] = buf(B, 2 * VS, D)
    scratch |= {k: buf(B * V, D) for k in ("view", "dw")}
    for k in ("hin", "gin", "gout", "n1", "a1", "do1", "n2", "a2", "q2", "dq2", "do2"):
        scratch[k] = buf(B * T, D)
    scratch |= {k: buf(B * T, D, dtype=f32) for k in ("u1", "u2", "dn1", "dn2", "dm")}
    scratch |= {k: buf(B * T, 1, dtype=f32) for k in ("s1", "s2")}
    scratch |= {k: buf(B * T, 3 * D) for k in ("qkv1", "dqkv1")}
    scratch |= {k: buf(B * V, 2 * D) for k in ("kv2", "dkv2")}
    scratch["p1"] = buf(B * T, 2 * T * pairs, dtype=f32)
    W = max(H, 2 * V * pairs)
    scratch |= {"g": buf(B * T, H), "da": buf(B * T, W), "gp": buf(B * T, W, dtype=f32)}
    scratch |= {
        "w_sem": dma((8,)),
        "ex_sem": dma((4,)),
        "oi_send": dma((B,)),
        "oi_recv": dma((B,)),
        "ov_send": dma((B,)),
        "ov_recv": dma((B,)),
        "l_sem": dma((3,)),
        "gi_send": dma((B,)),
        "gi_recv": dma((B, S)),
        "gv_send": dma((B,)),
        "gv_recv": dma((B, S)),
        "f_send": dma((2 * B,)),
        "f_recv": dma((2 * B,)),
        "b_send": dma((2 * B,)),
        "b_recv": dma((2 * B,)),
        "sv_send": dma((B, 2)),
        "sv_recv": dma((B,)),
        "hi_send": dma((B, S)),
        "hi_recv": dma((B,)),
        "hv_send": dma((B, 2)),
        "hv_recv": dma((B,)),
        "lend_send": dma,
        "lend_recv": dma,
        "back_send": dma,
        "back_recv": dma,
        "r_send": dma((11, 8)),
        "r_recv": dma((11, 8)),
        "v_send": dma((3,)),
        "v_recv": dma((3,)),
    }
    names = list(args) + list(outs) + list(scratch)
    fused = lax.axis_size("dp") == 8
    *small, total = pl.pallas_call(
        partial(kernel, names, fused),
        out_shape=[pltpu.VMEM(s[:-1], s[-1]) for s in outs.values()],
        in_specs=[spec for _, spec in args.values()],
        out_specs=[vmem] * len(outs),
        scratch_shapes=list(scratch.values()),
        compiler_params=pltpu.CompilerParams(
            collective_id=0, has_side_effects=True, vmem_limit_bytes=50 << 20
        ),
        name="relay",
    )(*[value for value, _ in args.values()])
    if not fused:
        total, small[-1] = lax.psum((total, small[-1]), "dp")
    piece = D // 4
    wide, records, in_grad, view_grad, vector_grad = pl.pallas_call(
        widen,
        out_shape=[jax.ShapeDtypeStruct(mats.shape, f32)]
        + [jax.ShapeDtypeStruct(x.shape, x.dtype) for x in small],
        in_specs=[vmem] * 5,
        out_specs=[hbm] * 5,
        scratch_shapes=[pltpu.VMEM((4, piece, H), f32), dma((4,)), dma((4,))],
        compiler_params=pltpu.CompilerParams(vmem_limit_bytes=16 << 20),
        name="widen",
    )(total, *small)
    records = records.reshape(1, B, T, D)
    return records, in_grad, view_grad, wide, jnp.swapaxes(vector_grad, 0, 1)


def widen(total, *refs):
    small, wide, outs, slots, sems, small_sems = refs[:4], refs[4], refs[5:9], *refs[9:]
    held, piece, H = slots.shape
    D = total.shape[1]
    copies = [
        pltpu.make_async_copy(a, b, small_sems.at[i]) for i, (a, b) in enumerate(zip(small, outs))
    ]
    for copy in copies:
        copy.start()

    def write(i):
        t, rows = i * piece // D, pl.ds(i * piece % D, piece)
        return pltpu.make_async_copy(slots.at[i % held], wide.at[0, t, rows], sems.at[i % held])

    steps = 2 * D // piece
    for i in range(steps):
        if i >= held:
            write(i - held).wait()
        t, start = i * piece // D, i * piece % D
        for c in range(H // D):
            values = total[t * (H // D) + c, start : start + piece].astype(f32)
            slots[i % held, :, c * D : (c + 1) * D] = values
        write(i).start()
    for i in range(steps - held, steps):
        write(i).wait()
    for copy in copies:
        copy.wait()


def solution(mesh):
    in_specs = (
        P("dp", "section", None),
        P("dp", "section", None),
        P("section", None, None, None),
        P("section", None, None),
        P("dp"),
        P("dp"),
        P("dp", None),
        P("dp", None, None),
    )
    out_specs = (
        P("section", "dp", None, None),
        P("dp", "section", None),
        P("dp", "section", None),
        P("section", None, None, None),
        P("section", None, None),
    )
    return jax.shard_map(
        on_device, mesh=mesh, in_specs=in_specs, out_specs=out_specs, check_vma=False
    )
```

```python
from functools import partial

import jax
import jax.numpy as jnp
from jax import lax
from jax.experimental import pallas as pl
from jax.experimental.pallas import tpu as pltpu
from jax.sharding import PartitionSpec as P

HEAD = 64
PAIR = 2 * HEAD
MESH = pl.DeviceIdType.MESH
bf16 = jnp.bfloat16
f32 = jnp.float32


def dot(a, b):
    return lax.dot_general(a, b, (((1,), (0,)), ((), ())), preferred_element_type=f32)


def dot_t(a, b):
    return lax.dot_general(a, b, (((1,), (1,)), ((), ())), preferred_element_type=f32)


def t_dot(a, b):
    return lax.dot_general(a, b, (((0,), (0,)), ((), ())), preferred_element_type=f32)


def row_mean(x):
    return jnp.sum(x, axis=-1, keepdims=True) * (1.0 / x.shape[-1])


def normalize(h):
    center = h - row_mean(h)
    scale = lax.rsqrt(row_mean(center * center) + 1e-06)
    return center * scale, scale


def normalize_back(grad, unit, scale, gain):
    inner = grad * gain
    return scale * (inner - row_mean(inner) - unit * row_mean(inner * unit))


def gelu_parts(a):
    cdf = 0.5 * (1.0 + lax.erf(a * (0.5**0.5)))
    pdf = jnp.exp(a * a * (-0.5)) * 0.3989422804014327
    return a * cdf, cdf + a * pdf


def halves(x):
    low = lax.broadcasted_iota(jnp.int32, x.shape, 1) < HEAD
    zero = jnp.zeros_like(x)
    return jnp.concatenate([jnp.where(low, x, zero), jnp.where(low, zero, x)], axis=0)


def attend(queries, keys, values, allowed):
    n = keys[0].shape[0]
    scores = [dot_t(q, halves(k)) for q, k in zip(queries, keys)]
    split = [[jnp.where(allowed, x[:, h : h + n], -1000000000.0) for h in (0, n)] for x in scores]
    peaks = [[jnp.max(x, axis=-1, keepdims=True) for x in pair] for pair in split]
    raised = [[jnp.exp(x - m) for x, m in zip(*both)] for both in zip(split, peaks)]
    shares = [[1.0 / jnp.sum(x, axis=-1, keepdims=True) for x in pair] for pair in raised]
    weights = [
        jnp.concatenate([x * m for x, m in zip(*both)], axis=1) for both in zip(raised, shares)
    ]
    outs = [dot(x.astype(bf16), halves(v)) for x, v in zip(weights, values)]
    return outs, weights


def score_grads(values, weights, grads):
    n = values[0].shape[0]
    grad_weights = [dot_t(x, halves(v)) for x, v in zip(grads, values)]
    products = [x * y for x, y in zip(weights, grad_weights)]
    totals = [
        [jnp.sum(x[:, h : h + n], axis=-1, keepdims=True) for h in (0, n)] for x in products
    ]
    return [
        jnp.concatenate(
            [
                (x[:, h : h + n] - y[:, h : h + n] * total).astype(bf16)
                for h, total in zip((0, n), pair)
            ],
            axis=1,
        )
        for x, y, pair in zip(products, weights, totals)
    ]


def query_grads(keys, grad_scores):
    return [dot(x, halves(k)) * (HEAD**-0.5) for x, k in zip(grad_scores, keys)]


def stacked(x):
    n = x.shape[1] // 2
    return jnp.concatenate([x[:, :n], x[:, n:]], axis=0)


def key_grads(queries, weights, grads, grad_scores):
    grad_k = [t_dot(stacked(x), halves(q)) for x, q in zip(grad_scores, queries)]
    grad_v = [t_dot(stacked(x.astype(bf16)), halves(y)) for x, y in zip(weights, grads)]
    return grad_k, grad_v


def column_sum(x):
    return jnp.sum(x.astype(f32), axis=0, keepdims=True)


def kernel(names, fused, *refs):
    R = dict(zip(names, refs))
    inputs, other_view, mats, vec = (R[k] for k in ("inputs", "other_view", "mats", "vec"))
    mixing, partner, cot = R["mixing"], R["partner"], R["gin"]
    segments, seg_q, seg_v = R["segments"], R["seg_q"], R["seg_v"]
    records, in_grad, view_grad = R["records"], R["in_grad"], R["view_grad"]
    G, gv, w = R["G"], R["gv"], R["w"]
    wt = G
    hin, gin, gout = R["hin"], R["gin"], R["gout"]
    B, TS, D = inputs.shape
    VS = other_view.shape[1]
    T = segments.shape[1]
    V = seg_v.shape[2]
    S = lax.axis_size("section")
    n_dp = lax.axis_size("dp")
    z = lax.axis_index("section")
    d = lax.axis_index("dp")
    far = {"dp": lax.rem(d + n_dp // 2, n_dp)}
    pairs = D // PAIR
    CH = T // 2
    chunks = B * 2
    core, x_bit, y_bit = lax.rem(d, 2), lax.rem(d // 2, 2), d // 4
    beside = {"dp": d + 1 - 2 * core}
    x_next = {"dp": d + 2 - 4 * x_bit}

    def remote(src, dst, send, recv, device):
        return pltpu.make_async_remote_copy(
            src_ref=src,
            dst_ref=dst,
            send_sem=send,
            recv_sem=recv,
            device_id=device,
            device_id_type=MESH,
        )

    def block_columns(b):
        return pl.ds(b * D, D)

    def table(b):
        return pltpu.make_async_copy(
            mats.at[0, b // 4, :, block_columns(b % 4)], w.at[b], R["w_sem"].at[b]
        )

    def local(src, dst, k):
        return pltpu.make_async_copy(src, dst, R["l_sem"].at[k])

    def at(i, length):
        return pl.ds(pl.multiple_of(i * length, length), length)

    own_i = local(inputs, R["own_i"], 0)
    own_v = local(other_view, R["own_v"], 1)
    own_cot = local(R["cot"], gin, 2)
    barrier = pltpu.get_barrier_semaphore()
    others = [far] + [{"section": lax.rem(z + o, S)} for o in range(1, S)]
    if fused:
        others += [beside, x_next]
    for other in others:
        pl.semaphore_signal(barrier, inc=1, device_id=other, device_id_type=MESH)
    own_i.start()
    own_v.start()

    gv[...] = jnp.zeros_like(gv)
    pick = [[(partner[r] == j).astype(f32) for j in range(B)] for r in range(B)]
    mix = [mixing[r] for r in range(B)]
    pl.semaphore_wait(barrier, len(others))

    ex = R["ex_sem"]
    far_i = remote(inputs, R["far_i"], ex.at[0], ex.at[1], far)
    far_v = remote(other_view, R["far_v"], ex.at[2], ex.at[3], far)
    far_i.start()

    @pl.when(z == 0)
    def _():
        far_v.start()

    across = lax.broadcasted_iota(jnp.int32, (T, T), 1)
    down = lax.broadcasted_iota(jnp.int32, (T, T), 0)
    wide_across = lax.broadcasted_iota(jnp.int32, (T, V), 1)
    wide_down = lax.broadcasted_iota(jnp.int32, (T, V), 0)
    spread = (wide_across // (V // T) == wide_down).astype(f32)
    for r in range(B):
        ids = segments[r : r + 1].astype(f32)
        column = jnp.sum(jnp.where(across == down, ids, 0.0), axis=1, keepdims=True)
        seg_q[r] = column
        seg_v[r] = jnp.sum(spread * column, axis=0, keepdims=True)

    def blend(own, other, r):
        chosen = sum(pick[r][j] * other[j].astype(f32) for j in range(B))
        return (mix[r] * own[r].astype(f32) + (1.0 - mix[r]) * chosen).astype(bf16)

    def gather_i(r, source):
        return remote(
            R["stage_i"].at[r],
            hin.at[pl.ds(pl.multiple_of(r * T + source * TS, TS), TS)],
            R["gi_send"].at[r],
            R["gi_recv"].at[r, source],
            {"section": 0},
        )

    def gather_v(r, source):
        return remote(
            R["stage_v"].at[r],
            R["view"].at[pl.ds(pl.multiple_of(r * V + source * VS, VS), VS)],
            R["gv_send"].at[r],
            R["gv_recv"].at[r, source],
            {"section": 2},
        )

    own_i.wait()
    far_i.wait_recv()
    for r in range(B):
        mixed = blend(R["own_i"], R["far_i"], r)

        @pl.when(z == 0)
        def _():
            hin[r * T : r * T + TS] = mixed

        @pl.when(z != 0)
        def _():
            R["stage_i"][r] = mixed
            gather_i(r, z).start()

    for b in range(8):
        table(b).start()

    @pl.when(z == S - 1)
    def _():
        own_cot.start()

    @pl.when(z != 0)
    def _():
        far_v.start()

    own_v.wait()
    far_v.wait_recv()
    for r in range(B):
        mixed_view = blend(R["own_v"], R["far_v"], r)

        @pl.when(z == 2)
        def _():
            R["view"][r * V + 2 * VS : r * V + 3 * VS] = mixed_view

        @pl.when(z != 2)
        def _():
            R["stage_v"][r] = mixed_view
            gather_v(r, z).start()

    far_i.wait_send()
    far_v.wait_send()

    def forward_hop(i):
        part = at(i, CH)
        return remote(
            records.at[part],
            hin.at[part],
            R["f_send"].at[i],
            R["f_recv"].at[i],
            {"section": z + 1},
        )

    def backward_hop(i):
        part = at(i, CH)
        return remote(
            gout.at[part], gin.at[part], R["b_send"].at[i], R["b_recv"].at[i], {"section": z - 1}
        )

    def entered(i):
        part = hin.at[at(i, CH)]
        remote(
            part, part, R["f_send"].at[i], R["f_recv"].at[i], {"section": z - 1}
        ).wait_recv()

    def returned(i):
        part = gin.at[at(i, CH)]
        remote(
            part, part, R["b_send"].at[i], R["b_recv"].at[i], {"section": z + 1}
        ).wait_recv()

    def both(step, r):
        step(2 * r)
        step(2 * r + 1)

    def forward_hops(r):
        forward_hop(2 * r).start()
        forward_hop(2 * r + 1).start()

    def backward_hops(r):
        backward_hop(2 * r).start()
        backward_hop(2 * r + 1).start()

    def each_row(step):
        lax.fori_loop(0, B, lambda r, c: (step(r), c)[1], 0)

    def each_chunk(step):
        lax.fori_loop(0, chunks, lambda i, c: (step(i), c)[1], 0)

    def cols(b, width=D):
        return slice(b * width, (b + 1) * width)

    def tables_ready():
        for b in range(8):
            table(b).wait()

    def turned(first, last):
        def one(b, c):
            wt[b] = jnp.transpose(w[b])
            return c

        lax.fori_loop(first, last, one, 0)

    def norm_in(h, rows, unit, scale, normed, gain, shift):
        unit_value, scale_value = normalize(h)
        unit[rows] = unit_value
        scale[rows] = scale_value
        value = (unit_value * vec[gain] + vec[shift]).astype(bf16)
        normed[rows] = value
        return value

    def norm_out(grad, rows, unit, scale, gain):
        return normalize_back(grad, unit[rows], scale[rows], vec[gain])

    def norm_sums(grad, unit, gain, shift):
        gv[gain : gain + 1] = column_sum(grad[...] * unit[...])
        gv[shift : shift + 1] = column_sum(grad[...])

    def heads(ref, rows, start=0):
        return [ref[rows, start + p * PAIR : start + (p + 1) * PAIR] for p in range(pairs)]

    def put(ref, rows, values, start=0):
        width = values[0].shape[1]
        for p, value in enumerate(values):
            ref[rows, start + p * width : start + (p + 1) * width] = value.astype(ref.dtype)

    def self_attend(r, rows, qkv, weights, attended):
        allowed = seg_q[r] == segments[pl.ds(r, 1)].astype(f32)
        q, k, v = (heads(qkv, rows, start) for start in (0, D, 2 * D))
        out, kept = attend(q, k, v, allowed)
        put(attended, rows, out)
        put(weights, rows, kept)

    def held(weights, rows, n):
        return [weights[rows, cols(p, 2 * n)] for p in range(pairs)]

    def self_attend_back(r, rows, qkv, weights, grad, dqkv):
        q, k, v = (heads(qkv, rows, start) for start in (0, D, 2 * D))
        kept, do = held(weights, rows, T), heads(grad, rows)
        ds = score_grads(v, kept, do)
        dk, dv = key_grads(q, kept, do, ds)
        put(dqkv, rows, query_grads(k, ds))
        put(dqkv, rows, dk, D)
        put(dqkv, rows, dv, 2 * D)

    half = D // 2

    def sems(kind, b):
        return R["r_send"].at[kind, b], R["r_recv"].at[kind, b]

    def core_send(b):
        rows = pl.ds(pl.multiple_of((1 - core) * half, half), half)
        return remote(G.at[b, rows], R["core_in"].at[b], *sems(0, b), beside)

    def produce(b, value):
        G[b] = value.astype(bf16)
        if fused:
            core_send(b).start()

    def follow(b):
        if fused:
            sum_core(b)

    part_v = R["part_v"]

    VH = 2 * VS

    def part_copy(r, k):
        return remote(
            R["dw"].at[pl.ds(pl.multiple_of(r * V + k * VH, VH), VH)],
            part_v.at[r],
            R["sv_send"].at[r, k],
            R["sv_recv"].at[r],
            {"section": 3 * k},
        )

    def scatter_v(r):
        for k in range(2):
            part_copy(r, k).start()

    def hand_i(r, k):
        return remote(
            R["fin_i"].at[pl.ds(r * T + k * TS, TS)],
            in_grad.at[r],
            R["hi_send"].at[r, k],
            R["hi_recv"].at[r],
            {"section": k},
        )

    def hand_v(r, k):
        return remote(
            R["fin_v"].at[r, pl.ds((1 - k) * VS, VS)],
            view_grad.at[r],
            R["hv_send"].at[r, k],
            R["hv_recv"].at[r],
            {"section": 1 + k},
        )

    owed_i, owed_v = R["owed_i"], R["owed_v"]

    def owed_i_copy(r):
        rows = pl.ds(r * T, T)
        return remote(
            owed_i.at[rows], R["arr_i"].at[rows], R["oi_send"].at[r], R["oi_recv"].at[r], far
        )

    def owed_v_copy(r):
        return remote(
            owed_v.at[r], R["arr_v"].at[r], R["ov_send"].at[r], R["ov_recv"].at[r], far
        )

    def owed(t, rows):
        return sum(
            pick[r][t] * (1.0 - mix[r]) * rows[r].astype(f32) for r in range(B)
        ).astype(bf16)

    def combined(r, own, arrived):
        return (mix[r] * own.astype(f32) + arrived.astype(f32)).astype(bf16)

    def mixup_i():
        rows = [gout[r * T : (r + 1) * T] for r in range(B)]
        for t in range(B):
            owed_i[t * T : (t + 1) * T] = owed(t, rows)

    rx, ry, rx2, ry2, core_in = (R[k] for k in ("rx", "ry", "rx2", "ry2", "core_in"))
    quarter, eighth = half // 4, half // 8
    own = core * half
    a0, b0 = own, own + half // 2
    a_own, a_far = a0 + x_bit * quarter, a0 + (1 - x_bit) * quarter
    a_end, a_out = a_own + y_bit * eighth, a_own + (1 - y_bit) * eighth

    def turned_round(b):
        return jnp.where(b < jnp.where(z == 0, 2, jnp.where(z == 3, 1, 0)), 1, 0)

    def second_half(b):
        flip = turned_round(b)
        first = y_bit + flip * (x_bit - y_bit)
        then = x_bit + flip * (y_bit - x_bit)
        mine, other = b0 + first * quarter, b0 + (1 - first) * quarter
        return mine, other, mine + then * eighth, mine + (1 - then) * eighth

    def first_way(b):
        flip = turned_round(b)
        return {"dp": (1 - flip) * far["dp"] + flip * x_next["dp"]}

    def second_way(b):
        flip = turned_round(b)
        return {"dp": flip * far["dp"] + (1 - flip) * x_next["dp"]}
    LENT, TAKEN = 0, 4
    own_blocks = jnp.where(z == 0, 4, 8)
    blocks = jnp.where(z == 0, 5, jnp.where(z == 1, 7, 8))
    wrap = jnp.where(z == 0, 5, 8)
    shift = jnp.where(z == 2, 4, jnp.where(z == 1, 1, 0))
    shift_back = jnp.where(z == 0, TAKEN, shift)

    def lend():
        rows = part(own, half)
        return remote(
            G.at[LENT, rows], G.at[TAKEN, rows], R["lend_send"], R["lend_recv"], {"section": 0}
        )

    def give_back():
        rows = part(own, half)
        return remote(
            w.at[TAKEN, rows], w.at[LENT, rows], R["back_send"], R["back_recv"], {"section": 1}
        )

    def part(start, length):
        return pl.ds(pl.multiple_of(start, eighth), length)

    def final(b, start, length):
        return w.at[b, part(start, length)]

    def scatter_x(b):
        return remote(G.at[b, part(a_far, quarter)], rx.at[b], *sems(1, b), x_next)

    def scatter_y(b):
        rows = part(second_half(b)[1], quarter)
        return remote(G.at[b, rows], ry.at[b], *sems(2, b), first_way(b))

    def scatter_xy(b):
        return remote(G.at[b, part(a_out, eighth)], ry2.at[b], *sems(3, b), far)

    def scatter_yx(b):
        rows = part(second_half(b)[3], eighth)
        return remote(G.at[b, rows], rx2.at[b], *sems(4, b), second_way(b))

    def spread_y(b):
        return remote(final(b, a_end, eighth), final(b, a_end, eighth), *sems(5, b), far)

    def spread_x(b):
        rows = final(b, second_half(b)[2], eighth)
        return remote(rows, rows, *sems(6, b), second_way(b))

    def spread_yx(b):
        return remote(final(b, a_own, quarter), final(b, a_own, quarter), *sems(7, b), x_next)

    def spread_xy(b):
        rows = final(b, second_half(b)[0], quarter)
        return remote(rows, rows, *sems(8, b), first_way(b))

    def spread_core(b, k):
        rows = final(b, own + k * (half // 2), half // 2)
        return remote(rows, rows, *sems(9 + k, b), beside)

    def add(b, start, length, arrived):
        rows = part(start, length)
        G[b, rows] = (G[b, rows].astype(f32) + arrived[b].astype(f32)).astype(bf16)

    def finish(b, start, arrived):
        rows = part(start, eighth)
        total = (G[b, rows].astype(f32) + arrived[b].astype(f32)).astype(bf16)
        w[b, rows] = total

    def sum_core(b):
        core_send(b).wait_recv()
        add(b, own, half, core_in)
        lent = (z == 1) & (b == LENT)

        @pl.when(lent)
        def _():
            lend().start()

        @pl.when(jnp.logical_not(lent))
        def _():
            scatter_x(b).start()
            scatter_y(b).start()

    def take():
        lend().wait_recv()
        scatter_x(TAKEN).start()
        scatter_y(TAKEN).start()

    n1, u1, s1, p1, a1 = R["n1"], R["u1"], R["s1"], R["p1"], R["a1"]
    qkv1, dqkv1, do1, dn1 = R["qkv1"], R["dqkv1"], R["do1"], R["dn1"]
    n2, u2, s2, a2 = R["n2"], R["u2"], R["s2"], R["a2"]
    q2, dq2, kv2, dkv2, do2, dn2 = (R[k] for k in ("q2", "dq2", "kv2", "dkv2", "do2", "dn2"))
    view, dm = R["view"], R["dm"]
    g, gp, da = R["g"], R["gp"], R["da"]
    p2, ds2 = gp, da
    SCALE = HEAD**-0.5

    def wide_t(first, count):
        return wt[first : first + count].reshape(count * D, D)

    @pl.when(z == 0)
    def _():
        tables_ready()

        def forward(r):
            rows = at(r, T)
            for k in range(1, S):
                gather_i(r, k).wait_recv()
            h = hin[rows].astype(f32)
            n = norm_in(h, rows, u1, s1, n1, 0, 1)
            q = (dot(n, w[0]) + vec[5]).astype(bf16)
            qkv1[rows, cols(0)] = q * SCALE
            qkv1[rows, cols(1)] = dot(n, w[1]).astype(bf16)
            qkv1[rows, cols(2)] = (dot(n, w[2]) + vec[2]).astype(bf16)
            self_attend(r, rows, qkv1, p1, a1)
            out = h + dot(a1[rows], w[3]) + vec[4]
            records[rows] = out.astype(bf16)
            forward_hops(r)

        each_row(forward)
        turned(0, 4)

        def backward(r):
            rows = at(r, T)
            both(returned, r)
            e = gin[rows]
            do1[rows] = dot(e, wt[3]).astype(bf16)
            self_attend_back(r, rows, qkv1, p1, do1, dqkv1)
            dn = dot(dqkv1[rows], wide_t(0, 3))
            dn1[rows] = dn
            gout[rows] = (e.astype(f32) + norm_out(dn, rows, u1, s1, 0)).astype(bf16)

        each_row(backward)
        for b in range(3):
            produce(b, t_dot(n1[...], dqkv1[:, cols(b)]))
        mixup_i()
        follow(0)
        owed_i_copy(0).start()
        produce(3, t_dot(a1[...], gin[...]))
        follow(1)
        for r in range(1, B):
            owed_i_copy(r).start()
        for b in range(2, 4):
            follow(b)
        norm_sums(dn1, u1, 0, 1)
        gv[2:3] = column_sum(dqkv1[:, cols(2)])
        gv[4:5] = column_sum(gin[...])
        gv[5:6] = column_sum(dqkv1[:, cols(0)])
        if fused:
            for b in range(5, 8):
                w[b] = jnp.zeros((D, D), bf16)
        else:
            for b in range(4, 8):
                G[b] = jnp.zeros((D, D), bf16)

    def feed_grads(first, last, left, right, start):
        def one(c, _):
            produce(first + c, t_dot(left[...], right[:, at(c, D)]))
            pl.when(first + c >= 2)(lambda: follow(first + c - 2))
            return 0

        lax.fori_loop(0, last - first, one, 0)

    def feed_sums():
        norm_sums(dn1, u1, 0, 1)
        for c in range(4):
            gv[2 + c : 3 + c] = column_sum(da[:, cols(c)])
        gv[6:7] = column_sum(gin[...])

    @pl.when(z == 1)
    def _():
        tables_ready()
        turned(0, 8)

        def forward(i):
            rows = at(i, CH)
            entered(i)
            h = hin[rows].astype(f32)
            n = norm_in(h, rows, u1, s1, n1, 0, 1)
            hidden = [dot(n, w[c]) + vec[2 + c] for c in range(4)]
            parts = [gelu_parts(a) for a in hidden]
            actives = [active.astype(bf16) for active, _ in parts]
            out = sum([dot(active, wt[4 + c]) for c, active in enumerate(actives)], h + vec[6])
            records[rows] = out.astype(bf16)
            forward_hop(i).start()
            for c in range(4):
                g[rows, cols(c)] = actives[c]
                gp[rows, cols(c)] = parts[c][1]

        each_chunk(forward)

        def backward(i):
            rows = at(i, CH)
            returned(i)
            e = gin[rows]
            dgs = [dot(e, w[4 + c]) for c in range(4)]
            dcs = [(dg * gp[rows, cols(c)]).astype(bf16) for c, dg in enumerate(dgs)]
            dn = sum([dot(dc, wt[c]) for c, dc in enumerate(dcs)])
            for c in range(4):
                da[rows, cols(c)] = dcs[c]
            dn1[rows] = dn
            gout[rows] = (e.astype(f32) + norm_out(dn, rows, u1, s1, 0)).astype(bf16)
            backward_hop(i).start()

        each_chunk(backward)
        feed_grads(0, 4, n1, da, 0)
        feed_grads(4, 8, gin, g, 4)
        follow(6)
        follow(7)
        feed_sums()

    @pl.when(z == 3)
    def _():
        tables_ready()
        turned(0, 4)
        own_cot.wait()

        def ahead(r):
            rows = at(r, T)
            e = cot[rows]
            for c in range(4):
                gp[rows, cols(c)] = dot(e, w[4 + c])

        each_row(ahead)

        def turn(i):
            rows = at(i, CH)
            entered(i)
            e = cot[rows]
            n = norm_in(hin[rows].astype(f32), rows, u1, s1, n1, 0, 1)
            hidden = [dot(n, w[c]) + vec[2 + c] for c in range(4)]
            parts = [gelu_parts(a) for a in hidden]
            dcs = [(gp[rows, cols(c)] * parts[c][1]).astype(bf16) for c in range(4)]
            dn = sum([dot(dc, wt[c]) for c, dc in enumerate(dcs)])
            for c in range(4):
                g[rows, cols(c)] = parts[c][0].astype(bf16)
                da[rows, cols(c)] = dcs[c]
            dn1[rows] = dn
            gout[rows] = (e.astype(f32) + norm_out(dn, rows, u1, s1, 0)).astype(bf16)
            backward_hop(i).start()

        each_chunk(turn)
        feed_grads(0, 4, n1, da, 0)

        def output(r):
            rows = at(r, T)
            out = hin[rows].astype(f32) + vec[6]
            for c in range(4):
                out += dot_t(g[rows, cols(c)], w[4 + c])
            records[rows] = out.astype(bf16)

        each_row(output)
        feed_grads(4, 8, cot, g, 4)
        follow(6)
        follow(7)
        feed_sums()

    @pl.when(z == 2)
    def _():
        tables_ready()

        def ahead(r):
            wide = at(r, V)
            for k in (0, 1, 3):
                gather_v(r, k).wait_recv()
            for b in range(2):
                kv2[wide, cols(b)] = dot(view[wide], w[1 + b]).astype(bf16)

        each_row(ahead)
        turned(3, 8)
        wt[0] = jnp.transpose(w[0])

        def forward(r):
            rows, wide = at(r, T), at(r, V)
            both(entered, r)
            h = hin[rows].astype(f32)
            n = norm_in(h, rows, u2, s2, n2, 0, 1)
            q2[rows] = dot(n, w[0]).astype(bf16) * SCALE
            keys, values = heads(kv2, wide), heads(kv2, wide, D)
            out, kept = attend(heads(q2, rows), keys, values, seg_q[r] == seg_v[r])
            put(a2, rows, out)
            put(p2, rows, kept)
            m = h + dot(a2[rows], w[3]) + vec[4]
            n = norm_in(m, rows, u1, s1, n1, 2, 3)
            q = (dot(n, w[4]) + vec[5]).astype(bf16)
            qkv1[rows, cols(0)] = q * SCALE
            qkv1[rows, cols(1)] = dot(n, w[5]).astype(bf16)
            qkv1[rows, cols(2)] = dot(n, w[6]).astype(bf16)
            self_attend(r, rows, qkv1, p1, a1)
            out = m + dot(a1[rows], w[7]) + vec[6]
            records[rows] = out.astype(bf16)
            forward_hops(r)

        each_row(forward)

        def backward(r):
            rows, wide = at(r, T), at(r, V)
            both(returned, r)
            e = gin[rows]
            do1[rows] = dot(e, wt[7]).astype(bf16)
            self_attend_back(r, rows, qkv1, p1, do1, dqkv1)
            dn = dot(dqkv1[rows], wide_t(4, 3))
            dn1[rows] = dn
            dmid = e.astype(f32) + norm_out(dn, rows, u1, s1, 2)
            dm[rows] = dmid
            do2[rows] = dot(dmid.astype(bf16), wt[3]).astype(bf16)
            ds = score_grads(heads(kv2, wide, D), held(p2, rows, V), heads(do2, rows))
            put(ds2, rows, ds)
            put(dq2, rows, query_grads(heads(kv2, wide), ds))
            dn = dot(dq2[rows], wt[0])
            dn2[rows] = dn
            gout[rows] = (dmid + norm_out(dn, rows, u2, s2, 0)).astype(bf16)
            backward_hops(r)

        each_row(backward)
        for b in range(3):
            produce(4 + b, t_dot(n1[...], dqkv1[:, cols(b)]))
        follow(4)
        produce(7, t_dot(a1[...], gin[...]))
        follow(5)

        def source_grad(r):
            rows, wide = at(r, T), at(r, V)
            dk, dv = key_grads(
                heads(q2, rows), held(p2, rows, V), heads(do2, rows), held(ds2, rows, V)
            )
            put(dkv2, wide, dk)
            put(dkv2, wide, dv, D)
            dw = dot_t(dkv2[wide, cols(0)], w[1]) + dot_t(dkv2[wide, cols(1)], w[2])
            R["dw"][wide] = dw.astype(bf16)

        each_row(source_grad)
        for b in range(2):
            produce(b, t_dot(n2[...], dq2[...]) if b == 0 else t_dot(view[...], dkv2[:, cols(0)]))
            follow(6 + b)
        produce(2, t_dot(view[...], dkv2[:, cols(1)]))
        follow(0)
        produce(3, t_dot(a2[...], dm[...].astype(bf16)))
        for b in range(1, 4):
            follow(b)
        norm_sums(dn1, u1, 2, 3)
        norm_sums(dn2, u2, 0, 1)
        each_row(scatter_v)
        gv[4:5] = column_sum(dm[...])
        gv[5:6] = column_sum(dqkv1[:, cols(0)])
        gv[6:7] = column_sum(gin[...])

    def mixup_v():
        for r in range(B):
            part_copy(r, 0).wait_recv()
        rows = [part_v[r] for r in range(B)]
        for t in range(B):
            owed_v[t] = owed(t, rows)

    def mixup_i_end():
        for r in range(B):
            owed_i_copy(r).wait()
        for r in range(B):
            rows = slice(r * T, (r + 1) * T)
            R["fin_i"][rows] = combined(r, gout[rows], R["arr_i"][rows])
        for r in range(B):
            for k in range(1, S):
                hand_i(r, k).start()
            in_grad[r] = R["fin_i"][r * T : r * T + TS]

    def mixup_v_end(k):
        for r in range(B):
            owed_v_copy(r).wait()
        for r in range(B):
            R["fin_v"][r] = combined(r, part_v[r], R["arr_v"][r])
        for r in range(B):
            hand_v(r, k).start()
            view_grad[r] = R["fin_v"][r, k * VS : (k + 1) * VS]

    def mixup_handed():
        for r in range(B):

            @pl.when(z != 0)
            def _():
                hand_i(r, 1).wait_recv()

            @pl.when((z == 1) | (z == 2))
            def _():
                hand_v(r, 0).wait_recv()

            @pl.when(z == 0)
            def _():
                for k in range(1, S):
                    hand_i(r, k).wait_send()

            for end, k in ((0, 0), (3, 1)):

                @pl.when(z == end)
                def _():
                    hand_v(r, k).wait_send()

    def sum_first(b):
        scatter_x(b).wait_recv()
        add(b, a_own, quarter, rx)
        scatter_xy(b).start()
        scatter_y(b).wait_recv()
        add(b, second_half(b)[0], quarter, ry)
        scatter_yx(b).start()

    def sum_second(b):
        scatter_xy(b).wait_recv()
        finish(b, a_end, ry2)
        spread_y(b).start()
        scatter_yx(b).wait_recv()
        finish(b, second_half(b)[2], rx2)
        spread_x(b).start()

        @pl.when((z == 3) & (b < B))
        def _():
            owed_v_copy(b).start()

    def pass_on(b):
        spread_y(b).wait_recv()
        spread_yx(b).start()
        spread_x(b).wait_recv()
        spread_xy(b).start()

        @pl.when((z == 0) & (b < B))
        def _():
            owed_v_copy(b).start()

    def pass_core(b):
        taken = (z == 0) & (b == TAKEN)
        spread_yx(b).wait_recv()

        @pl.when(jnp.logical_not(taken))
        def _():
            spread_core(b, 0).start()

        spread_xy(b).wait_recv()

        @pl.when(taken)
        def _():
            give_back().start()

        @pl.when(jnp.logical_not(taken))
        def _():
            spread_core(b, 1).start()

    def arrive(b):
        spread_core(b, 0).wait_recv()
        spread_core(b, 1).wait_recv()

    def sent_early(b):
        for copy in (scatter_x, scatter_y, scatter_xy, scatter_yx, spread_y, spread_x):
            copy(b).wait_send()

    def sent(b):
        spread_yx(b).wait_send()
        spread_xy(b).wait_send()

    def core_sent(b):
        spread_core(b, 0).wait_send()
        spread_core(b, 1).wait_send()

    def vector_round(k, device):
        return remote(gv, R["gv_in"].at[k], R["v_send"].at[k], R["v_recv"].at[k], device)

    def vector_sum(k, device):
        copy = vector_round(k, device)
        copy.wait()
        gv[...] += R["gv_in"][k]

    def relay_sent():
        for i in range(vec.shape[0]):
            R["gv_out"][i] = gv[i : i + 1]

        @pl.when(z == 2)
        def _():
            for r in range(B):
                for k in range(2):
                    part_copy(r, k).wait_send()

        for r in range(B):

            @pl.when(z != 0)
            def _():
                gather_i(r, z).wait_send()

            @pl.when(z != 2)
            def _():
                gather_v(r, z).wait_send()

        for i in range(chunks):

            @pl.when(z != 0)
            def _():
                backward_hop(i).wait_send()

            @pl.when(z != S - 1)
            def _():
                forward_hop(i).wait_send()

    def loop(first, last, step):
        lax.fori_loop(first, last, lambda i, c: (step(i), c)[1], 0)

    def each_block(step):
        loop(0, blocks, lambda i: step(lax.rem(i + shift, wrap)))

    def each_back(step):
        loop(0, blocks, lambda i: step(lax.rem(i + shift_back, wrap)))

    if fused:
        vector_round(0, beside).start()
        vector_sum(0, beside)
        vector_round(1, x_next).start()

        @pl.when(z == 0)
        def _():
            take()

        each_block(sum_first)
        vector_sum(1, x_next)
        vector_round(2, far).start()

        @pl.when(z == 3)
        def _():
            mixup_v()

        each_back(sum_second)
        vector_sum(2, far)

        @pl.when(z == 0)
        def _():
            mixup_i_end()
            mixup_v()

        each_back(pass_on)
        each_block(sent_early)
        loop(0, own_blocks, lambda b: core_send(b).wait_send())
        relay_sent()

        @pl.when(z == 3)
        def _():
            mixup_v_end(1)

        most = blocks - 2
        loop(0, most, lambda i: pass_core(lax.rem(i + shift_back, wrap)))

        @pl.when(z == 0)
        def _():
            mixup_v_end(0)

        loop(most, blocks, lambda i: pass_core(lax.rem(i + shift_back, wrap)))


        @pl.when(z == 1)
        def _():
            give_back().wait_recv()
            spread_core(LENT, 0).start()
            spread_core(LENT, 1).start()

        loop(0, own_blocks, arrive)
        mixup_handed()
        each_block(sent)
        loop(0, own_blocks, core_sent)

        @pl.when(z == 1)
        def _():
            lend().wait_send()

        @pl.when(z == 0)
        def _():
            give_back().wait_send()
            w[TAKEN] = jnp.zeros((D, D), bf16)

    else:
        @pl.when(z == 0)
        def _():
            mixup_i_end()

        @pl.when((z == 0) | (z == 3))
        def _():
            mixup_v()
            for r in range(B):
                owed_v_copy(r).start()

        for end, k in ((0, 0), (3, 1)):
            pl.when(z == end)(partial(mixup_v_end, k))
        mixup_handed()
        relay_sent()
        for b in range(8):
            w[b] = G[b]


def on_device(inputs, other_view, mats, vectors, mixing, partner, segments, cotangent):
    B, TS, D = inputs.shape
    VS = other_view.shape[1]
    T = segments.shape[1]
    S = lax.axis_size("section")
    V = VS * S
    H = mats.shape[3]
    pairs = D // PAIR
    vmem = pl.BlockSpec(memory_space=pltpu.VMEM)
    smem = pl.BlockSpec(memory_space=pltpu.SMEM)
    hbm = pl.BlockSpec(memory_space=pl.ANY)
    args = {
        "inputs": (inputs, hbm),
        "other_view": (other_view, hbm),
        "mats": (mats, hbm),
        "vec": (jnp.swapaxes(vectors, 0, 1), vmem),
        "mixing": (mixing, smem),
        "partner": (partner, smem),
        "segments": (segments, vmem),
        "cot": (cotangent.reshape(B * T, D), hbm),
    }
    outs = {
        "records": (B * T, D, bf16),
        "in_grad": (B, TS, D, bf16),
        "view_grad": (B, VS, D, bf16),
        "gv_out": (vectors.shape[1], 1, D, f32),
        "w": (8, D, D, bf16),
    }
    dma = pltpu.SemaphoreType.DMA

    def buf(*shape, dtype=bf16):
        return pltpu.VMEM(shape, dtype)

    scratch = {"G": buf(8, D, D), "core_in": buf(8, D // 2, D)}
    scratch |= {k: buf(8, D // 8, D) for k in ("rx", "ry")}
    scratch |= {k: buf(8, D // 16, D) for k in ("rx2", "ry2")}
    scratch |= {"gv": buf(8, D, dtype=f32), "gv_in": buf(3, 8, D, dtype=f32)}
    scratch |= {"seg_q": buf(B, T, 1, dtype=f32), "seg_v": buf(B, 1, V, dtype=f32)}
    for k in ("own", "far", "stage"):
        scratch |= {k + "_i": buf(B, TS, D), k + "_v": buf(B, VS, D)}
    for k in ("owed", "arr", "fin"):
        scratch |= {k + "_i": buf(B * T, D), k + "_v": buf(B, 2 * VS, D)}
    scratch["part_v"] = buf(B, 2 * VS, D)
    scratch |= {k: buf(B * V, D) for k in ("view", "dw")}
    for k in ("hin", "gin", "gout", "n1", "a1", "do1", "n2", "a2", "q2", "dq2", "do2"):
        scratch[k] = buf(B * T, D)
    scratch |= {k: buf(B * T, D, dtype=f32) for k in ("u1", "u2", "dn1", "dn2", "dm")}
    scratch |= {k: buf(B * T, 1, dtype=f32) for k in ("s1", "s2")}
    scratch |= {k: buf(B * T, 3 * D) for k in ("qkv1", "dqkv1")}
    scratch |= {k: buf(B * V, 2 * D) for k in ("kv2", "dkv2")}
    scratch["p1"] = buf(B * T, 2 * T * pairs, dtype=f32)
    W = max(H, 2 * V * pairs)
    scratch |= {"g": buf(B * T, H), "da": buf(B * T, W), "gp": buf(B * T, W, dtype=f32)}
    scratch |= {
        "w_sem": dma((8,)),
        "ex_sem": dma((4,)),
        "oi_send": dma((B,)),
        "oi_recv": dma((B,)),
        "ov_send": dma((B,)),
        "ov_recv": dma((B,)),
        "l_sem": dma((3,)),
        "gi_send": dma((B,)),
        "gi_recv": dma((B, S)),
        "gv_send": dma((B,)),
        "gv_recv": dma((B, S)),
        "f_send": dma((2 * B,)),
        "f_recv": dma((2 * B,)),
        "b_send": dma((2 * B,)),
        "b_recv": dma((2 * B,)),
        "sv_send": dma((B, 2)),
        "sv_recv": dma((B,)),
        "hi_send": dma((B, S)),
        "hi_recv": dma((B,)),
        "hv_send": dma((B, 2)),
        "hv_recv": dma((B,)),
        "lend_send": dma,
        "lend_recv": dma,
        "back_send": dma,
        "back_recv": dma,
        "r_send": dma((11, 8)),
        "r_recv": dma((11, 8)),
        "v_send": dma((3,)),
        "v_recv": dma((3,)),
    }
    names = list(args) + list(outs) + list(scratch)
    fused = lax.axis_size("dp") == 8
    *small, total = pl.pallas_call(
        partial(kernel, names, fused),
        out_shape=[pltpu.VMEM(s[:-1], s[-1]) for s in outs.values()],
        in_specs=[spec for _, spec in args.values()],
        out_specs=[vmem] * len(outs),
        scratch_shapes=list(scratch.values()),
        compiler_params=pltpu.CompilerParams(
            collective_id=0, has_side_effects=True, vmem_limit_bytes=50 << 20
        ),
        name="relay",
    )(*[value for value, _ in args.values()])
    if not fused:
        total, small[-1] = lax.psum((total, small[-1]), "dp")
    piece = D // 4
    wide, records, in_grad, view_grad, vector_grad = pl.pallas_call(
        widen,
        out_shape=[jax.ShapeDtypeStruct(mats.shape, f32)]
        + [jax.ShapeDtypeStruct(x.shape, x.dtype) for x in small],
        in_specs=[vmem] * 5,
        out_specs=[hbm] * 5,
        scratch_shapes=[pltpu.VMEM((4, piece, H), f32), dma((4,)), dma((4,))],
        compiler_params=pltpu.CompilerParams(vmem_limit_bytes=16 << 20),
        name="widen",
    )(total, *small)
    records = records.reshape(1, B, T, D)
    return records, in_grad, view_grad, wide, jnp.swapaxes(vector_grad, 0, 1)


def widen(total, *refs):
    small, wide, outs, slots, sems, small_sems = refs[:4], refs[4], refs[5:9], *refs[9:]
    held, piece, H = slots.shape
    D = total.shape[1]
    copies = [
        pltpu.make_async_copy(a, b, small_sems.at[i]) for i, (a, b) in enumerate(zip(small, outs))
    ]
    for copy in copies:
        copy.start()

    def write(i):
        t, rows = i * piece // D, pl.ds(i * piece % D, piece)
        return pltpu.make_async_copy(slots.at[i % held], wide.at[0, t, rows], sems.at[i % held])

    steps = 2 * D // piece
    for i in range(steps):
        if i >= held:
            write(i - held).wait()
        t, start = i * piece // D, i * piece % D
        for c in range(H // D):
            values = total[t * (H // D) + c, start : start + piece].astype(f32)
            slots[i % held, :, c * D : (c + 1) * D] = values
        write(i).start()
    for i in range(steps - held, steps):
        write(i).wait()
    for copy in copies:
        copy.wait()


def solution(mesh):
    in_specs = (
        P("dp", "section", None),
        P("dp", "section", None),
        P("section", None, None, None),
        P("section", None, None),
        P("dp"),
        P("dp"),
        P("dp", None),
        P("dp", None, None),
    )
    out_specs = (
        P("section", "dp", None, None),
        P("dp", "section", None),
        P("dp", "section", None),
        P("section", None, None, None),
        P("section", None, None),
    )
    return jax.shard_map(
        on_device, mesh=mesh, in_specs=in_specs, out_specs=out_specs, check_vma=False
    )
```
